256 devices in a mesh: pair: 8 (over y, z_hi), row: 8 (over z_lo, core), col: 4 (over x).
Axes of the slice: x: 4, y: 4, z: 8 (z_hi: 2, z_lo: 4; z = z_hi * 4 + z_lo), core: 2. Of those that a mesh axis runs over, the one named last changes fastest.
Arguments:
- voxels: float32 [2, 15, 128, 640], P(None, None, ('pair', 'row'), 'col'), parts along dimension 2, may hold values from -6 to 6
- disparity: float32 [2, 128, 640], P(None, ('pair', 'row'), 'col'), parts along dimension 1, may hold values from 0 to 192
- hidden: bfloat16 [2, 128, 640, 128], P(None, ('pair', 'row'), 'col'), parts along dimension 1, may hold values from -1 to 1
- context: bfloat16 [2, 128, 640, 384], P(None, ('pair', 'row'), 'col'), parts along dimension 1, may hold values from -6 to 6
- embed_first: float32 [15, 256], replicated, may hold values from -1.5 to 1.5
- embed_bias: float32 [256], replicated, may hold values from -4 to 4
- embed_second: bfloat16 [256, 256], replicated, may hold values from -0.375 to 0.375
- motion_weight: float32 [36, 128], replicated, may hold values from -1 to 1
- motion_scale: float32 [128], replicated, may hold values from -4 to 4
- motion_bias: float32 [128], replicated, may hold values from -3 to 3
- gate_kernel: bfloat16 [3, 3, 256, 256], replicated, may hold values from -0.125 to 0.125
- candidate_kernel: bfloat16 [3, 3, 256, 128], replicated, may hold values from -0.125 to 0.125
- head_weight: bfloat16 [128], replicated, may hold values from -0.5 to 0.5
Outputs:
- new_hidden: bfloat16 [2, 128, 640, 128], P(None, ('pair', 'row'), 'col'), parts along dimension 1
- increment: float32 [2, 128, 640], P(None, ('pair', 'row'), 'col'), parts along dimension 1
The draws below stay inside these ranges and needn't reach their ends.
There are 8 independent parts, one for each index of `pair`. The reference program is written for one: setup_inputs(seed, part) draws one part's arguments, and reference() takes and returns one part's arrays. A program takes and returns all parts, laid end to end along the dimension named above; an argument that names none is the same for every part. Nothing has to cross between parts.
All inputs are finite; a program needn't handle non-finite values.
Results may differ from the reference program's by a relative error of at most 0.0085.
Values may be sent and summed in bfloat16 or wider, within the bound.
No kernel may reach another device: no remote copies, remote signals or barrier semaphores. Data moves between devices by JAX's collectives and lax.ppermute only.
A program may use at most 128 MiB of HBM per device.

```python
import jax
import jax.numpy as jnp
from jax import lax

C = 256
HID = 128
BINS = 15
LEVELS = 4
RADIUS = 4
TAPS = 9
MAXDISP = 192
H = 16
W = 640


def block_scale(rng, shape, shards, least, top_value):
    def one(dim, parts):
        draws = jax.random.uniform(jax.random.fold_in(jax.random.fold_in(rng, 6), dim), (parts,), jnp.float32, least / len(shards), top_value / len(shards))
        return jnp.repeat(jnp.exp(draws), shape[dim] // parts).reshape((-1,) + (1,) * (len(shape) - dim - 1))

    gain = one(*shards[0])
    for cut in shards[1:]:
        gain = gain * one(*cut)
    return gain


def scatter_about(own_key, extent, spread, reach, split=(), held_as=jnp.bfloat16):
    gain = block_scale(own_key, extent, split, -0.22, 0.18) if split else 1.0
    values = jax.random.normal(own_key, extent, jnp.float32) * spread * gain
    return jnp.minimum(jnp.maximum(values, -reach), reach).astype(held_as)


def setup_inputs(seed: int = 0, part: int = 0) -> dict:
    key_list = jax.random.split(jax.random.key(seed), 14)
    own_keys = jax.random.split(jax.random.fold_in(key_list[13], part), 14)
    return {
        "voxels": scatter_about(own_keys[0], (2, BINS, H, W), 1.0, 6.0, ((2, 8), (3, 4)), jnp.float32),
        "disparity": jnp.clip(192.0 * jax.random.uniform(own_keys[1], (2, H, W), jnp.float32) ** block_scale(own_keys[1], (2, H, W), ((1, 8), (2, 4)), -0.2, 0.2), 0.0, 192.0),
        "hidden": jnp.clip(jax.random.uniform(own_keys[2], (2, H, W, HID), jnp.float32, -1.0, 1.0) * block_scale(own_keys[2], (2, H, W, HID), ((1, 8), (2, 4)), -0.4, 0.0), -1.0, 1.0).astype(jnp.bfloat16),
        "context": scatter_about(own_keys[3], (2, H, W, 3 * HID), 1.0, 6.0, ((1, 8), (2, 4))),
        "embed_first": scatter_about(key_list[4], (BINS, C), BINS ** -0.5, 1.5, (), jnp.float32),
        "embed_bias": scatter_about(key_list[5], (C,), 1.0, 4.0, (), jnp.float32),
        "embed_second": scatter_about(key_list[6], (C, C), C ** -0.5, 0.375),
        "motion_weight": scatter_about(key_list[7], (LEVELS * TAPS, HID), (LEVELS * TAPS) ** -0.5, 1.0, (), jnp.float32),
        "motion_scale": scatter_about(key_list[8], (HID,), 1.0, 4.0, (), jnp.float32),
        "motion_bias": scatter_about(key_list[9], (HID,), 0.5, 3.0, (), jnp.float32),
        "gate_kernel": scatter_about(key_list[10], (3, 3, 2 * HID, 2 * HID), (18 * HID) ** -0.5, 0.125),
        "candidate_kernel": scatter_about(key_list[11], (3, 3, 2 * HID, HID), (18 * HID) ** -0.5, 0.125),
        "head_weight": scatter_about(key_list[12], (HID,), HID ** -0.5, 0.5),
    }


def encode(grid, embed_first, embed_bias, embed_second):
    first_layer = jnp.einsum("bhw,bc->hwc", grid, embed_first, precision=lax.Precision.HIGHEST)
    first_layer = jax.nn.silu(first_layer + embed_bias).astype(jnp.bfloat16)
    return jnp.dot(first_layer, embed_second, preferred_element_type=jnp.float32).astype(jnp.bfloat16)


def pyramid(scores):
    levels = [scores]
    for level_at in range(1, LEVELS):
        finer = levels[-1]
        paired = finer.reshape(finer.shape[:-1] + (finer.shape[-1] // 2, 2))
        levels.append((paired[..., 0] + paired[..., 1]) * 0.5)
    return levels


def pick(source, index, length):
    inside = (index >= 0) & (index < length)
    place = jnp.clip(index, 0, length - 1)
    value = jnp.take_along_axis(source, place[..., None], axis=-1)[..., 0]
    return jnp.where(inside, value, 0.0)


def sample(levels, position, offsets):
    gathered = []
    for level_at in range(LEVELS):
        source = levels[level_at]
        length = source.shape[-1]
        factor = 1.0 / (2 ** level_at)
        centre = position * factor - offsets * factor
        for tap_index in range(2 * RADIUS + 1):
            spot = centre + float(tap_index - RADIUS)
            floor_value = jnp.floor(spot)
            weight = spot - floor_value
            lower = floor_value.astype(jnp.int32)
            gathered.append((1.0 - weight) * pick(source, lower, length) + weight * pick(source, lower + 1, length))
    return jnp.stack(gathered, axis=-1)


def convolve(padded, kernel, row_count, col_count):
    summed = jnp.zeros((row_count, col_count, kernel.shape[-1]), jnp.float32)
    for row_shift in range(3):
        for col_shift in range(3):
            window = padded[row_shift:row_shift + row_count, col_shift:col_shift + col_count]
            summed = summed + jnp.dot(window, kernel[row_shift, col_shift], preferred_element_type=jnp.float32)
    return summed


def surround(field):
    return jnp.pad(field, ((1, 1), (1, 1), (0, 0)))


def update(query, match, offsets, state, context, motion_weight, motion_scale, motion_bias, gate_kernel, candidate_kernel, head_weight):
    row_count, col_count, channels = query.shape
    units = state.shape[-1]
    scores = jnp.einsum("yxc,ypc->yxp", query.astype(jnp.float32), match.astype(jnp.float32), precision=lax.Precision.HIGHEST)
    scores = scores * (channels ** -0.5)
    levels = pyramid(scores)
    position = jnp.arange(col_count).astype(jnp.float32)
    lookups = sample(levels, position, offsets)
    motion = jnp.dot(lookups, motion_weight, precision=lax.Precision.HIGHEST)
    motion = jax.nn.silu(motion + (offsets / MAXDISP)[..., None] * motion_scale + motion_bias).astype(jnp.bfloat16)
    gate_input = jnp.concatenate([state, motion], axis=-1)
    gate_terms = convolve(surround(gate_input), gate_kernel, row_count, col_count)
    update_gate = jax.nn.sigmoid(gate_terms[..., :units] + context[..., :units].astype(jnp.float32))
    reset_gate = jax.nn.sigmoid(gate_terms[..., units:] + context[..., units:2 * units].astype(jnp.float32))
    reset_state = (reset_gate * state.astype(jnp.float32)).astype(jnp.bfloat16)
    candidate_input = jnp.concatenate([reset_state, motion], axis=-1)
    candidate = jnp.tanh(convolve(surround(candidate_input), candidate_kernel, row_count, col_count) + context[..., 2 * units:].astype(jnp.float32))
    updated = ((1.0 - update_gate) * state.astype(jnp.float32) + update_gate * candidate).astype(jnp.bfloat16)
    return updated, jnp.dot(updated, head_weight, preferred_element_type=jnp.float32)


def mirror(array):
    return jnp.flip(array, axis=1)


def reference(voxels, disparity, hidden, context, embed_first, embed_bias, embed_second, motion_weight, motion_scale, motion_bias, gate_kernel, candidate_kernel, head_weight):
    left_features = encode(voxels[0], embed_first, embed_bias, embed_second)
    right_features = encode(voxels[1], embed_first, embed_bias, embed_second)
    weights = (motion_weight, motion_scale, motion_bias, gate_kernel, candidate_kernel, head_weight)
    left_state, left_step = update(left_features, right_features, disparity[0], hidden[0], context[0], *weights)
    right_state, right_step = update(mirror(right_features), mirror(left_features), mirror(disparity[1]), mirror(hidden[1]), mirror(context[1]), *weights)
    new_hidden = jnp.stack([left_state, mirror(right_state)])
    increment = jnp.stack([left_step, mirror(right_step)])
    return new_hidden, increment
```

```python
import jax
import jax.numpy as jnp
import numpy as np
from jax import lax
from jax.experimental import pallas as pl
from jax.experimental.pallas import tpu as pltpu
from jax.sharding import PartitionSpec as P

BF = jnp.bfloat16
F32 = jnp.float32

ROWS = 2
TILE = 160
IMAGE = 640
PAD = 16
EXT = TILE + 2 * PAD
BINS = 15
UNITS = 128
NEAR = 48
FAR = 72
WINDOW = 512
LAST = FAR + 2 * TILE + NEAR - 1
TAPS = 9
LEVELS = 4
GROUP = 40
STARTS = (0, 17, 30, 41)
VMEM_LIMIT = 48 * 1024 * 1024


def tables():
    pool = np.zeros((128, 128), np.float32)
    firsts = (28, 12, 4, 0)
    counts = (17, 13, 11, 10)
    for level in range(LEVELS):
        width = 2**level
        for k in range(counts[level]):
            entry = firsts[level] + k
            pool[entry * width : (entry + 1) * width, STARTS[level] + k] = 1.0 / (16 * width)
    lane = np.arange(128)
    member = lane % GROUP
    used = (member < LEVELS * TAPS) & (lane < 3 * GROUP)
    level = np.where(used, member // TAPS, 0)
    first = np.where(used, np.take(np.array(STARTS), level) + member % TAPS, 0)
    scale = np.where(used, 0.5**level, 0.0)
    low = ((lane >= GROUP) & (lane < 2 * GROUP)).astype(np.float32)
    rows = np.zeros((8, 128), np.float32)
    rows[0], rows[1], rows[2] = first, scale, low
    return np.concatenate([pool, pool]).astype(jnp.bfloat16), rows


def split(value):
    high = value.astype(BF).astype(F32)
    return high, value - high


def silu_of_half(half):
    return half + half * jnp.tanh(half)


def sigmoid(value):
    return 0.5 * jnp.tanh(0.5 * value) + 0.5


def pack_kernel(vox, disp, hidden, context, own, right, left, far, down, up):
    col = lax.axis_index("col")
    row_at = lax.broadcasted_iota(jnp.int32, (8, 128), 0)
    parts = []
    edges_right, edges_left = [], []
    for v in range(2):
        for y in range(ROWS):
            high, low = split(vox[v, :, y, :])
            ones = jnp.ones((1, TILE), F32)
            block = jnp.concatenate([high, ones, low, ones], axis=0)
            parts.append(block)
            own[2 * v + y] = jnp.concatenate(
                [block, jnp.zeros((32, 256 - TILE), F32)], axis=1
            ).astype(BF)
            hid_last = pltpu.roll(hidden[v, y, 144:160, :].astype(F32)[8:16], 2, 0)
            con_last = pltpu.roll(context[v, y, 144:160, UNITS : 2 * UNITS].astype(F32)[8:16], 3, 0)
            hid_first = hidden[v, y, 0:16, :].astype(F32)[0:8]
            con_first = pltpu.roll(context[v, y, 0:16, UNITS : 2 * UNITS].astype(F32)[0:8], 2, 0)
            depth = disp[v, y : y + 1, :]
            d_last = pltpu.roll(jnp.broadcast_to(depth[:, 32:160], (8, 128)), 8, 1)
            d_first = jnp.broadcast_to(depth[:, 0:128], (8, 128))

            def edge(hid, con, dis):
                d_high, rest = split(dis)
                d_mid, d_low = split(rest)
                out = jnp.where(row_at < 2, hid, con)
                out = jnp.where(row_at == 3, d_high, out)
                out = jnp.where(row_at == 4, d_mid, out)
                return jnp.where(row_at >= 5, d_low, out)

            edges_right.append(edge(hid_last, con_last, d_last))
            edges_left.append(edge(hid_first, con_first, d_first))
            for target, con_row in ((down, ROWS - 1), (up, 0)):
                target[v, y] = hidden[v, y]
                if y == con_row:
                    target[v, ROWS] = context[v, y, :, UNITS : 2 * UNITS]
    blank = jnp.zeros((32, 256 - TILE - NEAR), F32)
    for y in range(ROWS):
        f0, f1 = parts[y], parts[ROWS + y]
        right[32 * y : 32 * y + 32, :] = jnp.concatenate(
            [f1, f0[:, TILE - NEAR :], blank], axis=1
        ).astype(BF)
        left[32 * y : 32 * y + 32, :] = jnp.concatenate([f0, f1[:, :NEAR], blank], axis=1).astype(BF)
        tail = jnp.concatenate([f1[:, TILE - FAR :], jnp.zeros((32, 128 - FAR), F32)], axis=1)
        far[32 * y : 32 * y + 32, :] = jnp.where(col < 2, tail, f0[:, :128]).astype(BF)
    for target, edges in ((right, edges_right), (left, edges_left)):
        target[64:80, :] = jnp.concatenate(
            [
                jnp.concatenate([edges[0], edges[1]], axis=0),
                jnp.concatenate([edges[2], edges[3]], axis=0),
            ],
            axis=1,
        ).astype(BF)


def weight_kernel(first, bias, second, motion, w1, w1t, w2t, mw):
    w_high, w_low = split(first[...] * 0.5)
    b_high, rest = split(bias[...] * 0.5)
    b_mid, b_low = split(rest)
    stacked = jnp.concatenate([w_high, b_high, w_high, b_mid, w_low, b_low], axis=0)
    w1[...] = stacked.astype(BF)
    w1t[...] = jnp.concatenate([stacked, jnp.zeros((80, 256), F32)], axis=0).T.astype(BF)
    w2t[...] = second[...].astype(F32).T.astype(BF)
    m_high, m_low = split(motion[...])
    gap = jnp.zeros((GROUP - LEVELS * TAPS, 128), F32)
    mw[...] = jnp.concatenate(
        [m_high, gap, m_high, gap, m_low, gap, jnp.zeros((8, 128), F32)], axis=0
    ).astype(BF)


def motion_kernel(
    own, from_left, from_right, from_far, disp, w1, w1t, w2, w2t, mw, scale, bias, pool, rows, out
):
    col = lax.axis_index("col")
    far_scale_left = jnp.where(col >= 2, 1.0, 0.0).astype(F32)
    far_scale_right = 1.0 - far_scale_left
    edge_left = from_left[64:80, :].astype(F32)
    edge_right = from_right[64:80, :].astype(F32)

    def edge_of(edges, v, y):
        return edges[8 * y : 8 * y + 8, 128 * v : 128 * v + 128]

    depth_rows = []
    for v in range(2):
        for y in range(ROWS):
            e_l, e_r = edge_of(edge_left, v, y), edge_of(edge_right, v, y)
            d_l = e_l[3:4] + e_l[4:5] + e_l[5:6]
            d_r = e_r[3:4] + e_r[4:5] + e_r[5:6]
            depth_rows.append(
                jnp.concatenate(
                    [
                        jnp.zeros((1, 8), F32),
                        d_l[:, :8],
                        disp[v, y : y + 1, :],
                        d_r[:, :8],
                        jnp.zeros((1, 72), F32),
                    ],
                    axis=1,
                )
            )
    depth_rows.append(jnp.zeros((4, 256), F32))
    depths = jnp.concatenate(depth_rows, axis=0).T

    first = rows[0:1, :].astype(jnp.int32)
    level_scale = rows[1:2, :]
    is_low = rows[2:3, :] > 0.5
    lane = lax.broadcasted_iota(jnp.int32, (EXT, 128), 1)
    pixel = lax.broadcasted_iota(jnp.int32, (EXT, 1), 0)
    column = pixel + (col * TILE - PAD)
    inside = (column >= 0) & (column < IMAGE)
    pixel = pixel.astype(F32)
    depth_scale = scale[...] * (1.0 / 192.0)

    def lookups(scores, depth, v):
        spot = (pixel - PAD if v == 0 else (EXT - 1 - PAD) - pixel) - depth
        eighth = jnp.floor(spot * 0.125)
        rest = spot - 8.0 * eighth
        start = (8.0 * eighth).astype(jnp.int32) + (FAR + TILE - 32)
        index = start + lane if v == 0 else (LAST - start) - lane
        block, place = index >> 7, index & 127
        near = jnp.zeros((EXT, 128), F32)
        for k in range(WINDOW // 128):
            taken = jnp.take_along_axis(
                scores[:, 128 * k : 128 * k + 128], place, axis=1, mode="promise_in_bounds"
            )
            near = jnp.where(block == k, taken, near)
        high, low = split(near)
        pooled = jnp.dot(
            jnp.concatenate([high.astype(BF), low.astype(BF)], axis=1),
            pool[...],
            preferred_element_type=F32,
        )
        at = rest * level_scale
        floor = jnp.floor(at)
        weight = at - floor
        index = floor.astype(jnp.int32) + first
        lower = jnp.take_along_axis(pooled, index, axis=1, mode="promise_in_bounds")
        upper = jnp.take_along_axis(pooled, index + 1, axis=1, mode="promise_in_bounds")
        return lower + weight * (upper - lower)

    for y in range(ROWS):
        left = from_left[32 * y : 32 * y + 32, :].astype(F32)
        right = from_right[32 * y : 32 * y + 32, :].astype(F32)
        far = from_far[32 * y : 32 * y + 32, :].astype(F32)[:, :FAR]
        f0 = own[y].astype(F32)[:, :TILE]
        f1 = own[ROWS + y].astype(F32)[:, :TILE]
        blank = jnp.zeros((32, WINDOW - 1 - LAST), F32)
        win1 = jnp.concatenate(
            [far * far_scale_left, left[:, :TILE], f1, right[:, TILE : TILE + NEAR], blank], axis=1
        )
        win0 = jnp.concatenate(
            [left[:, TILE : TILE + NEAR], f0, right[:, :TILE], far * far_scale_right, blank], axis=1
        )
        query0 = win0[:, NEAR - PAD : NEAR - PAD + EXT]
        query1 = win1[:, FAR + TILE - PAD : FAR + TILE - PAD + EXT]
        for v, query, window in ((0, query0, win1), (1, query1, win0)):
            stacked = jnp.concatenate([query, query[:16]], axis=0)
            stacked = jnp.concatenate(
                [
                    jnp.concatenate([stacked, jnp.zeros((48, 256 - EXT), F32)], axis=1),
                    jnp.zeros((80, 256), F32),
                ],
                axis=0,
            ).T.astype(BF)
            layer = silu_of_half(
                jnp.dot(stacked[:EXT, :48], w1[...], preferred_element_type=F32)
            ).astype(BF)
            features = jnp.dot(layer, w2[...], preferred_element_type=F32).astype(BF)
            stacked = jnp.concatenate([window, window[:16]], axis=0).astype(BF)
            layer = silu_of_half(
                jnp.dot(w1t[:, :48], stacked, preferred_element_type=F32)
            ).astype(BF)
            match = jnp.dot(w2t[...], layer, preferred_element_type=F32).astype(BF)
            scores = jnp.dot(features, match, preferred_element_type=F32)
            depth = depths[:EXT, 2 * v + y : 2 * v + y + 1]
            look = lookups(scores, depth, v)
            high, low = split(look)
            half = 0.5 * (
                jnp.dot(
                    jnp.where(is_low, low, high).astype(BF), mw[...], preferred_element_type=F32
                )
                + depth * depth_scale
                + bias[...]
            )
            value = jnp.where(inside, silu_of_half(half), 0.0)
            out[v, y] = jnp.concatenate(
                [edge_of(edge_left, v, y), value[8 : EXT - 8], edge_of(edge_right, v, y)], axis=0
            ).astype(BF)


def update_kernel(
    hidden, context, hc_up, hc_down, mot, mot_up, mot_down, gate_k, cand_k, head, new, inc, state, reset
):
    def mot_of(v, yy):
        if yy < 2:
            return mot_up[v, yy]
        if yy < 4:
            return mot[v, yy - 2]
        return mot_down[v, yy - 4]

    def widened(middle, value, shift_left, shift_right):
        ends_left = pltpu.roll(value[0:16].astype(F32), shift_left, 0).astype(BF)
        ends_right = pltpu.roll(value[EXT - 16 :].astype(F32), shift_right, 0).astype(BF)
        return jnp.concatenate([ends_left, middle, ends_right], axis=0)

    def spread(products, width, v):
        before, at, after = (products[:, width * b : width * b + width] for b in range(3))
        if v == 1:
            before, after = after, before
        return pltpu.roll(before, 1, 0) + at + pltpu.roll(after, EXT - 1, 0)

    gate_all = jnp.concatenate(
        [jnp.concatenate([gate_k[a, b] for a in range(3)], axis=0) for b in range(3)], axis=1
    )
    gate_reset = jnp.concatenate(
        [
            jnp.concatenate([gate_k[a, b, :, UNITS:] for a in range(3)], axis=0)
            for b in range(3)
        ],
        axis=1,
    )
    cand_all = jnp.concatenate(
        [jnp.concatenate([cand_k[a, b] for a in range(3)], axis=0) for b in range(3)], axis=1
    )
    head_rows = jnp.broadcast_to(head[...].astype(F32), (8, UNITS)).astype(BF)
    for v in range(2):
        for yy in range(6):
            if yy < 2:
                middle = hc_up[v, yy]
            elif yy < 4:
                middle = hidden[v, yy - 2]
            else:
                middle = hc_down[v, yy - 4]
            state[v, yy] = widened(middle, mot_of(v, yy), 14, 8)
        gates = [None, None]
        for yy in range(1, 5):
            stacked = jnp.concatenate(
                [piece for k in (yy - 1, yy, yy + 1) for piece in (state[v, k], mot_of(v, k))],
                axis=1,
            )
            if yy in (2, 3):
                terms = spread(
                    jnp.dot(stacked, gate_all, preferred_element_type=F32), 2 * UNITS, v
                )
                gates[yy - 2] = terms[PAD : PAD + TILE, :UNITS]
                terms = terms[:, UNITS:]
                own_context = context[v, yy - 2, :, UNITS : 2 * UNITS]
            else:
                terms = spread(jnp.dot(stacked, gate_reset, preferred_element_type=F32), UNITS, v)
                own_context = hc_up[v, ROWS] if yy == 1 else hc_down[v, ROWS]
            wide = widened(own_context, mot_of(v, yy), 13, 6)
            gate = sigmoid(terms + wide.astype(F32))
            reset[v, yy - 1] = (gate * state[v, yy].astype(F32)).astype(BF)
        for y in range(ROWS):
            stacked = jnp.concatenate(
                [piece for k in range(3) for piece in (reset[v, y + k], mot_of(v, y + 1 + k))],
                axis=1,
            )
            terms = spread(jnp.dot(stacked, cand_all, preferred_element_type=F32), UNITS, v)
            candidate = jnp.tanh(
                terms[PAD : PAD + TILE] + context[v, y, :, 2 * UNITS :].astype(F32)
            )
            update = sigmoid(gates[y] + context[v, y, :, :UNITS].astype(F32))
            old = hidden[v, y].astype(F32)
            fresh = ((1.0 - update) * old + update * candidate).astype(BF)
            new[v, y] = fresh
            inc[v, y : y + 1, :] = lax.dot_general(
                head_rows, fresh, (((1,), (1,)), ((), ())), preferred_element_type=F32
            )[0:1]


def call(kernel, outs, scratch=(), **cost):
    return pl.pallas_call(
        kernel,
        out_shape=[jax.ShapeDtypeStruct(shape, dtype) for shape, dtype in outs],
        scratch_shapes=list(scratch),
        compiler_params=pltpu.CompilerParams(vmem_limit_bytes=VMEM_LIMIT),
        cost_estimate=pl.CostEstimate(transcendentals=0, **cost),
    )


def local(
    voxels,
    disparity,
    hidden,
    context,
    embed_first,
    embed_bias,
    embed_second,
    motion_weight,
    motion_scale,
    motion_bias,
    gate_kernel,
    candidate_kernel,
    head_weight,
):
    cols = lax.axis_size("col")
    rows = lax.axis_size("row")
    onward = [(i, i + 1) for i in range(cols - 1)]
    back = [(i + 1, i) for i in range(cols - 1)]
    across = [(i, (i + 2) % cols) for i in range(cols)]
    downward = [(i, i + 1) for i in range(rows - 1)]
    upward = [(i + 1, i) for i in range(rows - 1)]
    pool, lane_rows = tables()

    own, right, left, far, down, up = call(
        pack_kernel,
        [
            ((4, 32, 256), BF),
            ((80, 256), BF),
            ((80, 256), BF),
            ((64, 128), BF),
            ((2, 3, TILE, UNITS), BF),
            ((2, 3, TILE, UNITS), BF),
        ],
        flops=10**6,
        bytes_accessed=2 * 10**6,
    )(voxels, disparity, hidden, context)
    from_left = lax.ppermute(right, "col", onward)
    from_right = lax.ppermute(left, "col", back)
    from_far = lax.ppermute(far, "col", across)
    hc_up = lax.ppermute(down, "row", downward)
    hc_down = lax.ppermute(up, "row", upward)
    w1, w1t, w2t, mw = call(
        weight_kernel,
        [((48, 256), BF), ((256, 128), BF), ((256, 256), BF), ((128, 128), BF)],
        flops=10**6,
        bytes_accessed=10**6,
    )(embed_first, embed_bias.reshape(1, -1), embed_second, motion_weight)
    (motion,) = call(
        motion_kernel,
        [((2, ROWS, EXT, UNITS), BF)],
        flops=10**9,
        bytes_accessed=10**6,
    )(
        own,
        from_left,
        from_right,
        from_far,
        disparity,
        w1,
        w1t,
        embed_second,
        w2t,
        mw,
        motion_scale.reshape(1, -1),
        motion_bias.reshape(1, -1),
        jnp.asarray(pool),
        jnp.asarray(lane_rows),
    )
    motion_up = lax.ppermute(motion, "row", downward)
    motion_down = lax.ppermute(motion, "row", upward)
    new_hidden, increment = call(
        update_kernel,
        [((2, ROWS, TILE, UNITS), BF), ((2, ROWS, TILE), F32)],
        scratch=[pltpu.VMEM((2, 6, EXT, UNITS), BF), pltpu.VMEM((2, 4, EXT, UNITS), BF)],
        flops=2 * 10**9,
        bytes_accessed=4 * 10**6,
    )(
        hidden,
        context,
        hc_up,
        hc_down,
        motion,
        motion_up,
        motion_down,
        gate_kernel,
        candidate_kernel,
        head_weight.reshape(1, -1),
    )
    return new_hidden, increment


def solution(mesh):
    band = ("pair", "row")
    in_specs = (
        P(None, None, band, "col"),
        P(None, band, "col"),
        P(None, band, "col", None),
        P(None, band, "col", None),
    ) + (P(),) * 9
    out_specs = (P(None, band, "col", None), P(None, band, "col"))
    return jax.shard_map(local, mesh=mesh, in_specs=in_specs, out_specs=out_specs, check_vma=False)
```

```python
import jax
import jax.numpy as jnp
import numpy as np
from jax import lax
from jax.experimental import pallas as pl
from jax.experimental.pallas import tpu as pltpu
from jax.sharding import PartitionSpec as P

BF = jnp.bfloat16
F32 = jnp.float32

ROWS = 2
TILE = 160
IMAGE = 640
PAD = 16
EXT = TILE + 2 * PAD
BINS = 15
UNITS = 128
NEAR = 48
FAR = 72
WINDOW = 512
LAST = FAR + 2 * TILE + NEAR - 1
TAPS = 9
LEVELS = 4
GROUP = 40
STARTS = (0, 17, 30, 41)
VMEM_LIMIT = 48 * 1024 * 1024


def tables():
    pool = np.zeros((128, 128), np.float32)
    firsts = (28, 12, 4, 0)
    counts = (17, 13, 11, 10)
    for level in range(LEVELS):
        width = 2**level
        for k in range(counts[level]):
            entry = firsts[level] + k
            pool[entry * width : (entry + 1) * width, STARTS[level] + k] = 1.0 / (16 * width)
    lane = np.arange(128)
    member = lane % GROUP
    used = (member < LEVELS * TAPS) & (lane < 3 * GROUP)
    level = np.where(used, member // TAPS, 0)
    first = np.where(used, np.take(np.array(STARTS), level) + member % TAPS, 0)
    scale = np.where(used, 0.5**level, 0.0)
    low = ((lane >= GROUP) & (lane < 2 * GROUP)).astype(np.float32)
    rows = np.zeros((8, 128), np.float32)
    rows[0], rows[1], rows[2] = first, scale, low
    return np.concatenate([pool, pool]).astype(jnp.bfloat16), rows


def split(value):
    high = value.astype(BF).astype(F32)
    return high, value - high


def silu_of_half(half):
    return half + half * jnp.tanh(half)


def sigmoid(value):
    return 0.5 * jnp.tanh(0.5 * value) + 0.5


def pack_kernel(
    vox_h,
    disp_h,
    hidden_h,
    context_h,
    first_h,
    bias_h,
    second_h,
    motion_h,
    scale_h,
    mbias_h,
    pool_h,
    rows_h,
    own,
    right,
    left,
    far,
    down,
    up,
    w1,
    w1t,
    w2,
    w2t,
    mw,
    pool,
    rows,
    scale,
    mbias,
    disp,
    vox,
    first,
    bias,
    motion,
    sems,
):
    pairs = [(vox_h, vox), (disp_h, disp)]
    for v in range(2):
        pairs += [
            (hidden_h.at[v], down.at[v, 0:ROWS]),
            (hidden_h.at[v], up.at[v, 0:ROWS]),
            (context_h.at[v, ROWS - 1, :, UNITS : 2 * UNITS], down.at[v, ROWS]),
            (context_h.at[v, 0, :, UNITS : 2 * UNITS], up.at[v, ROWS]),
        ]
    data = len(pairs)
    pairs += [
        (first_h, first),
        (bias_h, bias),
        (second_h, w2),
        (motion_h, motion),
        (scale_h, scale),
        (mbias_h, mbias),
        (pool_h, pool),
        (rows_h, rows),
    ]
    copies = [pltpu.make_async_copy(a, b, sems.at[k]) for k, (a, b) in enumerate(pairs)]
    for copy in copies:
        copy.start()
    for copy in copies[:data]:
        copy.wait()
    col = lax.axis_index("col")
    row_at = lax.broadcasted_iota(jnp.int32, (8, 128), 0)
    parts = []
    edges_right, edges_left = [], []
    for v in range(2):
        for y in range(ROWS):
            high, low = split(vox[v, :, y, :])
            ones = jnp.ones((1, TILE), F32)
            block = jnp.concatenate([high, ones, low, ones], axis=0)
            parts.append(block)
            own[2 * v + y] = jnp.concatenate(
                [block, jnp.zeros((32, 256 - TILE), F32)], axis=1
            ).astype(BF)
            con = (up, down)[y]
            hid_last = pltpu.roll(down[v, y, 144:160, :].astype(F32)[8:16], 2, 0)
            con_last = pltpu.roll(con[v, ROWS, 144:160, :].astype(F32)[8:16], 3, 0)
            hid_first = down[v, y, 0:16, :].astype(F32)[0:8]
            con_first = pltpu.roll(con[v, ROWS, 0:16, :].astype(F32)[0:8], 2, 0)
            depth = disp[v, y : y + 1, :]
            d_last = pltpu.roll(jnp.broadcast_to(depth[:, 32:160], (8, 128)), 8, 1)
            d_first = jnp.broadcast_to(depth[:, 0:128], (8, 128))

            def edge(hid, con, dis):
                d_high, rest = split(dis)
                d_mid, d_low = split(rest)
                out = jnp.where(row_at < 2, hid, con)
                out = jnp.where(row_at == 3, d_high, out)
                out = jnp.where(row_at == 4, d_mid, out)
                return jnp.where(row_at >= 5, d_low, out)

            edges_right.append(edge(hid_last, con_last, d_last))
            edges_left.append(edge(hid_first, con_first, d_first))
    blank = jnp.zeros((32, 256 - TILE - NEAR), F32)
    for y in range(ROWS):
        f0, f1 = parts[y], parts[ROWS + y]
        right[32 * y : 32 * y + 32, :] = jnp.concatenate(
            [f1, f0[:, TILE - NEAR :], blank], axis=1
        ).astype(BF)
        left[32 * y : 32 * y + 32, :] = jnp.concatenate([f0, f1[:, :NEAR], blank], axis=1).astype(BF)
        tail = jnp.concatenate([f1[:, TILE - FAR :], jnp.zeros((32, 128 - FAR), F32)], axis=1)
        far[32 * y : 32 * y + 32, :] = jnp.where(col < 2, tail, f0[:, :128]).astype(BF)
    for target, edges in ((right, edges_right), (left, edges_left)):
        target[64:80, :] = jnp.concatenate(
            [
                jnp.concatenate([edges[0], edges[1]], axis=0),
                jnp.concatenate([edges[2], edges[3]], axis=0),
            ],
            axis=1,
        ).astype(BF)
    for copy in copies[data:]:
        copy.wait()
    w_high, w_low = split(first[...] * 0.5)
    b_high, rest = split(bias[...] * 0.5)
    b_mid, b_low = split(rest)
    stacked = jnp.concatenate([w_high, b_high, w_high, b_mid, w_low, b_low], axis=0)
    w1[...] = stacked.astype(BF)
    w1t[...] = jnp.concatenate([stacked, jnp.zeros((80, 256), F32)], axis=0).T.astype(BF)
    w2t[...] = w2[...].astype(F32).T.astype(BF)
    m_high, m_low = split(motion[...])
    gap = jnp.zeros((GROUP - LEVELS * TAPS, 128), F32)
    mw[...] = jnp.concatenate(
        [m_high, gap, m_high, gap, m_low, gap, jnp.zeros((8, 128), F32)], axis=0
    ).astype(BF)


def motion_kernel(
    own, from_left, from_right, from_far, disp, w1, w1t, w2, w2t, mw, scale, bias, pool, rows, out
):
    col = lax.axis_index("col")
    far_scale_left = jnp.where(col >= 2, 1.0, 0.0).astype(F32)
    far_scale_right = 1.0 - far_scale_left
    edge_left = from_left[64:80, :].astype(F32)
    edge_right = from_right[64:80, :].astype(F32)

    def edge_of(edges, v, y):
        return edges[8 * y : 8 * y + 8, 128 * v : 128 * v + 128]

    depth_rows = []
    for v in range(2):
        for y in range(ROWS):
            e_l, e_r = edge_of(edge_left, v, y), edge_of(edge_right, v, y)
            d_l = e_l[3:4] + e_l[4:5] + e_l[5:6]
            d_r = e_r[3:4] + e_r[4:5] + e_r[5:6]
            depth_rows.append(
                jnp.concatenate(
                    [
                        jnp.zeros((1, 8), F32),
                        d_l[:, :8],
                        disp[v, y : y + 1, :],
                        d_r[:, :8],
                        jnp.zeros((1, 72), F32),
                    ],
                    axis=1,
                )
            )
    depth_rows.append(jnp.zeros((4, 256), F32))
    depths = jnp.concatenate(depth_rows, axis=0).T

    first = rows[0:1, :].astype(jnp.int32)
    level_scale = rows[1:2, :]
    is_low = rows[2:3, :] > 0.5
    lane = lax.broadcasted_iota(jnp.int32, (EXT, 128), 1)
    pixel = lax.broadcasted_iota(jnp.int32, (EXT, 1), 0)
    column = pixel + (col * TILE - PAD)
    inside = (column >= 0) & (column < IMAGE)
    pixel = pixel.astype(F32)
    depth_scale = scale[...] * (1.0 / 192.0)

    def lookups(scores, depth, v):
        spot = (pixel - PAD if v == 0 else (EXT - 1 - PAD) - pixel) - depth
        eighth = jnp.floor(spot * 0.125)
        rest = spot - 8.0 * eighth
        start = (8.0 * eighth).astype(jnp.int32) + (FAR + TILE - 32)
        index = start + lane if v == 0 else (LAST - start) - lane
        block, place = index >> 7, index & 127
        near = jnp.zeros((EXT, 128), F32)
        for k in range(WINDOW // 128):
            taken = jnp.take_along_axis(
                scores[:, 128 * k : 128 * k + 128], place, axis=1, mode="promise_in_bounds"
            )
            near = jnp.where(block == k, taken, near)
        high, low = split(near)
        pooled = jnp.dot(
            jnp.concatenate([high.astype(BF), low.astype(BF)], axis=1),
            pool[...],
            preferred_element_type=F32,
        )
        at = rest * level_scale
        floor = jnp.floor(at)
        weight = at - floor
        index = floor.astype(jnp.int32) + first
        lower = jnp.take_along_axis(pooled, index, axis=1, mode="promise_in_bounds")
        upper = jnp.take_along_axis(pooled, index + 1, axis=1, mode="promise_in_bounds")
        return lower + weight * (upper - lower)

    for y in range(ROWS):
        left = from_left[32 * y : 32 * y + 32, :].astype(F32)
        right = from_right[32 * y : 32 * y + 32, :].astype(F32)
        far = from_far[32 * y : 32 * y + 32, :].astype(F32)[:, :FAR]
        f0 = own[y].astype(F32)[:, :TILE]
        f1 = own[ROWS + y].astype(F32)[:, :TILE]
        blank = jnp.zeros((32, WINDOW - 1 - LAST), F32)
        win1 = jnp.concatenate(
            [far * far_scale_left, left[:, :TILE], f1, right[:, TILE : TILE + NEAR], blank], axis=1
        )
        win0 = jnp.concatenate(
            [left[:, TILE : TILE + NEAR], f0, right[:, :TILE], far * far_scale_right, blank], axis=1
        )
        query0 = win0[:, NEAR - PAD : NEAR - PAD + EXT]
        query1 = win1[:, FAR + TILE - PAD : FAR + TILE - PAD + EXT]
        for v, query, window in ((0, query0, win1), (1, query1, win0)):
            stacked = jnp.concatenate([query, query[:16]], axis=0)
            stacked = jnp.concatenate(
                [
                    jnp.concatenate([stacked, jnp.zeros((48, 256 - EXT), F32)], axis=1),
                    jnp.zeros((80, 256), F32),
                ],
                axis=0,
            ).T.astype(BF)
            layer = silu_of_half(
                jnp.dot(stacked[:EXT, :48], w1[...], preferred_element_type=F32)
            ).astype(BF)
            features = jnp.dot(layer, w2[...], preferred_element_type=F32).astype(BF)
            stacked = jnp.concatenate([window, window[:16]], axis=0).astype(BF)
            layer = silu_of_half(
                jnp.dot(w1t[:, :48], stacked, preferred_element_type=F32)
            ).astype(BF)
            match = jnp.dot(w2t[...], layer, preferred_element_type=F32).astype(BF)
            scores = jnp.dot(features, match, preferred_element_type=F32)
            depth = depths[:EXT, 2 * v + y : 2 * v + y + 1]
            look = lookups(scores, depth, v)
            high, low = split(look)
            half = 0.5 * (
                jnp.dot(
                    jnp.where(is_low, low, high).astype(BF), mw[...], preferred_element_type=F32
                )
                + depth * depth_scale
                + bias[...]
            )
            value = jnp.where(inside, silu_of_half(half), 0.0)
            out[v, y] = jnp.concatenate(
                [edge_of(edge_left, v, y), value[8 : EXT - 8], edge_of(edge_right, v, y)], axis=0
            ).astype(BF)


def update_kernel(
    hidden, context, hc_up, hc_down, mot, mot_up, mot_down, gate_k, cand_k, head, new, inc, state, reset
):
    def mot_of(v, yy):
        if yy < 2:
            return mot_up[v, yy]
        if yy < 4:
            return mot[v, yy - 2]
        return mot_down[v, yy - 4]

    def widened(middle, value, shift_left, shift_right):
        ends_left = pltpu.roll(value[0:16].astype(F32), shift_left, 0).astype(BF)
        ends_right = pltpu.roll(value[EXT - 16 :].astype(F32), shift_right, 0).astype(BF)
        return jnp.concatenate([ends_left, middle, ends_right], axis=0)

    def spread(products, width, v):
        before, at, after = (products[:, width * b : width * b + width] for b in range(3))
        if v == 1:
            before, after = after, before
        return pltpu.roll(before, 1, 0) + at + pltpu.roll(after, EXT - 1, 0)

    gate_all = jnp.concatenate(
        [jnp.concatenate([gate_k[a, b] for a in range(3)], axis=0) for b in range(3)], axis=1
    )
    gate_reset = jnp.concatenate(
        [
            jnp.concatenate([gate_k[a, b, :, UNITS:] for a in range(3)], axis=0)
            for b in range(3)
        ],
        axis=1,
    )
    cand_all = jnp.concatenate(
        [jnp.concatenate([cand_k[a, b] for a in range(3)], axis=0) for b in range(3)], axis=1
    )
    head_rows = jnp.broadcast_to(head[...].astype(F32), (8, UNITS)).astype(BF)
    for v in range(2):
        for yy in range(6):
            if yy < 2:
                middle = hc_up[v, yy]
            elif yy < 4:
                middle = hidden[v, yy - 2]
            else:
                middle = hc_down[v, yy - 4]
            state[v, yy] = widened(middle, mot_of(v, yy), 14, 8)
        gates = [None, None]
        for yy in range(1, 5):
            stacked = jnp.concatenate(
                [piece for k in (yy - 1, yy, yy + 1) for piece in (state[v, k], mot_of(v, k))],
                axis=1,
            )
            if yy in (2, 3):
                terms = spread(
                    jnp.dot(stacked, gate_all, preferred_element_type=F32), 2 * UNITS, v
                )
                gates[yy - 2] = terms[PAD : PAD + TILE, :UNITS]
                terms = terms[:, UNITS:]
                own_context = context[v, yy - 2, :, UNITS : 2 * UNITS]
            else:
                terms = spread(jnp.dot(stacked, gate_reset, preferred_element_type=F32), UNITS, v)
                own_context = hc_up[v, ROWS] if yy == 1 else hc_down[v, ROWS]
            wide = widened(own_context, mot_of(v, yy), 13, 6)
            gate = sigmoid(terms + wide.astype(F32))
            reset[v, yy - 1] = (gate * state[v, yy].astype(F32)).astype(BF)
        for y in range(ROWS):
            stacked = jnp.concatenate(
                [piece for k in range(3) for piece in (reset[v, y + k], mot_of(v, y + 1 + k))],
                axis=1,
            )
            terms = spread(jnp.dot(stacked, cand_all, preferred_element_type=F32), UNITS, v)
            candidate = jnp.tanh(
                terms[PAD : PAD + TILE] + context[v, y, :, 2 * UNITS :].astype(F32)
            )
            update = sigmoid(gates[y] + context[v, y, :, :UNITS].astype(F32))
            old = hidden[v, y].astype(F32)
            fresh = ((1.0 - update) * old + update * candidate).astype(BF)
            new[v, y] = fresh
            inc[v, y : y + 1, :] = lax.dot_general(
                head_rows, fresh, (((1,), (1,)), ((), ())), preferred_element_type=F32
            )[0:1]


def call(kernel, outs, in_specs=None, scratch=(), **cost):
    return pl.pallas_call(
        kernel,
        **({} if in_specs is None else {"in_specs": in_specs}),
        out_shape=[jax.ShapeDtypeStruct(shape, dtype) for shape, dtype in outs],
        scratch_shapes=list(scratch),
        compiler_params=pltpu.CompilerParams(vmem_limit_bytes=VMEM_LIMIT),
        cost_estimate=pl.CostEstimate(transcendentals=0, **cost),
    )


def local(
    voxels,
    disparity,
    hidden,
    context,
    embed_first,
    embed_bias,
    embed_second,
    motion_weight,
    motion_scale,
    motion_bias,
    gate_kernel,
    candidate_kernel,
    head_weight,
):
    cols = lax.axis_size("col")
    rows = lax.axis_size("row")
    onward = [(i, i + 1) for i in range(cols - 1)]
    back = [(i + 1, i) for i in range(cols - 1)]
    across = [(i, (i + 2) % cols) for i in range(cols)]
    downward = [(i, i + 1) for i in range(rows - 1)]
    upward = [(i + 1, i) for i in range(rows - 1)]
    pool, lane_rows = tables()

    (own, right, left, far, down, up, w1, w1t, w2, w2t, mw, pool, lane_rows, scale, bias, disp) = call(
        pack_kernel,
        [
            ((4, 32, 256), BF),
            ((80, 256), BF),
            ((80, 256), BF),
            ((64, 128), BF),
            ((2, ROWS + 1, TILE, UNITS), BF),
            ((2, ROWS + 1, TILE, UNITS), BF),
            ((48, 256), BF),
            ((256, 128), BF),
            ((256, 256), BF),
            ((256, 256), BF),
            ((128, 128), BF),
            ((256, 128), BF),
            ((8, 128), F32),
            ((1, 128), F32),
            ((1, 128), F32),
            ((2, ROWS, TILE), F32),
        ],
        in_specs=[pl.BlockSpec(memory_space=pltpu.MemorySpace.HBM)] * 12,
        scratch=[
            pltpu.VMEM((2, BINS, ROWS, TILE), F32),
            pltpu.VMEM((BINS, 256), F32),
            pltpu.VMEM((1, 256), F32),
            pltpu.VMEM((LEVELS * TAPS, 128), F32),
            pltpu.SemaphoreType.DMA((18,)),
        ],
        flops=10**6,
        bytes_accessed=2 * 10**6,
    )(
        *(
            pltpu.with_memory_space_constraint(x, pltpu.MemorySpace.HBM)
            for x in (
                voxels,
                disparity,
                hidden,
                context,
                embed_first,
                embed_bias.reshape(1, -1),
                embed_second,
                motion_weight,
                motion_scale.reshape(1, -1),
                motion_bias.reshape(1, -1),
                jnp.asarray(pool),
                jnp.asarray(lane_rows),
            )
        )
    )
    from_left = lax.ppermute(right, "col", onward)
    from_right = lax.ppermute(left, "col", back)
    from_far = lax.ppermute(far, "col", across)
    hc_up = lax.ppermute(down, "row", downward)
    hc_down = lax.ppermute(up, "row", upward)
    (motion,) = call(
        motion_kernel,
        [((2, ROWS, EXT, UNITS), BF)],
        flops=10**9,
        bytes_accessed=10**6,
    )(own, from_left, from_right, from_far, disp, w1, w1t, w2, w2t, mw, scale, bias, pool, lane_rows)
    motion_up = lax.ppermute(motion, "row", downward)
    motion_down = lax.ppermute(motion, "row", upward)
    new_hidden, increment = call(
        update_kernel,
        [((2, ROWS, TILE, UNITS), BF), ((2, ROWS, TILE), F32)],
        scratch=[pltpu.VMEM((2, 6, EXT, UNITS), BF), pltpu.VMEM((2, 4, EXT, UNITS), BF)],
        flops=2 * 10**9,
        bytes_accessed=4 * 10**6,
    )(
        hidden,
        context,
        hc_up,
        hc_down,
        motion,
        motion_up,
        motion_down,
        gate_kernel,
        candidate_kernel,
        head_weight.reshape(1, -1),
    )
    return new_hidden, increment


def solution(mesh):
    band = ("pair", "row")
    in_specs = (
        P(None, None, band, "col"),
        P(None, band, "col"),
        P(None, band, "col", None),
        P(None, band, "col", None),
    ) + (P(),) * 9
    out_specs = (P(None, band, "col", None), P(None, band, "col"))
    return jax.shard_map(local, mesh=mesh, in_specs=in_specs, out_specs=out_specs, check_vma=False)
```

```python
import functools

import jax
import jax.numpy as jnp
import numpy as np
from jax import lax
from jax.experimental import pallas as pl
from jax.experimental.pallas import tpu as pltpu
from jax.sharding import PartitionSpec as P

BF = jnp.bfloat16
F32 = jnp.float32

ROWS = 2
TILE = 160
IMAGE = 640
PAD = 16
EXT = TILE + 2 * PAD
BINS = 15
UNITS = 128
NEAR = 48
FAR = 72
WINDOW = 512
LAST = FAR + 2 * TILE + NEAR - 1
TAPS = 9
LEVELS = 4
GROUP = 40
STARTS = (0, 17, 30, 41)
VMEM_LIMIT = 48 * 1024 * 1024


def tables():
    pool = np.zeros((128, 128), np.float32)
    firsts = (28, 12, 4, 0)
    counts = (17, 13, 11, 10)
    for level in range(LEVELS):
        width = 2**level
        for k in range(counts[level]):
            entry = firsts[level] + k
            pool[entry * width : (entry + 1) * width, STARTS[level] + k] = 1.0 / (16 * width)
    lane = np.arange(128)
    member = lane % GROUP
    used = (member < LEVELS * TAPS) & (lane < 3 * GROUP)
    level = np.where(used, member // TAPS, 0)
    first = np.where(used, np.take(np.array(STARTS), level) + member % TAPS, 0)
    scale = np.where(used, 0.5**level, 0.0)
    low = ((lane >= GROUP) & (lane < 2 * GROUP)).astype(np.float32)
    rows = np.zeros((8, 128), np.float32)
    rows[0], rows[1], rows[2] = first, scale, low
    return np.concatenate([pool, pool]).astype(jnp.bfloat16), rows


def split(value):
    high = value.astype(BF).astype(F32)
    return high, value - high


def silu_of_half(half):
    return half + half * jnp.tanh(half)


def sigmoid(value):
    return 0.5 * jnp.tanh(0.5 * value) + 0.5


def pack_kernel(
    vox_h,
    disp_h,
    hidden_h,
    context_h,
    first_h,
    bias_h,
    second_h,
    motion_h,
    scale_h,
    mbias_h,
    pool_h,
    rows_h,
    own,
    odd_out,
    even_out,
    far,
    hid,
    con,
    w1,
    w1t,
    w2,
    w2t,
    mw,
    pool,
    rows,
    scale,
    mbias,
    disp,
    vox,
    first,
    bias,
    motion,
    sems,
):
    pairs = [
        (vox_h, vox),
        (disp_h, disp),
        (hidden_h, hid),
        (context_h.at[:, :, :, UNITS : 2 * UNITS], con),
    ]
    data = len(pairs)
    pairs += [
        (first_h, first),
        (bias_h, bias),
        (second_h, w2),
        (motion_h, motion),
        (scale_h, scale),
        (mbias_h, mbias),
        (pool_h, pool),
        (rows_h, rows),
    ]
    copies = [pltpu.make_async_copy(a, b, sems.at[k]) for k, (a, b) in enumerate(pairs)]
    for copy in copies:
        copy.start()
    for copy in copies[:data]:
        copy.wait()
    col = lax.axis_index("col")
    is_even = col % 2 == 0
    row_at = lax.broadcasted_iota(jnp.int32, (8, 128), 0)
    parts = []
    edges_right, edges_left = [], []
    for v in range(2):
        for y in range(ROWS):
            high, low = split(vox[v, :, y, :])
            ones = jnp.ones((1, TILE), F32)
            block = jnp.concatenate([high, ones, low, ones], axis=0)
            parts.append(block)
            own[2 * v + y] = jnp.concatenate(
                [block, jnp.zeros((32, 256 - TILE), F32)], axis=1
            ).astype(BF)
            hid_last = pltpu.roll(hid[v, y, 144:160, :].astype(F32)[8:16], 2, 0)
            con_last = pltpu.roll(con[v, y, 144:160, :].astype(F32)[8:16], 3, 0)
            hid_first = hid[v, y, 0:16, :].astype(F32)[0:8]
            con_first = pltpu.roll(con[v, y, 0:16, :].astype(F32)[0:8], 2, 0)
            depth = disp[v, y : y + 1, :]
            d_last = pltpu.roll(jnp.broadcast_to(depth[:, 32:160], (8, 128)), 8, 1)
            d_first = jnp.broadcast_to(depth[:, 0:128], (8, 128))

            def edge(hid, con, dis):
                d_high, rest = split(dis)
                d_mid, d_low = split(rest)
                out = jnp.where(row_at < 2, hid, con)
                out = jnp.where(row_at == 3, d_high, out)
                out = jnp.where(row_at == 4, d_mid, out)
                return jnp.where(row_at >= 5, d_low, out)

            edges_right.append(edge(hid_last, con_last, d_last))
            edges_left.append(edge(hid_first, con_first, d_first))

    def emit(at, to_right, to_left):
        odd_out[at, :] = jnp.where(is_even, to_right, to_left).astype(BF)
        even_out[at, :] = jnp.where(is_even, to_left, to_right).astype(BF)

    blank = jnp.zeros((32, 256 - TILE - NEAR), F32)
    for y in range(ROWS):
        f0, f1 = parts[y], parts[ROWS + y]
        rows_at = pl.ds(32 * y, 32)
        emit(
            rows_at,
            jnp.concatenate([f1, f0[:, TILE - NEAR :], blank], axis=1),
            jnp.concatenate([f0, f1[:, :NEAR], blank], axis=1),
        )
        tail = jnp.concatenate([f1[:, TILE - FAR :], jnp.zeros((32, 128 - FAR), F32)], axis=1)
        far[rows_at, :] = jnp.where(col < 2, tail, f0[:, :128]).astype(BF)

    def gathered(edges):
        return jnp.concatenate(
            [
                jnp.concatenate([edges[0], edges[1]], axis=0),
                jnp.concatenate([edges[2], edges[3]], axis=0),
            ],
            axis=1,
        )

    emit(pl.ds(64, 16), gathered(edges_right), gathered(edges_left))
    for copy in copies[data:]:
        copy.wait()
    w_high, w_low = split(first[...] * 0.5)
    b_high, rest = split(bias[...] * 0.5)
    b_mid, b_low = split(rest)
    stacked = jnp.concatenate([w_high, b_high, w_high, b_mid, w_low, b_low], axis=0)
    w1[...] = stacked.astype(BF)
    w1t[...] = jnp.concatenate([stacked, jnp.zeros((80, 256), F32)], axis=0).T.astype(BF)
    w2t[...] = w2[...].astype(F32).T.astype(BF)
    m_high, m_low = split(motion[...])
    gap = jnp.zeros((GROUP - LEVELS * TAPS, 128), F32)
    mw[...] = jnp.concatenate(
        [m_high, gap, m_high, gap, m_low, gap, jnp.zeros((8, 128), F32)], axis=0
    ).astype(BF)


def motion_kernel(
    v,
    own,
    odd_in,
    even_in,
    far_in,
    hid,
    con,
    disp,
    w1,
    w1t,
    w2,
    w2t,
    mw,
    scale,
    bias,
    pool,
    rows,
    chip_out,
    link_out,
):
    col = lax.axis_index("col")
    is_even = col % 2 == 0
    row_even = lax.axis_index("row") % 2 == 0

    def received(at, lanes):
        first, second = odd_in[at, lanes].astype(F32), even_in[at, lanes].astype(F32)
        left = jnp.where(col > 0, jnp.where(is_even, second, first), 0.0)
        right = jnp.where(col < 3, jnp.where(is_even, first, second), 0.0)
        return left, right

    lanes = pl.ds(128 * v, 128)
    edge_left, edge_right = received(pl.ds(64, 16), lanes)
    edges = [
        (edge_left[8 * y : 8 * y + 8], edge_right[8 * y : 8 * y + 8]) for y in range(ROWS)
    ]
    depth_rows = []
    for y in range(ROWS):
        e_l, e_r = edges[y]
        d_l = e_l[3:4] + e_l[4:5] + e_l[5:6]
        d_r = e_r[3:4] + e_r[4:5] + e_r[5:6]
        depth_rows.append(
            jnp.concatenate(
                [
                    jnp.zeros((1, 8), F32),
                    d_l[:, :8],
                    disp[v, y : y + 1, :],
                    d_r[:, :8],
                    jnp.zeros((1, 72), F32),
                ],
                axis=1,
            )
        )
    depth_rows.append(jnp.zeros((8 - ROWS, 256), F32))
    depths = jnp.concatenate(depth_rows, axis=0).T

    first = rows[0:1, :].astype(jnp.int32)
    level_scale = rows[1:2, :]
    is_low = rows[2:3, :] > 0.5
    lane = lax.broadcasted_iota(jnp.int32, (EXT, 128), 1)
    pixel = lax.broadcasted_iota(jnp.int32, (EXT, 1), 0)
    column = pixel + (col * TILE - PAD)
    inside = (column >= 0) & (column < IMAGE)
    pixel = pixel.astype(F32)
    depth_scale = scale[...] * (1.0 / 192.0)

    def lookups(scores, depth):
        spot = (pixel - PAD if v == 0 else (EXT - 1 - PAD) - pixel) - depth
        eighth = jnp.floor(spot * 0.125)
        rest = spot - 8.0 * eighth
        start = (8.0 * eighth).astype(jnp.int32) + (FAR + TILE - 32)
        index = start + lane if v == 0 else (LAST - start) - lane
        block, place = index >> 7, index & 127
        near = jnp.zeros((EXT, 128), F32)
        for k in range(WINDOW // 128):
            taken = jnp.take_along_axis(
                scores[:, 128 * k : 128 * k + 128], place, axis=1, mode="promise_in_bounds"
            )
            near = jnp.where(block == k, taken, near)
        high, low = split(near)
        pooled = jnp.dot(
            jnp.concatenate([high.astype(BF), low.astype(BF)], axis=1),
            pool[...],
            preferred_element_type=F32,
        )
        at = rest * level_scale
        floor = jnp.floor(at)
        weight = at - floor
        index = floor.astype(jnp.int32) + first
        lower = jnp.take_along_axis(pooled, index, axis=1, mode="promise_in_bounds")
        upper = jnp.take_along_axis(pooled, index + 1, axis=1, mode="promise_in_bounds")
        return lower + weight * (upper - lower)

    for y in range(ROWS):
        e_l, e_r = edges[y]
        pad8 = jnp.zeros((8, 128), F32)
        for k, value, to_last, to_first in ((y, hid, 6, 0), (2, con, 5, 6)):
            before = jnp.concatenate([pad8, pltpu.roll(e_l, to_last, 0)], axis=0).astype(BF)
            after = pltpu.roll(e_r, to_first, 0) if to_first else e_r
            after = jnp.concatenate([after, pad8], axis=0).astype(BF)
            if k == 2:

                @pl.when(row_even == (y == 1))
                def _(before=before, after=after):
                    chip_out[2, 0:PAD] = before
                    chip_out[2, PAD : PAD + TILE] = con[v, y]
                    chip_out[2, PAD + TILE :] = after

                @pl.when(row_even == (y == 0))
                def _(before=before, after=after):
                    link_out[2, 0:PAD] = before
                    link_out[2, PAD : PAD + TILE] = con[v, y]
                    link_out[2, PAD + TILE :] = after

            else:
                for target in (chip_out, link_out):
                    target[k, 0:PAD] = before
                    target[k, PAD : PAD + TILE] = value[v, y]
                    target[k, PAD + TILE :] = after
    for y in range(ROWS):
        left, right = received(pl.ds(32 * y, 32), slice(None))
        far = far_in[32 * y : 32 * y + 32, :].astype(F32)[:, :FAR]
        mine, other = own[ROWS * v + y].astype(F32), own[ROWS * (1 - v) + y].astype(F32)[:, :TILE]
        blank = jnp.zeros((32, WINDOW - 1 - LAST), F32)
        if v == 0:
            far = jnp.where(col >= 2, far, 0.0)
            pieces = [far, left[:, :TILE], other, right[:, TILE : TILE + NEAR], blank]
            ends = (left[:, TILE + NEAR - PAD : TILE + NEAR], right[:, :PAD])
        else:
            far = jnp.where(col < 2, far, 0.0)
            pieces = [left[:, TILE : TILE + NEAR], other, right[:, :TILE], far, blank]
            ends = (left[:, TILE - PAD : TILE], right[:, TILE : TILE + PAD])
        window = jnp.concatenate(pieces, axis=1)
        query = jnp.concatenate([ends[0], mine[:, :TILE], ends[1]], axis=1)
        stacked = jnp.concatenate([query, query[:16]], axis=0)
        stacked = jnp.concatenate(
            [
                jnp.concatenate([stacked, jnp.zeros((48, 256 - EXT), F32)], axis=1),
                jnp.zeros((80, 256), F32),
            ],
            axis=0,
        ).T.astype(BF)
        layer = silu_of_half(
            jnp.dot(stacked[:EXT, :48], w1[...], preferred_element_type=F32)
        ).astype(BF)
        features = jnp.dot(layer, w2[...], preferred_element_type=F32).astype(BF)
        stacked = jnp.concatenate([window, window[:16]], axis=0).astype(BF)
        layer = silu_of_half(
            jnp.dot(w1t[:, :48], stacked, preferred_element_type=F32)
        ).astype(BF)
        match = jnp.dot(w2t[...], layer, preferred_element_type=F32).astype(BF)
        scores = jnp.dot(features, match, preferred_element_type=F32)
        depth = depths[:EXT, y : y + 1]
        look = lookups(scores, depth)
        high, low = split(look)
        half = 0.5 * (
            jnp.dot(jnp.where(is_low, low, high).astype(BF), mw[...], preferred_element_type=F32)
            + depth * depth_scale
            + bias[...]
        )
        value = jnp.where(inside, silu_of_half(half), 0.0).astype(BF)
        chip_out[3 + y] = value
        link_out[3 + y] = value


def update_kernel(
    v,
    hidden,
    context,
    chip_own,
    link_own,
    chip_in,
    link_in,
    gate_k,
    cand_k,
    head,
    *refs,
):
    if v == 1:
        new_before, inc_before, new, inc, halo, reset = refs
        new[0] = new_before[...]
        inc[0] = inc_before[...]
        new, inc = new.at[1], inc.at[1]
    else:
        new, inc, halo, reset = refs
    row = lax.axis_index("row")
    row_even = row % 2 == 0
    last = lax.axis_size("row") - 1
    blank = jnp.zeros((5, EXT, UNITS), BF)

    @pl.when(row_even)
    def _():
        halo[0] = jnp.where(row > 0, link_in[...], blank)
        halo[1] = chip_in[...]

    @pl.when(jnp.logical_not(row_even))
    def _():
        halo[0] = chip_in[...]
        halo[1] = jnp.where(row < last, link_in[...], blank)

    def pick(k, yy):
        if yy < 2:
            return halo[0, k + yy]
        if yy < 4:
            return chip_own[k + yy - 2]
        return halo[1, k + yy - 4]

    def con_of(yy):
        if yy == 1:
            return halo[0, 2]
        if yy == 4:
            return halo[1, 2]
        near, far = chip_own[2].astype(F32), link_own[2].astype(F32)
        return jnp.where(row_even == (yy == 3), near, far)

    def spread(products, width):
        before, at, after = (products[:, width * b : width * b + width] for b in range(3))
        if v == 1:
            before, after = after, before
        return pltpu.roll(before, 1, 0) + at + pltpu.roll(after, EXT - 1, 0)

    gate_all = jnp.concatenate(
        [jnp.concatenate([gate_k[a, b] for a in range(3)], axis=0) for b in range(3)], axis=1
    )
    gate_reset = jnp.concatenate(
        [
            jnp.concatenate([gate_k[a, b, :, UNITS:] for a in range(3)], axis=0)
            for b in range(3)
        ],
        axis=1,
    )
    cand_all = jnp.concatenate(
        [jnp.concatenate([cand_k[a, b] for a in range(3)], axis=0) for b in range(3)], axis=1
    )
    head_rows = jnp.broadcast_to(head[...].astype(F32), (8, UNITS)).astype(BF)
    gates = [None, None]
    for yy in range(1, 5):
        stacked = jnp.concatenate(
            [piece for k in (yy - 1, yy, yy + 1) for piece in (pick(0, k), pick(3, k))], axis=1
        )
        if yy in (2, 3):
            terms = spread(jnp.dot(stacked, gate_all, preferred_element_type=F32), 2 * UNITS)
            gates[yy - 2] = terms[PAD : PAD + TILE, :UNITS]
            terms = terms[:, UNITS:]
        else:
            terms = spread(jnp.dot(stacked, gate_reset, preferred_element_type=F32), UNITS)
        gate = sigmoid(terms + con_of(yy).astype(F32))
        reset[yy - 1] = (gate * pick(0, yy).astype(F32)).astype(BF)
    for y in range(ROWS):
        stacked = jnp.concatenate(
            [piece for k in range(3) for piece in (reset[y + k], pick(3, y + 1 + k))], axis=1
        )
        terms = spread(jnp.dot(stacked, cand_all, preferred_element_type=F32), UNITS)
        candidate = jnp.tanh(terms[PAD : PAD + TILE] + context[v, y, :, 2 * UNITS :].astype(F32))
        update = sigmoid(gates[y] + context[v, y, :, :UNITS].astype(F32))
        old = hidden[v, y].astype(F32)
        fresh = ((1.0 - update) * old + update * candidate).astype(BF)
        new[y] = fresh
        inc[y : y + 1, :] = lax.dot_general(
            head_rows, fresh, (((1,), (1,)), ((), ())), preferred_element_type=F32
        )[0:1]


def call(kernel, outs, in_specs=None, scratch=(), **cost):
    return pl.pallas_call(
        kernel,
        **({} if in_specs is None else {"in_specs": in_specs}),
        out_shape=[jax.ShapeDtypeStruct(shape, dtype) for shape, dtype in outs],
        scratch_shapes=list(scratch),
        compiler_params=pltpu.CompilerParams(vmem_limit_bytes=VMEM_LIMIT),
        cost_estimate=pl.CostEstimate(transcendentals=0, **cost),
    )


def local(
    voxels,
    disparity,
    hidden,
    context,
    embed_first,
    embed_bias,
    embed_second,
    motion_weight,
    motion_scale,
    motion_bias,
    gate_kernel,
    candidate_kernel,
    head_weight,
):
    cols = lax.axis_size("col")
    rows = lax.axis_size("row")
    odd = [(i, i ^ 1) for i in range(cols)]
    even = [(i, (cols - 1) - i) for i in range(cols)]
    across = [(i, (i + 2) % cols) for i in range(cols)]
    chip = [(i, i ^ 1) for i in range(rows)]
    link = [(0, 0), (rows - 1, rows - 1)]
    link += [(i, ((i + 1) ^ 1) - 1) for i in range(1, rows - 1)]
    pool, lane_rows = tables()

    (own, odd_out, even_out, far, hid, con, w1, w1t, w2, w2t, mw, pool, lane_rows, scale, bias, disp) = call(
        pack_kernel,
        [
            ((4, 32, 256), BF),
            ((80, 256), BF),
            ((80, 256), BF),
            ((64, 128), BF),
            ((2, ROWS, TILE, UNITS), BF),
            ((2, ROWS, TILE, UNITS), BF),
            ((48, 256), BF),
            ((256, 128), BF),
            ((256, 256), BF),
            ((256, 256), BF),
            ((128, 128), BF),
            ((256, 128), BF),
            ((8, 128), F32),
            ((1, 128), F32),
            ((1, 128), F32),
            ((2, ROWS, TILE), F32),
        ],
        in_specs=[pl.BlockSpec(memory_space=pltpu.MemorySpace.HBM)] * 12,
        scratch=[
            pltpu.VMEM((2, BINS, ROWS, TILE), F32),
            pltpu.VMEM((BINS, 256), F32),
            pltpu.VMEM((1, 256), F32),
            pltpu.VMEM((LEVELS * TAPS, 128), F32),
            pltpu.SemaphoreType.DMA((12,)),
        ],
        flops=10**6,
        bytes_accessed=2 * 10**6,
    )(
        *(
            pltpu.with_memory_space_constraint(x, pltpu.MemorySpace.HBM)
            for x in (
                voxels,
                disparity,
                hidden,
                context,
                embed_first,
                embed_bias.reshape(1, -1),
                embed_second,
                motion_weight,
                motion_scale.reshape(1, -1),
                motion_bias.reshape(1, -1),
                jnp.asarray(pool),
                jnp.asarray(lane_rows),
            )
        )
    )
    odd_in = lax.ppermute(odd_out, "col", odd)
    even_in = lax.ppermute(even_out, "col", even)
    far_in = lax.ppermute(far, "col", across)
    halos = []
    for v in range(2):
        chip_out, link_out = call(
            functools.partial(motion_kernel, v),
            [((5, EXT, UNITS), BF)] * 2,
            flops=5 * 10**8,
            bytes_accessed=10**6,
        )(own, odd_in, even_in, far_in, hid, con, disp, w1, w1t, w2, w2t, mw, scale, bias, pool, lane_rows)
        link_in = lax.ppermute(link_out, "row", link)
        chip_in = lax.ppermute(chip_out, "row", chip)
        halos.append((chip_out, link_out, chip_in, link_in))
    done = ()
    for v in range(2):
        lead = (2,) * v
        done = call(
            functools.partial(update_kernel, v),
            [(lead + (ROWS, TILE, UNITS), BF), (lead + (ROWS, TILE), F32)],
            scratch=[pltpu.VMEM((2, 5, EXT, UNITS), BF), pltpu.VMEM((4, EXT, UNITS), BF)],
            flops=10**9,
            bytes_accessed=4 * 10**6,
        )(
            hidden,
            context,
            *halos[v],
            gate_kernel,
            candidate_kernel,
            head_weight.reshape(1, -1),
            *done,
        )
    return tuple(done)


def solution(mesh):
    band = ("pair", "row")
    in_specs = (
        P(None, None, band, "col"),
        P(None, band, "col"),
        P(None, band, "col", None),
        P(None, band, "col", None),
    ) + (P(),) * 9
    out_specs = (P(None, band, "col", None), P(None, band, "col"))
    return jax.shard_map(local, mesh=mesh, in_specs=in_specs, out_specs=out_specs, check_vma=False)
```

```python
import functools

import jax
import jax.numpy as jnp
import numpy as np
from jax import lax
from jax.experimental import pallas as pl
from jax.experimental.pallas import tpu as pltpu
from jax.sharding import PartitionSpec as P

BF = jnp.bfloat16
F32 = jnp.float32

ROWS = 2
TILE = 160
IMAGE = 640
PAD = 16
EXT = TILE + 2 * PAD
BINS = 15
UNITS = 128
NEAR = 48
FAR = 72
WINDOW = 512
LAST = FAR + 2 * TILE + NEAR - 1
TAPS = 9
LEVELS = 4
GROUP = 40
STARTS = (0, 17, 30, 41)
VMEM_LIMIT = 48 * 1024 * 1024


def tables():
    pool = np.zeros((128, 128), np.float32)
    firsts = (28, 12, 4, 0)
    counts = (17, 13, 11, 10)
    for level in range(LEVELS):
        width = 2**level
        for k in range(counts[level]):
            entry = firsts[level] + k
            pool[entry * width : (entry + 1) * width, STARTS[level] + k] = 1.0 / (16 * width)
    lane = np.arange(128)
    member = lane % GROUP
    used = (member < LEVELS * TAPS) & (lane < 3 * GROUP)
    level = np.where(used, member // TAPS, 0)
    first = np.where(used, np.take(np.array(STARTS), level) + member % TAPS, 0)
    scale = np.where(used, 0.5**level, 0.0)
    low = ((lane >= GROUP) & (lane < 2 * GROUP)).astype(np.float32)
    rows = np.zeros((8, 128), np.float32)
    rows[0], rows[1], rows[2] = first, scale, low
    return np.concatenate([pool, pool]).astype(jnp.bfloat16), rows


def split(value):
    high = value.astype(BF).astype(F32)
    return high, value - high


def silu_of_half(half):
    return half + half * jnp.tanh(half)


def sigmoid(value):
    return 0.5 * jnp.tanh(0.5 * value) + 0.5


def pack_kernel(
    vox_h,
    disp_h,
    hidden_h,
    context_h,
    first_h,
    bias_h,
    second_h,
    motion_h,
    scale_h,
    mbias_h,
    pool_h,
    rows_h,
    own,
    odd_out,
    even_out,
    far,
    hid,
    con,
    w1,
    w1t,
    w2,
    w2t,
    mw,
    pool,
    rows,
    scale,
    mbias,
    disp,
    vox,
    first,
    bias,
    motion,
    sems,
):
    pairs = [
        (vox_h, vox),
        (disp_h, disp),
        (hidden_h, hid),
        (context_h.at[:, :, :, UNITS : 2 * UNITS], con),
    ]
    data = len(pairs)
    pairs += [
        (first_h, first),
        (bias_h, bias),
        (second_h, w2),
        (motion_h, motion),
        (scale_h, scale),
        (mbias_h, mbias),
        (pool_h, pool),
        (rows_h, rows),
    ]
    copies = [pltpu.make_async_copy(a, b, sems.at[k]) for k, (a, b) in enumerate(pairs)]
    for copy in copies:
        copy.start()
    for copy in copies[:data]:
        copy.wait()
    col = lax.axis_index("col")
    is_even = col % 2 == 0
    row_at = lax.broadcasted_iota(jnp.int32, (8, 128), 0)
    parts = []
    edges_right, edges_left = [], []
    for v in range(2):
        for y in range(ROWS):
            high, low = split(vox[v, :, y, :])
            ones = jnp.ones((1, TILE), F32)
            block = jnp.concatenate([high, ones, low, ones], axis=0)
            parts.append(block)
            own[2 * v + y] = jnp.concatenate(
                [block, jnp.zeros((32, 256 - TILE), F32)], axis=1
            ).astype(BF)
            hid_last = pltpu.roll(hid[v, y, 144:160, :].astype(F32)[8:16], 2, 0)
            con_last = pltpu.roll(con[v, y, 144:160, :].astype(F32)[8:16], 3, 0)
            hid_first = hid[v, y, 0:16, :].astype(F32)[0:8]
            con_first = pltpu.roll(con[v, y, 0:16, :].astype(F32)[0:8], 2, 0)
            depth = disp[v, y : y + 1, :]
            d_last = pltpu.roll(jnp.broadcast_to(depth[:, 32:160], (8, 128)), 8, 1)
            d_first = jnp.broadcast_to(depth[:, 0:128], (8, 128))

            def edge(hid, con, dis):
                d_high, rest = split(dis)
                d_mid, d_low = split(rest)
                out = jnp.where(row_at < 2, hid, con)
                out = jnp.where(row_at == 3, d_high, out)
                out = jnp.where(row_at == 4, d_mid, out)
                return jnp.where(row_at >= 5, d_low, out)

            edges_right.append(edge(hid_last, con_last, d_last))
            edges_left.append(edge(hid_first, con_first, d_first))

    def emit(at, to_right, to_left):
        odd_out[at, :] = jnp.where(is_even, to_right, to_left).astype(BF)
        even_out[at, :] = jnp.where(is_even, to_left, to_right).astype(BF)

    blank = jnp.zeros((32, 256 - TILE - NEAR), F32)
    for y in range(ROWS):
        f0, f1 = parts[y], parts[ROWS + y]
        rows_at = pl.ds(32 * y, 32)
        emit(
            rows_at,
            jnp.concatenate([f1, f0[:, TILE - NEAR :], blank], axis=1),
            jnp.concatenate([f0, f1[:, :NEAR], blank], axis=1),
        )
        tail = jnp.concatenate([f1[:, TILE - FAR :], jnp.zeros((32, 128 - FAR), F32)], axis=1)
        far[rows_at, :] = jnp.where(col < 2, tail, f0[:, :128]).astype(BF)

    def gathered(edges):
        return jnp.concatenate(
            [
                jnp.concatenate([edges[0], edges[1]], axis=0),
                jnp.concatenate([edges[2], edges[3]], axis=0),
            ],
            axis=1,
        )

    emit(pl.ds(64, 16), gathered(edges_right), gathered(edges_left))
    for copy in copies[data:]:
        copy.wait()
    w_high, w_low = split(first[...] * 0.5)
    b_high, rest = split(bias[...] * 0.5)
    b_mid, b_low = split(rest)
    stacked = jnp.concatenate([w_high, b_high, w_high, b_mid, w_low, b_low], axis=0)
    w1[...] = stacked.astype(BF)
    w1t[...] = jnp.concatenate([stacked, jnp.zeros((80, 256), F32)], axis=0).T.astype(BF)
    w2t[...] = w2[...].astype(F32).T.astype(BF)
    m_high, m_low = split(motion[...])
    gap = jnp.zeros((GROUP - LEVELS * TAPS, 128), F32)
    mw[...] = jnp.concatenate(
        [m_high, gap, m_high, gap, m_low, gap, jnp.zeros((8, 128), F32)], axis=0
    ).astype(BF)


def motion_kernel(
    v,
    own,
    odd_in,
    even_in,
    far_in,
    hid,
    con,
    disp,
    w1,
    w1t,
    w2,
    w2t,
    mw,
    scale,
    bias,
    pool,
    rows,
    chip_out,
    link_out,
):
    col = lax.axis_index("col")
    is_even = col % 2 == 0
    row_even = lax.axis_index("row") % 2 == 0

    def received(at, lanes):
        first, second = odd_in[at, lanes].astype(F32), even_in[at, lanes].astype(F32)
        left = jnp.where(col > 0, jnp.where(is_even, second, first), 0.0)
        right = jnp.where(col < 3, jnp.where(is_even, first, second), 0.0)
        return left, right

    lanes = pl.ds(128 * v, 128)
    edge_left, edge_right = received(pl.ds(64, 16), lanes)
    edges = [
        (edge_left[8 * y : 8 * y + 8], edge_right[8 * y : 8 * y + 8]) for y in range(ROWS)
    ]
    depth_rows = []
    for y in range(ROWS):
        e_l, e_r = edges[y]
        d_l = e_l[3:4] + e_l[4:5] + e_l[5:6]
        d_r = e_r[3:4] + e_r[4:5] + e_r[5:6]
        depth_rows.append(
            jnp.concatenate(
                [
                    jnp.zeros((1, 8), F32),
                    d_l[:, :8],
                    disp[v, y : y + 1, :],
                    d_r[:, :8],
                    jnp.zeros((1, 72), F32),
                ],
                axis=1,
            )
        )
    depth_rows.append(jnp.zeros((8 - ROWS, 256), F32))
    depths = jnp.concatenate(depth_rows, axis=0).T

    first = rows[0:1, :].astype(jnp.int32)
    level_scale = rows[1:2, :]
    is_low = rows[2:3, :] > 0.5
    lane = lax.broadcasted_iota(jnp.int32, (EXT, 128), 1)
    pixel = lax.broadcasted_iota(jnp.int32, (EXT, 1), 0)
    column = pixel + (col * TILE - PAD)
    inside = (column >= 0) & (column < IMAGE)
    pixel = pixel.astype(F32)
    depth_scale = scale[...] * (1.0 / 192.0)

    def lookups(scores, depth):
        spot = (pixel - PAD if v == 0 else (EXT - 1 - PAD) - pixel) - depth
        eighth = jnp.floor(spot * 0.125)
        rest = spot - 8.0 * eighth
        start = (8.0 * eighth).astype(jnp.int32) + (FAR + TILE - 32)
        index = start + lane if v == 0 else (LAST - start) - lane
        block, place = index >> 7, index & 127
        near = jnp.zeros((EXT, 128), F32)
        for k in range(WINDOW // 128):
            taken = jnp.take_along_axis(
                scores[:, 128 * k : 128 * k + 128], place, axis=1, mode="promise_in_bounds"
            )
            near = jnp.where(block == k, taken, near)
        high, low = split(near)
        pooled = jnp.dot(
            jnp.concatenate([high.astype(BF), low.astype(BF)], axis=1),
            pool[...],
            preferred_element_type=F32,
        )
        at = rest * level_scale
        floor = jnp.floor(at)
        weight = at - floor
        index = floor.astype(jnp.int32) + first
        lower = jnp.take_along_axis(pooled, index, axis=1, mode="promise_in_bounds")
        upper = jnp.take_along_axis(pooled, index + 1, axis=1, mode="promise_in_bounds")
        return lower + weight * (upper - lower)

    for y in range(ROWS):
        e_l, e_r = edges[y]
        pad8 = jnp.zeros((8, 128), F32)
        for k, value, to_last, to_first in ((y, hid, 6, 0), (2, con, 5, 6)):
            before = jnp.concatenate([pad8, pltpu.roll(e_l, to_last, 0)], axis=0).astype(BF)
            after = pltpu.roll(e_r, to_first, 0) if to_first else e_r
            after = jnp.concatenate([after, pad8], axis=0).astype(BF)
            if k == 2:

                @pl.when(row_even == (y == 1))
                def _(before=before, after=after):
                    chip_out[2, 0:PAD] = before
                    chip_out[2, PAD : PAD + TILE] = con[v, y]
                    chip_out[2, PAD + TILE :] = after

                @pl.when(row_even == (y == 0))
                def _(before=before, after=after):
                    link_out[2, 0:PAD] = before
                    link_out[2, PAD : PAD + TILE] = con[v, y]
                    link_out[2, PAD + TILE :] = after

            else:
                for target in (chip_out, link_out):
                    target[k, 0:PAD] = before
                    target[k, PAD : PAD + TILE] = value[v, y]
                    target[k, PAD + TILE :] = after
    for y in range(ROWS):
        left, right = received(pl.ds(32 * y, 32), slice(None))
        far = far_in[32 * y : 32 * y + 32, :].astype(F32)[:, :FAR]
        mine, other = own[ROWS * v + y].astype(F32), own[ROWS * (1 - v) + y].astype(F32)[:, :TILE]
        blank = jnp.zeros((32, WINDOW - 1 - LAST), F32)
        if v == 0:
            far = jnp.where(col >= 2, far, 0.0)
            pieces = [far, left[:, :TILE], other, right[:, TILE : TILE + NEAR], blank]
            ends = (left[:, TILE + NEAR - PAD : TILE + NEAR], right[:, :PAD])
        else:
            far = jnp.where(col < 2, far, 0.0)
            pieces = [left[:, TILE : TILE + NEAR], other, right[:, :TILE], far, blank]
            ends = (left[:, TILE - PAD : TILE], right[:, TILE : TILE + PAD])
        window = jnp.concatenate(pieces, axis=1)
        query = jnp.concatenate([ends[0], mine[:, :TILE], ends[1]], axis=1)
        stacked = jnp.concatenate([query, query[:16]], axis=0)
        stacked = jnp.concatenate(
            [
                jnp.concatenate([stacked, jnp.zeros((48, 256 - EXT), F32)], axis=1),
                jnp.zeros((80, 256), F32),
            ],
            axis=0,
        ).T.astype(BF)
        layer = silu_of_half(
            jnp.dot(stacked[:EXT, :48], w1[...], preferred_element_type=F32)
        ).astype(BF)
        features = jnp.dot(layer, w2[...], preferred_element_type=F32).astype(BF)
        stacked = jnp.concatenate([window, window[:16]], axis=0).astype(BF)
        layer = silu_of_half(
            jnp.dot(w1t[:, :48], stacked, preferred_element_type=F32)
        ).astype(BF)
        match = jnp.dot(w2t[...], layer, preferred_element_type=F32).astype(BF)
        scores = jnp.dot(features, match, preferred_element_type=F32)
        depth = depths[:EXT, y : y + 1]
        look = lookups(scores, depth)
        high, low = split(look)
        half = 0.5 * (
            jnp.dot(jnp.where(is_low, low, high).astype(BF), mw[...], preferred_element_type=F32)
            + depth * depth_scale
            + bias[...]
        )
        value = jnp.where(inside, silu_of_half(half), 0.0).astype(BF)
        chip_out[3 + y] = value
        link_out[3 + y] = value


def update_kernel(
    v,
    hidden,
    context,
    chip_own,
    link_own,
    chip_in,
    link_in,
    gate_k,
    cand_k,
    head,
    *refs,
):
    if v == 1:
        new_before, inc_before, new, inc, halo, reset = refs
        new[0] = new_before[...]
        inc[0] = inc_before[...]
        new, inc = new.at[1], inc.at[1]
    else:
        new, inc, halo, reset = refs
    row = lax.axis_index("row")
    row_even = row % 2 == 0
    last = lax.axis_size("row") - 1
    blank = jnp.zeros((5, EXT, UNITS), BF)

    @pl.when(row_even)
    def _():
        halo[0] = jnp.where(row > 0, link_in[...], blank)
        halo[1] = chip_in[...]

    @pl.when(jnp.logical_not(row_even))
    def _():
        halo[0] = chip_in[...]
        halo[1] = jnp.where(row < last, link_in[...], blank)

    def pick(k, yy):
        if yy < 2:
            return halo[0, k + yy]
        if yy < 4:
            return chip_own[k + yy - 2]
        return halo[1, k + yy - 4]

    def con_of(yy):
        if yy == 1:
            return halo[0, 2]
        if yy == 4:
            return halo[1, 2]
        near, far = chip_own[2].astype(F32), link_own[2].astype(F32)
        return jnp.where(row_even == (yy == 3), near, far)

    def spread(products, width):
        before, at, after = (products[:, width * b : width * b + width] for b in range(3))
        if v == 1:
            before, after = after, before
        return pltpu.roll(before, 1, 0) + at + pltpu.roll(after, EXT - 1, 0)

    gate_all = jnp.concatenate(
        [jnp.concatenate([gate_k[a, b] for a in range(3)], axis=0) for b in range(3)], axis=1
    )
    gate_reset = jnp.concatenate(
        [
            jnp.concatenate([gate_k[a, b, :, UNITS:] for a in range(3)], axis=0)
            for b in range(3)
        ],
        axis=1,
    )
    cand_all = jnp.concatenate(
        [jnp.concatenate([cand_k[a, b] for a in range(3)], axis=0) for b in range(3)], axis=1
    )
    head_rows = jnp.broadcast_to(head[...].astype(F32), (8, UNITS)).astype(BF)
    gates = [None, None]
    for yy in range(1, 5):
        stacked = jnp.concatenate(
            [piece for k in (yy - 1, yy, yy + 1) for piece in (pick(0, k), pick(3, k))], axis=1
        )
        if yy in (2, 3):
            terms = spread(jnp.dot(stacked, gate_all, preferred_element_type=F32), 2 * UNITS)
            gates[yy - 2] = terms[PAD : PAD + TILE, :UNITS]
            terms = terms[:, UNITS:]
        else:
            terms = spread(jnp.dot(stacked, gate_reset, preferred_element_type=F32), UNITS)
        gate = sigmoid(terms + con_of(yy).astype(F32))
        reset[yy - 1] = (gate * pick(0, yy).astype(F32)).astype(BF)
    for y in range(ROWS):
        stacked = jnp.concatenate(
            [piece for k in range(3) for piece in (reset[y + k], pick(3, y + 1 + k))], axis=1
        )
        terms = spread(jnp.dot(stacked, cand_all, preferred_element_type=F32), UNITS)
        candidate = jnp.tanh(terms[PAD : PAD + TILE] + context[v, y, :, 2 * UNITS :].astype(F32))
        update = sigmoid(gates[y] + context[v, y, :, :UNITS].astype(F32))
        old = hidden[v, y].astype(F32)
        fresh = ((1.0 - update) * old + update * candidate).astype(BF)
        new[y] = fresh
        inc[y : y + 1, :] = lax.dot_general(
            head_rows, fresh, (((1,), (1,)), ((), ())), preferred_element_type=F32
        )[0:1]


def call(kernel, outs, in_specs=None, scratch=(), **cost):
    return pl.pallas_call(
        kernel,
        **({} if in_specs is None else {"in_specs": in_specs}),
        out_shape=[jax.ShapeDtypeStruct(shape, dtype) for shape, dtype in outs],
        scratch_shapes=list(scratch),
        compiler_params=pltpu.CompilerParams(vmem_limit_bytes=VMEM_LIMIT),
        cost_estimate=pl.CostEstimate(transcendentals=0, **cost),
    )


def local(
    voxels,
    disparity,
    hidden,
    context,
    embed_first,
    embed_bias,
    embed_second,
    motion_weight,
    motion_scale,
    motion_bias,
    gate_kernel,
    candidate_kernel,
    head_weight,
):
    cols = lax.axis_size("col")
    rows = lax.axis_size("row")
    odd = [(i, i ^ 1) for i in range(cols)]
    across = [(i, (i + 2) % cols) for i in range(cols)]
    chip = [(i, i ^ 1) for i in range(rows)]

    even, link = [], []
    for r in range(rows):
        for c in range(cols):
            outer_col, outer_row = c in (0, cols - 1), r in (0, rows - 1)
            even.append((r * cols + c, (r ^ 1) * cols + c if outer_col else r * cols + ((c - 1) ^ 1) + 1))
            link.append((r * cols + c, r * cols + (c ^ 1) if outer_row else (((r - 1) ^ 1) + 1) * cols + c))

    pool, lane_rows = tables()

    (own, odd_out, even_out, far, hid, con, w1, w1t, w2, w2t, mw, pool, lane_rows, scale, bias, disp) = call(
        pack_kernel,
        [
            ((4, 32, 256), BF),
            ((80, 256), BF),
            ((80, 256), BF),
            ((64, 128), BF),
            ((2, ROWS, TILE, UNITS), BF),
            ((2, ROWS, TILE, UNITS), BF),
            ((48, 256), BF),
            ((256, 128), BF),
            ((256, 256), BF),
            ((256, 256), BF),
            ((128, 128), BF),
            ((256, 128), BF),
            ((8, 128), F32),
            ((1, 128), F32),
            ((1, 128), F32),
            ((2, ROWS, TILE), F32),
        ],
        in_specs=[pl.BlockSpec(memory_space=pltpu.MemorySpace.HBM)] * 12,
        scratch=[
            pltpu.VMEM((2, BINS, ROWS, TILE), F32),
            pltpu.VMEM((BINS, 256), F32),
            pltpu.VMEM((1, 256), F32),
            pltpu.VMEM((LEVELS * TAPS, 128), F32),
            pltpu.SemaphoreType.DMA((12,)),
        ],
        flops=10**6,
        bytes_accessed=2 * 10**6,
    )(
        *(
            pltpu.with_memory_space_constraint(x, pltpu.MemorySpace.HBM)
            for x in (
                voxels,
                disparity,
                hidden,
                context,
                embed_first,
                embed_bias.reshape(1, -1),
                embed_second,
                motion_weight,
                motion_scale.reshape(1, -1),
                motion_bias.reshape(1, -1),
                jnp.asarray(pool),
                jnp.asarray(lane_rows),
            )
        )
    )
    odd_in = lax.ppermute(odd_out, "col", odd)
    even_in = lax.ppermute(even_out, ("row", "col"), even)
    far_in = lax.ppermute(far, "col", across)
    halos = []
    for v in range(2):
        chip_out, link_out = call(
            functools.partial(motion_kernel, v),
            [((5, EXT, UNITS), BF)] * 2,
            flops=5 * 10**8,
            bytes_accessed=10**6,
        )(own, odd_in, even_in, far_in, hid, con, disp, w1, w1t, w2, w2t, mw, scale, bias, pool, lane_rows)
        link_in = lax.ppermute(link_out, ("row", "col"), link)
        chip_in = lax.ppermute(chip_out, "row", chip)
        halos.append((chip_out, link_out, chip_in, link_in))
    done = ()
    for v in range(2):
        lead = (2,) * v
        done = call(
            functools.partial(update_kernel, v),
            [(lead + (ROWS, TILE, UNITS), BF), (lead + (ROWS, TILE), F32)],
            scratch=[pltpu.VMEM((2, 5, EXT, UNITS), BF), pltpu.VMEM((4, EXT, UNITS), BF)],
            flops=10**9,
            bytes_accessed=4 * 10**6,
        )(
            hidden,
            context,
            *halos[v],
            gate_kernel,
            candidate_kernel,
            head_weight.reshape(1, -1),
            *done,
        )
    return tuple(done)


def solution(mesh):
    band = ("pair", "row")
    in_specs = (
        P(None, None, band, "col"),
        P(None, band, "col"),
        P(None, band, "col", None),
        P(None, band, "col", None),
    ) + (P(),) * 9
    out_specs = (P(None, band, "col", None), P(None, band, "col"))
    return jax.shard_map(local, mesh=mesh, in_specs=in_specs, out_specs=out_specs, check_vma=False)
```

```python
import jax
import jax.numpy as jnp
import numpy as np
from jax import lax
from jax.experimental import pallas as pl
from jax.experimental.pallas import tpu as pltpu
from jax.sharding import PartitionSpec as P

BF = jnp.bfloat16
F32 = jnp.float32

ROWS = 2
TILE = 160
IMAGE = 640
PAD = 16
EXT = TILE + 2 * PAD
BINS = 15
UNITS = 128
NEAR = 48
FAR = 72
WINDOW = 512
LAST = FAR + 2 * TILE + NEAR - 1
TAPS = 9
LEVELS = 4
GROUP = 40
STARTS = (0, 17, 30, 41)
VMEM_LIMIT = 48 * 1024 * 1024


def tables():
    pool = np.zeros((128, 128), np.float32)
    firsts = (28, 12, 4, 0)
    counts = (17, 13, 11, 10)
    for level in range(LEVELS):
        width = 2**level
        for k in range(counts[level]):
            entry = firsts[level] + k
            pool[entry * width : (entry + 1) * width, STARTS[level] + k] = 1.0 / (16 * width)
    lane = np.arange(128)
    member = lane % GROUP
    used = (member < LEVELS * TAPS) & (lane < 3 * GROUP)
    level = np.where(used, member // TAPS, 0)
    first = np.where(used, np.take(np.array(STARTS), level) + member % TAPS, 0)
    scale = np.where(used, 0.5**level, 0.0)
    low = ((lane >= GROUP) & (lane < 2 * GROUP)).astype(np.float32)
    rows = np.zeros((8, 128), np.float32)
    rows[0], rows[1], rows[2] = first, scale, low
    return np.concatenate([pool, pool]).astype(jnp.bfloat16), rows


def split(value):
    high = value.astype(BF).astype(F32)
    return high, value - high


def silu_of_half(half):
    return half + half * jnp.tanh(half)


def sigmoid(value):
    return 0.5 * jnp.tanh(0.5 * value) + 0.5


def pack_kernel(
    vox_h,
    disp_h,
    hidden_h,
    context_h,
    first_h,
    bias_h,
    second_h,
    motion_h,
    scale_h,
    mbias_h,
    pool_h,
    rows_h,
    own,
    odd_out,
    even_out,
    far,
    chip,
    link,
    w1,
    w1t,
    w2,
    w2t,
    mw,
    pool,
    rows,
    scale,
    mbias,
    disp,
    vox,
    first,
    bias,
    motion,
    sems,
):
    row_odd = lax.axis_index("row") % 2
    pairs = [(vox_h, vox), (disp_h, disp)]
    for v in range(2):
        for target, y in ((chip, 1 - row_odd), (link, row_odd)):
            pairs += [
                (hidden_h.at[v], target.at[v, 0:ROWS]),
                (context_h.at[v, y, :, UNITS : 2 * UNITS], target.at[v, ROWS]),
            ]
    data = len(pairs)
    pairs += [
        (first_h, first),
        (bias_h, bias),
        (second_h, w2),
        (motion_h, motion),
        (scale_h, scale),
        (mbias_h, mbias),
        (pool_h, pool),
        (rows_h, rows),
    ]
    copies = [pltpu.make_async_copy(a, b, sems.at[k]) for k, (a, b) in enumerate(pairs)]
    for copy in copies:
        copy.start()
    for copy in copies[:data]:
        copy.wait()
    col = lax.axis_index("col")
    is_even = col % 2 == 0
    row_at = lax.broadcasted_iota(jnp.int32, (8, 128), 0)
    parts = []
    edges_right, edges_left = [], []
    for v in range(2):
        for y in range(ROWS):
            high, low = split(vox[v, :, y, :])
            ones = jnp.ones((1, TILE), F32)
            block = jnp.concatenate([high, ones, low, ones], axis=0)
            parts.append(block)
            own[2 * v + y] = jnp.concatenate(
                [block, jnp.zeros((32, 256 - TILE), F32)], axis=1
            ).astype(BF)

            def context_at(at):
                on_chip, on_link = chip[v, ROWS, at].astype(F32), link[v, ROWS, at].astype(F32)
                return jnp.where(row_odd == y, on_link, on_chip)

            hid_last = pltpu.roll(chip[v, y, 144:160, :].astype(F32)[8:16], 2, 0)
            con_last = pltpu.roll(context_at(slice(144, 160))[8:16], 3, 0)
            hid_first = chip[v, y, 0:16, :].astype(F32)[0:8]
            con_first = pltpu.roll(context_at(slice(0, 16))[0:8], 2, 0)
            depth = disp[v, y : y + 1, :]
            d_last = pltpu.roll(jnp.broadcast_to(depth[:, 32:160], (8, 128)), 8, 1)
            d_first = jnp.broadcast_to(depth[:, 0:128], (8, 128))

            def edge(hid, con, dis):
                d_high, rest = split(dis)
                d_mid, d_low = split(rest)
                out = jnp.where(row_at < 2, hid, con)
                out = jnp.where(row_at == 3, d_high, out)
                out = jnp.where(row_at == 4, d_mid, out)
                return jnp.where(row_at >= 5, d_low, out)

            edges_right.append(edge(hid_last, con_last, d_last))
            edges_left.append(edge(hid_first, con_first, d_first))

    def emit(at, to_right, to_left):
        odd_out[at, :] = jnp.where(is_even, to_right, to_left).astype(BF)
        even_out[at, :] = jnp.where(is_even, to_left, to_right).astype(BF)

    blank = jnp.zeros((32, 256 - TILE - NEAR), F32)
    for y in range(ROWS):
        f0, f1 = parts[y], parts[ROWS + y]
        rows_at = pl.ds(32 * y, 32)
        emit(
            rows_at,
            jnp.concatenate([f1, f0[:, TILE - NEAR :], blank], axis=1),
            jnp.concatenate([f0, f1[:, :NEAR], blank], axis=1),
        )
        tail = jnp.concatenate([f1[:, TILE - FAR :], jnp.zeros((32, 128 - FAR), F32)], axis=1)
        far[rows_at, :] = jnp.where(col < 2, tail, f0[:, :128]).astype(BF)

    def gathered(edges):
        return jnp.concatenate(
            [
                jnp.concatenate([edges[0], edges[1]], axis=0),
                jnp.concatenate([edges[2], edges[3]], axis=0),
            ],
            axis=1,
        )

    emit(pl.ds(64, 16), gathered(edges_right), gathered(edges_left))
    for copy in copies[data:]:
        copy.wait()
    w_high, w_low = split(first[...] * 0.5)
    b_high, rest = split(bias[...] * 0.5)
    b_mid, b_low = split(rest)
    stacked = jnp.concatenate([w_high, b_high, w_high, b_mid, w_low, b_low], axis=0)
    block = jnp.concatenate([stacked, jnp.zeros((16, 256), F32)], axis=0).astype(BF)
    empty = jnp.zeros((64, 256), BF)
    for k in range(4):
        for m in range(4):
            w1[64 * k : 64 * k + 64, 256 * m : 256 * m + 256] = block if k == m else empty
    w1t[...] = jnp.concatenate([stacked, jnp.zeros((80, 256), F32)], axis=0).T.astype(BF)
    w2t[...] = w2[...].astype(F32).T.astype(BF)
    m_high, m_low = split(motion[...])
    gap = jnp.zeros((GROUP - LEVELS * TAPS, 128), F32)
    mw[...] = jnp.concatenate(
        [m_high, gap, m_high, gap, m_low, gap, jnp.zeros((8, 128), F32)], axis=0
    ).astype(BF)


def motion_kernel(
    own,
    odd_in,
    even_in,
    far_in,
    disp,
    w1,
    w1t,
    w2,
    w2t,
    mw,
    scale,
    bias,
    pool,
    rows,
    out,
):
    col = lax.axis_index("col")
    is_even = col % 2 == 0

    def received(at):
        first, second = odd_in[at, :].astype(F32), even_in[at, :].astype(F32)
        left = jnp.where(col > 0, jnp.where(is_even, second, first), 0.0)
        right = jnp.where(col < 3, jnp.where(is_even, first, second), 0.0)
        return left, right

    cases = [(v, y) for v in range(2) for y in range(ROWS)]
    edge_left, edge_right = received(pl.ds(64, 16))
    edges = [
        tuple(e[8 * y : 8 * y + 8, 128 * v : 128 * v + 128] for e in (edge_left, edge_right))
        for v, y in cases
    ]
    depth_rows = []
    for (v, y), (e_l, e_r) in zip(cases, edges):
        d_l = e_l[3:4] + e_l[4:5] + e_l[5:6]
        d_r = e_r[3:4] + e_r[4:5] + e_r[5:6]
        depth_rows.append(
            jnp.concatenate(
                [
                    jnp.zeros((1, 8), F32),
                    d_l[:, :8],
                    disp[v, y : y + 1, :],
                    d_r[:, :8],
                    jnp.zeros((1, 72), F32),
                ],
                axis=1,
            )
        )
    depth_rows.append(jnp.zeros((4, 256), F32))
    depths = jnp.concatenate(depth_rows, axis=0).T

    blank = jnp.zeros((32, WINDOW - 1 - LAST), F32)
    sides = [received(pl.ds(32 * y, 32)) for y in range(ROWS)]
    queries, windows = [], []
    for v, y in cases:
        left, right = sides[y]
        far = far_in[32 * y : 32 * y + 32, :].astype(F32)[:, :FAR]
        mine = own[ROWS * v + y].astype(F32)[:, :TILE]
        other = own[ROWS * (1 - v) + y].astype(F32)[:, :TILE]
        if v == 0:
            far = jnp.where(col >= 2, far, 0.0)
            pieces = [far, left[:, :TILE], other, right[:, TILE : TILE + NEAR], blank]
            ends = (left[:, TILE + NEAR - PAD : TILE + NEAR], right[:, :PAD])
        else:
            far = jnp.where(col < 2, far, 0.0)
            pieces = [left[:, TILE : TILE + NEAR], other, right[:, :TILE], far, blank]
            ends = (left[:, TILE - PAD : TILE], right[:, TILE : TILE + PAD])
        window = jnp.concatenate(pieces, axis=1)
        windows.append(jnp.concatenate([window, window[:16]], axis=0).astype(BF))
        query = jnp.concatenate([ends[0], mine, ends[1], jnp.zeros((32, 256 - EXT), F32)], axis=1)
        queries += [query, query[:16], jnp.zeros((16, 256), F32)]

    stacked = jnp.concatenate(queries, axis=0).T.astype(BF)
    layer = silu_of_half(jnp.dot(stacked[:EXT], w1[...], preferred_element_type=F32)).astype(BF)
    layer = jnp.concatenate([layer[:, 256 * k : 256 * k + 256] for k in range(4)], axis=0)
    features = jnp.dot(layer, w2[...], preferred_element_type=F32).astype(BF)
    layer = silu_of_half(
        jnp.dot(w1t[:, :48], jnp.concatenate(windows, axis=1), preferred_element_type=F32)
    ).astype(BF)
    match = jnp.dot(w2t[...], layer, preferred_element_type=F32).astype(BF)

    first = rows[0:1, :].astype(jnp.int32)
    level_scale = rows[1:2, :]
    is_low = rows[2:3, :] > 0.5
    lane = lax.broadcasted_iota(jnp.int32, (EXT, 128), 1)
    pixel = lax.broadcasted_iota(jnp.int32, (EXT, 1), 0)
    column = pixel + (col * TILE - PAD)
    inside = (column >= 0) & (column < IMAGE)
    pixel = pixel.astype(F32)
    depth_scale = scale[...] * (1.0 / 192.0)

    nears, rests = [], []
    for k, (v, y) in enumerate(cases):
        scores = jnp.dot(
            features[EXT * k : EXT * k + EXT],
            match[:, WINDOW * k : WINDOW * k + WINDOW],
            preferred_element_type=F32,
        )
        spot = (pixel - PAD if v == 0 else (EXT - 1 - PAD) - pixel) - depths[:EXT, k : k + 1]
        eighth = jnp.floor(spot * 0.125)
        rests.append(spot - 8.0 * eighth)
        start = (8.0 * eighth).astype(jnp.int32) + (FAR + TILE - 32)
        index = start + lane if v == 0 else (LAST - start) - lane
        block, place = index >> 7, index & 127
        near = jnp.zeros((EXT, 128), F32)
        for m in range(WINDOW // 128):
            taken = jnp.take_along_axis(
                scores[:, 128 * m : 128 * m + 128], place, axis=1, mode="promise_in_bounds"
            )
            near = jnp.where(block == m, taken, near)
        high, low = split(near)
        nears.append(jnp.concatenate([high.astype(BF), low.astype(BF)], axis=1))
    pooled = jnp.dot(jnp.concatenate(nears, axis=0), pool[...], preferred_element_type=F32)
    looks = []
    for k in range(4):
        table = pooled[EXT * k : EXT * k + EXT]
        at = rests[k] * level_scale
        floor = jnp.floor(at)
        index = floor.astype(jnp.int32) + first
        lower = jnp.take_along_axis(table, index, axis=1, mode="promise_in_bounds")
        upper = jnp.take_along_axis(table, index + 1, axis=1, mode="promise_in_bounds")
        high, low = split(lower + (at - floor) * (upper - lower))
        looks.append(jnp.where(is_low, low, high).astype(BF))
    sums = jnp.dot(jnp.concatenate(looks, axis=0), mw[...], preferred_element_type=F32)
    for k, (v, y) in enumerate(cases):
        half = 0.5 * (
            sums[EXT * k : EXT * k + EXT] + depths[:EXT, k : k + 1] * depth_scale + bias[...]
        )
        value = jnp.where(inside, silu_of_half(half), 0.0)
        e_l, e_r = edges[k]
        out[v, y] = jnp.concatenate([e_l, value[8 : EXT - 8], e_r], axis=0).astype(BF)


def widened(middle, ends, shift_left, shift_right):
    before = pltpu.roll(ends[0:16].astype(F32), shift_left, 0).astype(BF)
    after = pltpu.roll(ends[EXT - 16 :].astype(F32), shift_right, 0).astype(BF)
    return jnp.concatenate([before, middle, after], axis=0)


def wide_hidden(middle, ends):
    return widened(middle, ends, 14, 8)


def wide_context(middle, ends):
    return widened(middle, ends, 13, 6)


def kernel_rows(kernel, rows, inputs=slice(None), outputs=slice(None)):
    return jnp.concatenate(
        [
            jnp.concatenate([kernel[a, b, inputs, outputs] for a in rows], axis=0)
            for b in range(3)
        ],
        axis=1,
    )


def convolved(pieces, weights):
    stacked = jnp.concatenate(
        [jnp.concatenate([piece[v] for piece in pieces], axis=1) for v in range(2)], axis=0
    )
    products = jnp.dot(stacked, weights, preferred_element_type=F32)
    width = weights.shape[1] // 3
    out = []
    for v in range(2):
        mine = products[EXT * v : EXT * v + EXT]
        before, at, after = (mine[:, width * b : width * b + width] for b in range(3))
        if v == 1:
            before, after = after, before
        out.append(pltpu.roll(before, 1, 0) + at + pltpu.roll(after, EXT - 1, 0))
    return out


RESET = slice(UNITS, 2 * UNITS)
FROM_STATE, FROM_MOTION = slice(0, UNITS), slice(UNITS, 2 * UNITS)


def inner_kernel(hidden, context, mot, gate_k, cand_k, gates, outer, cands, state):
    for v in range(2):
        for y in range(ROWS):
            state[v, y] = wide_hidden(hidden[v, y], mot[v, y])
    h2, h3 = ([state[v, y] for v in range(2)] for y in range(ROWS))
    m2, m3 = ([mot[v, y] for v in range(2)] for y in range(ROWS))
    for y, rows in ((0, (1, 2)), (1, (0, 1))):
        terms = convolved([h2, m2, h3, m3], kernel_rows(gate_k, rows))
        for v in range(2):
            wide = wide_context(context[v, y, :, RESET], mot[v, y])
            gates[v, y, :, :UNITS] = terms[v][:, :UNITS]
            gates[v, y, :, UNITS:] = terms[v][:, UNITS:] + wide.astype(F32)
        terms = convolved([m2, m3], kernel_rows(cand_k, rows, FROM_MOTION))
        for v in range(2):
            cands[v, y] = terms[v][PAD : PAD + TILE] + context[v, y, :, 2 * UNITS :].astype(F32)
    for side, pieces, rows in ((0, [h2, m2], (2,)), (1, [h3, m3], (0,))):
        terms = convolved(pieces, kernel_rows(gate_k, rows, outputs=RESET))
        for v in range(2):
            outer[v, side] = terms[v]


def outer_kernel(
    hidden,
    context,
    chip_in,
    link_in,
    mot_chip,
    mot_link,
    gates,
    outer,
    cands,
    state,
    gate_k,
    cand_k,
    head,
    new,
    inc,
    halo,
    halo_mot,
):
    row = lax.axis_index("row")
    row_even = row % 2 == 0
    last = lax.axis_size("row") - 1

    @pl.when(row_even)
    def _():
        halo[0] = jnp.where(row > 0, link_in[...], jnp.zeros_like(link_in))
        halo[1] = chip_in[...]
        halo_mot[0] = jnp.where(row > 0, mot_link[...], jnp.zeros_like(mot_link))
        halo_mot[1] = mot_chip[...]

    @pl.when(jnp.logical_not(row_even))
    def _():
        halo[0] = chip_in[...]
        halo[1] = jnp.where(row < last, link_in[...], jnp.zeros_like(link_in))
        halo_mot[0] = mot_chip[...]
        halo_mot[1] = jnp.where(row < last, mot_link[...], jnp.zeros_like(mot_link))

    def beyond(side, y):
        mots = [halo_mot[side, v, y] for v in range(2)]
        return [wide_hidden(halo[side, v, y], mots[v]) for v in range(2)], mots

    h0, m0 = beyond(0, 0)
    h1, m1 = beyond(0, 1)
    h4, m4 = beyond(1, 0)
    h5, m5 = beyond(1, 1)
    updates, resets = [], []
    for side, pieces, rows in ((0, [h0, m0, h1, m1], (0, 1)), (1, [h4, m4, h5, m5], (1, 2))):
        terms = convolved(pieces, kernel_rows(gate_k, rows, outputs=RESET))
        near_h, near_m = (h1, m1) if side == 0 else (h4, m4)
        resets.append([])
        for v in range(2):
            wide = wide_context(halo[side, v, ROWS], near_m[v]).astype(F32)
            gate = sigmoid(terms[v] + outer[v, side] + wide)
            resets[-1].append((gate * near_h[v].astype(F32)).astype(BF))
    for y, pieces, rows in ((0, [h1, m1], (0,)), (1, [h4, m4], (2,))):
        terms = convolved(pieces, kernel_rows(gate_k, rows))
        updates.append([])
        resets.append([])
        for v in range(2):
            both = terms[v] + gates[v, y]
            gate = sigmoid(both[:, UNITS:])
            resets[-1].append((gate * state[v, y].astype(F32)).astype(BF))
            updates[-1].append(
                sigmoid(
                    both[PAD : PAD + TILE, :UNITS] + context[v, y, :, :UNITS].astype(F32)
                )
            )
    r1, r4, r2, r3 = resets
    head_rows = jnp.broadcast_to(head[...].astype(F32), (8, UNITS)).astype(BF)
    for y, pieces, row_at in ((0, [r1, r2, r3, m1], 0), (1, [r2, r3, r4, m4], 2)):
        weights = jnp.concatenate(
            [
                kernel_rows(cand_k, (0, 1, 2), FROM_STATE),
                kernel_rows(cand_k, (row_at,), FROM_MOTION),
            ],
            axis=0,
        )
        terms = convolved(pieces, weights)
        for v in range(2):
            candidate = jnp.tanh(terms[v][PAD : PAD + TILE] + cands[v, y])
            old = hidden[v, y].astype(F32)
            update = updates[y][v]
            fresh = ((1.0 - update) * old + update * candidate).astype(BF)
            new[v, y] = fresh
            inc[v, y : y + 1, :] = lax.dot_general(
                head_rows, fresh, (((1,), (1,)), ((), ())), preferred_element_type=F32
            )[0:1]


def call(kernel, outs, in_specs=None, scratch=(), **cost):
    return pl.pallas_call(
        kernel,
        **({} if in_specs is None else {"in_specs": in_specs}),
        out_shape=[jax.ShapeDtypeStruct(shape, dtype) for shape, dtype in outs],
        scratch_shapes=list(scratch),
        compiler_params=pltpu.CompilerParams(vmem_limit_bytes=VMEM_LIMIT),
        cost_estimate=pl.CostEstimate(transcendentals=0, **cost),
    )


def local(
    voxels,
    disparity,
    hidden,
    context,
    embed_first,
    embed_bias,
    embed_second,
    motion_weight,
    motion_scale,
    motion_bias,
    gate_kernel,
    candidate_kernel,
    head_weight,
):
    cols = lax.axis_size("col")
    rows = lax.axis_size("row")
    odd = [(i, i ^ 1) for i in range(cols)]
    across = [(i, (i + 2) % cols) for i in range(cols)]
    chip = [(i, i ^ 1) for i in range(rows)]

    even, link = [], []
    for r in range(rows):
        for c in range(cols):
            outer_col, outer_row = c in (0, cols - 1), r in (0, rows - 1)
            even.append((r * cols + c, (r ^ 1) * cols + c if outer_col else r * cols + ((c - 1) ^ 1) + 1))
            link.append((r * cols + c, r * cols + (c ^ 1) if outer_row else (((r - 1) ^ 1) + 1) * cols + c))

    pool, lane_rows = tables()

    (own, odd_out, even_out, far, chip_out, link_out, w1, w1t, w2, w2t, mw, pool, lane_rows, scale, bias, disp) = call(
        pack_kernel,
        [
            ((4, 32, 256), BF),
            ((80, 256), BF),
            ((80, 256), BF),
            ((64, 128), BF),
            ((2, ROWS + 1, TILE, UNITS), BF),
            ((2, ROWS + 1, TILE, UNITS), BF),
            ((256, 1024), BF),
            ((256, 128), BF),
            ((256, 256), BF),
            ((256, 256), BF),
            ((128, 128), BF),
            ((256, 128), BF),
            ((8, 128), F32),
            ((1, 128), F32),
            ((1, 128), F32),
            ((2, ROWS, TILE), F32),
        ],
        in_specs=[pl.BlockSpec(memory_space=pltpu.MemorySpace.HBM)] * 12,
        scratch=[
            pltpu.VMEM((2, BINS, ROWS, TILE), F32),
            pltpu.VMEM((BINS, 256), F32),
            pltpu.VMEM((1, 256), F32),
            pltpu.VMEM((LEVELS * TAPS, 128), F32),
            pltpu.SemaphoreType.DMA((18,)),
        ],
        flops=10**6,
        bytes_accessed=2 * 10**6,
    )(
        *(
            pltpu.with_memory_space_constraint(x, pltpu.MemorySpace.HBM)
            for x in (
                voxels,
                disparity,
                hidden,
                context,
                embed_first,
                embed_bias.reshape(1, -1),
                embed_second,
                motion_weight,
                motion_scale.reshape(1, -1),
                motion_bias.reshape(1, -1),
                jnp.asarray(pool),
                jnp.asarray(lane_rows),
            )
        )
    )
    odd_in = lax.ppermute(odd_out, "col", odd)
    even_in = lax.ppermute(even_out, ("row", "col"), even)
    far_in = lax.ppermute(far, "col", across)
    link_in = lax.ppermute(link_out, ("row", "col"), link)
    chip_in = lax.ppermute(chip_out, "row", chip)
    (mot,) = call(
        motion_kernel,
        [((2, ROWS, EXT, UNITS), BF)],
        flops=10**9,
        bytes_accessed=10**6,
    )(own, odd_in, even_in, far_in, disp, w1, w1t, w2, w2t, mw, scale, bias, pool, lane_rows)
    mot_link = lax.ppermute(mot, ("row", "col"), link)
    mot_chip = lax.ppermute(mot, "row", chip)
    gates, outer, cands, state = call(
        inner_kernel,
        [
            ((2, ROWS, EXT, 2 * UNITS), F32),
            ((2, 2, EXT, UNITS), F32),
            ((2, ROWS, TILE, UNITS), F32),
            ((2, ROWS, EXT, UNITS), BF),
        ],
        flops=10**9,
        bytes_accessed=4 * 10**6,
    )(hidden, context, mot, gate_kernel, candidate_kernel)
    return tuple(
        call(
            outer_kernel,
            [((2, ROWS, TILE, UNITS), BF), ((2, ROWS, TILE), F32)],
            scratch=[
                pltpu.VMEM((2, 2, ROWS + 1, TILE, UNITS), BF),
                pltpu.VMEM((2, 2, ROWS, EXT, UNITS), BF),
            ],
            flops=10**9,
            bytes_accessed=4 * 10**6,
        )(
            hidden,
            context,
            chip_in,
            link_in,
            mot_chip,
            mot_link,
            gates,
            outer,
            cands,
            state,
            gate_kernel,
            candidate_kernel,
            head_weight.reshape(1, -1),
        )
    )


def solution(mesh):
    band = ("pair", "row")
    in_specs = (
        P(None, None, band, "col"),
        P(None, band, "col"),
        P(None, band, "col", None),
        P(None, band, "col", None),
    ) + (P(),) * 9
    out_specs = (P(None, band, "col", None), P(None, band, "col"))
    return jax.shard_map(local, mesh=mesh, in_specs=in_specs, out_specs=out_specs, check_vma=False)
```

```python
import jax
import jax.numpy as jnp
import numpy as np
from jax import lax
from jax.experimental import pallas as pl
from jax.experimental.pallas import tpu as pltpu
from jax.sharding import PartitionSpec as P

BF = jnp.bfloat16
F32 = jnp.float32

ROWS = 2
TILE = 160
IMAGE = 640
PAD = 16
EXT = TILE + 2 * PAD
BINS = 15
UNITS = 128
NEAR = 48
FAR = 72
WINDOW = 512
LAST = FAR + 2 * TILE + NEAR - 1
TAPS = 9
LEVELS = 4
GROUP = 40
STARTS = (0, 17, 30, 41)
VMEM_LIMIT = 48 * 1024 * 1024


def tables():
    pool = np.zeros((128, 256), np.float32)
    firsts = (28, 12, 4, 0)
    counts = (17, 13, 11, 10)
    for level in range(LEVELS):
        width = 2**level
        for k in range(counts[level]):
            entry = firsts[level] + k
            weight = 1.0 / (16 * width)
            pool[entry * width : (entry + 1) * width, STARTS[level] + k] = weight
            pool[entry * width : (entry + 1) * width, 128 + STARTS[level] + k] = -weight
            if k:
                pool[entry * width : (entry + 1) * width, 127 + STARTS[level] + k] = weight
    lane = np.arange(128)
    member = lane % GROUP
    used = (member < LEVELS * TAPS) & (lane < 3 * GROUP)
    level = np.where(used, member // TAPS, 0)
    first = np.where(used, np.take(np.array(STARTS), level) + member % TAPS, 0)
    scale = np.where(used, 0.5**level, 0.0)
    low = ((lane >= GROUP) & (lane < 2 * GROUP)).astype(np.float32)
    rows = np.zeros((8, 128), np.float32)
    rows[0], rows[1], rows[2] = first, scale, low
    for level in range(LEVELS):
        rows[3, STARTS[level] : STARTS[level] + counts[level]] = 0.5**level
    return np.concatenate([pool, pool]).astype(jnp.bfloat16), rows


def split(value):
    high = value.astype(BF).astype(F32)
    return high, value - high


def silu_of_half(half):
    return half + half * jnp.tanh(half)


def sigmoid(value):
    return 0.5 * jnp.tanh(0.5 * value) + 0.5


def pack_kernel(
    vox_h,
    disp_h,
    hidden_h,
    context_h,
    first_h,
    bias_h,
    second_h,
    motion_h,
    scale_h,
    mbias_h,
    pool_h,
    rows_h,
    own,
    odd_out,
    even_out,
    far,
    chip,
    link,
    first,
    bias,
    w2,
    motion,
    pool,
    rows,
    scale,
    mbias,
    disp,
    vox,
    sems,
):
    row_odd = lax.axis_index("row") % 2
    pairs = [(vox_h, vox), (disp_h, disp)]
    for v in range(2):
        for target, y in ((chip, 1 - row_odd), (link, row_odd)):
            pairs += [
                (hidden_h.at[v], target.at[v, 0:ROWS]),
                (context_h.at[v, y, :, UNITS : 2 * UNITS], target.at[v, ROWS]),
            ]
    data = len(pairs)
    pairs += [
        (first_h, first),
        (bias_h, bias),
        (second_h, w2),
        (motion_h, motion),
        (scale_h, scale),
        (mbias_h, mbias),
        (pool_h, pool),
        (rows_h, rows),
    ]
    copies = [pltpu.make_async_copy(a, b, sems.at[k]) for k, (a, b) in enumerate(pairs)]
    for copy in copies:
        copy.start()
    for copy in copies[:2]:
        copy.wait()
    col = lax.axis_index("col")
    is_even = col % 2 == 0

    def emit(at, to_right, to_left):
        odd_out[at, :] = jnp.where(is_even, to_right, to_left).astype(BF)
        even_out[at, :] = jnp.where(is_even, to_left, to_right).astype(BF)

    parts = []
    for v in range(2):
        for y in range(ROWS):
            high, low = split(vox[v, :, y, :])
            ones = jnp.ones((1, TILE), F32)
            block = jnp.concatenate([high, ones, low, ones], axis=0)
            parts.append(block)
            own[2 * v + y] = jnp.concatenate(
                [block, jnp.zeros((32, 256 - TILE), F32)], axis=1
            ).astype(BF)
    blank = jnp.zeros((32, 256 - TILE - NEAR), F32)
    for y in range(ROWS):
        f0, f1 = parts[y], parts[ROWS + y]
        rows_at = pl.ds(32 * y, 32)
        emit(
            rows_at,
            jnp.concatenate([f1, f0[:, TILE - NEAR :], blank], axis=1),
            jnp.concatenate([f0, f1[:, :NEAR], blank], axis=1),
        )
        tail = jnp.concatenate([f1[:, TILE - FAR :], jnp.zeros((32, 128 - FAR), F32)], axis=1)
        far[rows_at, :] = jnp.where(col < 2, tail, f0[:, :128]).astype(BF)

    for copy in copies[2:data]:
        copy.wait()
    row_at = lax.broadcasted_iota(jnp.int32, (8, 128), 0)
    edges_right, edges_left = [], []
    for v in range(2):
        for y in range(ROWS):

            def context_at(at):
                on_chip, on_link = chip[v, ROWS, at].astype(F32), link[v, ROWS, at].astype(F32)
                return jnp.where(row_odd == y, on_link, on_chip)

            hid_last = pltpu.roll(chip[v, y, 144:160, :].astype(F32)[8:16], 2, 0)
            con_last = pltpu.roll(context_at(slice(144, 160))[8:16], 3, 0)
            hid_first = chip[v, y, 0:16, :].astype(F32)[0:8]
            con_first = pltpu.roll(context_at(slice(0, 16))[0:8], 2, 0)
            depth = disp[v, y : y + 1, :]
            d_last = pltpu.roll(jnp.broadcast_to(depth[:, 32:160], (8, 128)), 8, 1)
            d_first = jnp.broadcast_to(depth[:, 0:128], (8, 128))

            def edge(hid, con, dis):
                d_high, rest = split(dis)
                d_mid, d_low = split(rest)
                out = jnp.where(row_at < 2, hid, con)
                out = jnp.where(row_at == 3, d_high, out)
                out = jnp.where(row_at == 4, d_mid, out)
                return jnp.where(row_at >= 5, d_low, out)

            edges_right.append(edge(hid_last, con_last, d_last))
            edges_left.append(edge(hid_first, con_first, d_first))

    def gathered(edges):
        return jnp.concatenate(
            [
                jnp.concatenate([edges[0], edges[1]], axis=0),
                jnp.concatenate([edges[2], edges[3]], axis=0),
            ],
            axis=1,
        )

    emit(pl.ds(64, 16), gathered(edges_right), gathered(edges_left))
    for copy in copies[data:]:
        copy.wait()


def weight_kernel(first, bias, w2, motion, w1, w1t, w2t, mw):
    w_high, w_low = split(first[...] * 0.5)
    b_high, rest = split(bias[...] * 0.5)
    b_mid, b_low = split(rest)
    stacked = jnp.concatenate([w_high, b_high, w_high, b_mid, w_low, b_low], axis=0)
    block = jnp.concatenate([stacked, jnp.zeros((16, 256), F32)], axis=0).astype(BF)
    empty = jnp.zeros((64, 256), BF)
    for k in range(4):
        for m in range(4):
            w1[64 * k : 64 * k + 64, 256 * m : 256 * m + 256] = block if k == m else empty
    w1t[...] = jnp.concatenate([stacked, jnp.zeros((80, 256), F32)], axis=0).T.astype(BF)
    w2t[...] = w2[...].astype(F32).T.astype(BF)
    m_high, m_low = split(motion[...])
    gap = jnp.zeros((GROUP - LEVELS * TAPS, 128), F32)
    mw[...] = jnp.concatenate(
        [m_high, gap, m_high, gap, m_low, gap, jnp.zeros((8, 128), F32)], axis=0
    ).astype(BF)


def motion_kernel(
    own,
    odd_in,
    even_in,
    far_in,
    disp,
    w1,
    w1t,
    w2,
    w2t,
    mw,
    scale,
    bias,
    pool,
    rows,
    out,
):
    col = lax.axis_index("col")
    is_even = col % 2 == 0

    def received(at):
        first, second = odd_in[at, :].astype(F32), even_in[at, :].astype(F32)
        left = jnp.where(col > 0, jnp.where(is_even, second, first), 0.0)
        right = jnp.where(col < 3, jnp.where(is_even, first, second), 0.0)
        return left, right

    cases = [(v, y) for v in range(2) for y in range(ROWS)]
    edge_left, edge_right = received(pl.ds(64, 16))
    edges = [
        tuple(e[8 * y : 8 * y + 8, 128 * v : 128 * v + 128] for e in (edge_left, edge_right))
        for v, y in cases
    ]
    depth_rows = []
    for (v, y), (e_l, e_r) in zip(cases, edges):
        d_l = e_l[3:4] + e_l[4:5] + e_l[5:6]
        d_r = e_r[3:4] + e_r[4:5] + e_r[5:6]
        depth_rows.append(
            jnp.concatenate(
                [
                    jnp.zeros((1, 8), F32),
                    d_l[:, :8],
                    disp[v, y : y + 1, :],
                    d_r[:, :8],
                    jnp.zeros((1, 72), F32),
                ],
                axis=1,
            )
        )
    depth_rows.append(jnp.zeros((4, 256), F32))
    depths = jnp.concatenate(depth_rows, axis=0).T

    blank = jnp.zeros((32, WINDOW - 1 - LAST), F32)
    sides = [received(pl.ds(32 * y, 32)) for y in range(ROWS)]
    queries, windows = [], []
    for v, y in cases:
        left, right = sides[y]
        far = far_in[32 * y : 32 * y + 32, :].astype(F32)[:, :FAR]
        mine = own[ROWS * v + y].astype(F32)[:, :TILE]
        other = own[ROWS * (1 - v) + y].astype(F32)[:, :TILE]
        if v == 0:
            far = jnp.where(col >= 2, far, 0.0)
            pieces = [far, left[:, :TILE], other, right[:, TILE : TILE + NEAR], blank]
            ends = (left[:, TILE + NEAR - PAD : TILE + NEAR], right[:, :PAD])
        else:
            far = jnp.where(col < 2, far, 0.0)
            pieces = [left[:, TILE : TILE + NEAR], other, right[:, :TILE], far, blank]
            ends = (left[:, TILE - PAD : TILE], right[:, TILE : TILE + PAD])
        window = jnp.concatenate(pieces, axis=1)
        windows.append(jnp.concatenate([window, window[:16]], axis=0).astype(BF))
        query = jnp.concatenate([ends[0], mine, ends[1], jnp.zeros((32, 256 - EXT), F32)], axis=1)
        queries += [query, query[:16], jnp.zeros((16, 256), F32)]

    stacked = jnp.concatenate(queries, axis=0).T.astype(BF)
    layer = silu_of_half(jnp.dot(stacked[:EXT], w1[...], preferred_element_type=F32)).astype(BF)
    layer = jnp.concatenate([layer[:, 256 * k : 256 * k + 256] for k in range(4)], axis=0)
    features = jnp.dot(layer, w2[...], preferred_element_type=F32).astype(BF)
    layer = silu_of_half(
        jnp.dot(w1t[:, :48], jnp.concatenate(windows, axis=1), preferred_element_type=F32)
    ).astype(BF)
    match = jnp.dot(w2t[...], layer, preferred_element_type=F32).astype(BF)

    first = rows[0:1, :].astype(jnp.int32)
    level_scale = rows[1:2, :]
    is_low = rows[2:3, :] > 0.5
    entry_scale = rows[3:4, :]
    lane = lax.broadcasted_iota(jnp.int32, (EXT, 128), 1)
    pixel = lax.broadcasted_iota(jnp.int32, (EXT, 1), 0)
    column = pixel + (col * TILE - PAD)
    inside = (column >= 0) & (column < IMAGE)
    pixel = pixel.astype(F32)
    depth_scale = scale[...] * (1.0 / 192.0)

    nears, rests = [], []
    for k, (v, y) in enumerate(cases):
        scores = jnp.dot(
            features[EXT * k : EXT * k + EXT],
            match[:, WINDOW * k : WINDOW * k + WINDOW],
            preferred_element_type=F32,
        )
        spot = (pixel - PAD if v == 0 else (EXT - 1 - PAD) - pixel) - depths[:EXT, k : k + 1]
        eighth = jnp.floor(spot * 0.125)
        rests.append(spot - 8.0 * eighth)
        start = (8.0 * eighth).astype(jnp.int32) + (FAR + TILE - 32)
        if v == 0:
            block, place = (start + 127 - lane) >> 7, (start + lane) & 127
        else:
            index = (LAST - start) - lane
            block, place = index >> 7, index & 127
        source = scores[:, :128]
        for m in range(1, WINDOW // 128):
            source = jnp.where(block == m, scores[:, 128 * m : 128 * m + 128], source)
        near = jnp.take_along_axis(source, place, axis=1, mode="promise_in_bounds")
        high, low = split(near)
        nears.append(jnp.concatenate([high.astype(BF), low.astype(BF)], axis=1))
    pooled = jnp.dot(jnp.concatenate(nears, axis=0), pool[...], preferred_element_type=F32)
    looks = []
    for k in range(4):
        table = pooled[EXT * k : EXT * k + EXT]
        at = rests[k] * entry_scale
        table = table[:, :128] + (at - jnp.floor(at)) * table[:, 128:]
        index = jnp.floor(rests[k] * level_scale).astype(jnp.int32) + first
        high, low = split(jnp.take_along_axis(table, index, axis=1, mode="promise_in_bounds"))
        looks.append(jnp.where(is_low, low, high).astype(BF))
    sums = jnp.dot(jnp.concatenate(looks, axis=0), mw[...], preferred_element_type=F32)
    for k, (v, y) in enumerate(cases):
        half = 0.5 * (
            sums[EXT * k : EXT * k + EXT] + depths[:EXT, k : k + 1] * depth_scale + bias[...]
        )
        value = jnp.where(inside, silu_of_half(half), 0.0)
        e_l, e_r = edges[k]
        out[v, y] = jnp.concatenate([e_l, value[8 : EXT - 8], e_r], axis=0).astype(BF)


def widened(middle, ends, shift_left, shift_right):
    before = pltpu.roll(ends[0:16].astype(F32), shift_left, 0).astype(BF)
    after = pltpu.roll(ends[EXT - 16 :].astype(F32), shift_right, 0).astype(BF)
    return jnp.concatenate([before, middle, after], axis=0)


def wide_hidden(middle, ends):
    return widened(middle, ends, 14, 8)


def wide_context(middle, ends):
    return widened(middle, ends, 13, 6)


def kernel_rows(kernel, rows, inputs=slice(None), outputs=slice(None)):
    return jnp.concatenate(
        [
            jnp.concatenate([kernel[a, b, inputs, outputs] for a in rows], axis=0)
            for b in range(3)
        ],
        axis=1,
    )


def convolved(pieces, weights):
    stacked = jnp.concatenate(
        [jnp.concatenate([piece[v] for piece in pieces], axis=1) for v in range(2)], axis=0
    )
    products = jnp.dot(stacked, weights, preferred_element_type=F32)
    width = weights.shape[1] // 3
    out = []
    for v in range(2):
        mine = products[EXT * v : EXT * v + EXT]
        before, at, after = (mine[:, width * b : width * b + width] for b in range(3))
        if v == 1:
            before, after = after, before
        out.append(pltpu.roll(before, 1, 0) + at + pltpu.roll(after, EXT - 1, 0))
    return out


RESET = slice(UNITS, 2 * UNITS)
FROM_STATE, FROM_MOTION = slice(0, UNITS), slice(UNITS, 2 * UNITS)


def inner_kernel(hidden, context, mot, gate_k, cand_k, gates, outer, cands, state):
    for v in range(2):
        for y in range(ROWS):
            state[v, y] = wide_hidden(hidden[v, y], mot[v, y])
    h2, h3 = ([state[v, y] for v in range(2)] for y in range(ROWS))
    m2, m3 = ([mot[v, y] for v in range(2)] for y in range(ROWS))
    for y, rows in ((0, (1, 2)), (1, (0, 1))):
        terms = convolved([h2, m2, h3, m3], kernel_rows(gate_k, rows))
        for v in range(2):
            wide = wide_context(context[v, y, :, RESET], mot[v, y])
            gates[v, y, :, :UNITS] = terms[v][:, :UNITS]
            gates[v, y, :, UNITS:] = terms[v][:, UNITS:] + wide.astype(F32)
        terms = convolved([m2, m3], kernel_rows(cand_k, rows, FROM_MOTION))
        for v in range(2):
            cands[v, y] = terms[v][PAD : PAD + TILE] + context[v, y, :, 2 * UNITS :].astype(F32)
    for side, pieces, rows in ((0, [h2, m2], (2,)), (1, [h3, m3], (0,))):
        terms = convolved(pieces, kernel_rows(gate_k, rows, outputs=RESET))
        for v in range(2):
            outer[v, side] = terms[v]


def outer_kernel(
    hidden,
    context,
    chip_in,
    link_in,
    mot_chip,
    mot_link,
    gates,
    outer,
    cands,
    state,
    gate_k,
    cand_k,
    head,
    new,
    inc,
    halo,
    halo_mot,
):
    row = lax.axis_index("row")
    row_even = row % 2 == 0
    last = lax.axis_size("row") - 1

    @pl.when(row_even)
    def _():
        halo[0] = jnp.where(row > 0, link_in[...], jnp.zeros_like(link_in))
        halo[1] = chip_in[...]
        halo_mot[0] = jnp.where(row > 0, mot_link[...], jnp.zeros_like(mot_link))
        halo_mot[1] = mot_chip[...]

    @pl.when(jnp.logical_not(row_even))
    def _():
        halo[0] = chip_in[...]
        halo[1] = jnp.where(row < last, link_in[...], jnp.zeros_like(link_in))
        halo_mot[0] = mot_chip[...]
        halo_mot[1] = jnp.where(row < last, mot_link[...], jnp.zeros_like(mot_link))

    def beyond(side, y):
        mots = [halo_mot[side, v, y] for v in range(2)]
        return [wide_hidden(halo[side, v, y], mots[v]) for v in range(2)], mots

    h0, m0 = beyond(0, 0)
    h1, m1 = beyond(0, 1)
    h4, m4 = beyond(1, 0)
    h5, m5 = beyond(1, 1)
    updates, resets = [], []
    for side, pieces, rows in ((0, [h0, m0, h1, m1], (0, 1)), (1, [h4, m4, h5, m5], (1, 2))):
        terms = convolved(pieces, kernel_rows(gate_k, rows, outputs=RESET))
        near_h, near_m = (h1, m1) if side == 0 else (h4, m4)
        resets.append([])
        for v in range(2):
            wide = wide_context(halo[side, v, ROWS], near_m[v]).astype(F32)
            gate = sigmoid(terms[v] + outer[v, side] + wide)
            resets[-1].append((gate * near_h[v].astype(F32)).astype(BF))
    for y, pieces, rows in ((0, [h1, m1], (0,)), (1, [h4, m4], (2,))):
        terms = convolved(pieces, kernel_rows(gate_k, rows))
        updates.append([])
        resets.append([])
        for v in range(2):
            both = terms[v] + gates[v, y]
            gate = sigmoid(both[:, UNITS:])
            resets[-1].append((gate * state[v, y].astype(F32)).astype(BF))
            updates[-1].append(
                sigmoid(
                    both[PAD : PAD + TILE, :UNITS] + context[v, y, :, :UNITS].astype(F32)
                )
            )
    r1, r4, r2, r3 = resets
    head_rows = jnp.broadcast_to(head[...].astype(F32), (8, UNITS)).astype(BF)
    for y, pieces, row_at in ((0, [r1, r2, r3, m1], 0), (1, [r2, r3, r4, m4], 2)):
        weights = jnp.concatenate(
            [
                kernel_rows(cand_k, (0, 1, 2), FROM_STATE),
                kernel_rows(cand_k, (row_at,), FROM_MOTION),
            ],
            axis=0,
        )
        terms = convolved(pieces, weights)
        for v in range(2):
            candidate = jnp.tanh(terms[v][PAD : PAD + TILE] + cands[v, y])
            old = hidden[v, y].astype(F32)
            update = updates[y][v]
            new[v, y] = ((1.0 - update) * old + update * candidate).astype(BF)
        for v in range(2):
            inc[v, y : y + 1, :] = lax.dot_general(
                head_rows, new[v, y], (((1,), (1,)), ((), ())), preferred_element_type=F32
            )[0:1]


def call(kernel, outs, in_specs=None, scratch=(), **cost):
    return pl.pallas_call(
        kernel,
        **({} if in_specs is None else {"in_specs": in_specs}),
        out_shape=[jax.ShapeDtypeStruct(shape, dtype) for shape, dtype in outs],
        scratch_shapes=list(scratch),
        compiler_params=pltpu.CompilerParams(vmem_limit_bytes=VMEM_LIMIT),
        cost_estimate=pl.CostEstimate(transcendentals=0, **cost),
    )


def local(
    voxels,
    disparity,
    hidden,
    context,
    embed_first,
    embed_bias,
    embed_second,
    motion_weight,
    motion_scale,
    motion_bias,
    gate_kernel,
    candidate_kernel,
    head_weight,
):
    cols = lax.axis_size("col")
    rows = lax.axis_size("row")
    odd = [(i, i ^ 1) for i in range(cols)]
    across = [(i, (i + 2) % cols) for i in range(cols)]
    chip = [(i, i ^ 1) for i in range(rows)]

    even, link = [], []
    for r in range(rows):
        for c in range(cols):
            outer_col, outer_row = c in (0, cols - 1), r in (0, rows - 1)
            even.append((r * cols + c, (r ^ 1) * cols + c if outer_col else r * cols + ((c - 1) ^ 1) + 1))
            link.append((r * cols + c, r * cols + (c ^ 1) if outer_row else (((r - 1) ^ 1) + 1) * cols + c))

    pool, lane_rows = tables()

    (own, odd_out, even_out, far, chip_out, link_out, *raw, pool, lane_rows, scale, bias, disp) = call(
        pack_kernel,
        [
            ((4, 32, 256), BF),
            ((80, 256), BF),
            ((80, 256), BF),
            ((64, 128), BF),
            ((2, ROWS + 1, TILE, UNITS), BF),
            ((2, ROWS + 1, TILE, UNITS), BF),
            ((BINS, 256), F32),
            ((1, 256), F32),
            ((256, 256), BF),
            ((LEVELS * TAPS, 128), F32),
            ((256, 256), BF),
            ((8, 128), F32),
            ((1, 128), F32),
            ((1, 128), F32),
            ((2, ROWS, TILE), F32),
        ],
        in_specs=[pl.BlockSpec(memory_space=pltpu.MemorySpace.HBM)] * 12,
        scratch=[
            pltpu.VMEM((2, BINS, ROWS, TILE), F32),
            pltpu.SemaphoreType.DMA((18,)),
        ],
        flops=10**6,
        bytes_accessed=2 * 10**6,
    )(
        *(
            pltpu.with_memory_space_constraint(x, pltpu.MemorySpace.HBM)
            for x in (
                voxels,
                disparity,
                hidden,
                context,
                embed_first,
                embed_bias.reshape(1, -1),
                embed_second,
                motion_weight,
                motion_scale.reshape(1, -1),
                motion_bias.reshape(1, -1),
                jnp.asarray(pool),
                jnp.asarray(lane_rows),
            )
        )
    )
    far_in = lax.ppermute(far, "col", across)
    odd_in = lax.ppermute(odd_out, "col", odd)
    even_in = lax.ppermute(even_out, ("row", "col"), even)
    link_in = lax.ppermute(link_out, ("row", "col"), link)
    chip_in = lax.ppermute(chip_out, "row", chip)
    w1, w1t, w2t, mw = call(
        weight_kernel,
        [((256, 1024), BF), ((256, 128), BF), ((256, 256), BF), ((128, 128), BF)],
        flops=10**6,
        bytes_accessed=2 * 10**6,
    )(*raw)
    w2 = raw[2]
    (mot,) = call(
        motion_kernel,
        [((2, ROWS, EXT, UNITS), BF)],
        flops=10**9,
        bytes_accessed=10**6,
    )(own, odd_in, even_in, far_in, disp, w1, w1t, w2, w2t, mw, scale, bias, pool, lane_rows)
    mot_link = lax.ppermute(mot, ("row", "col"), link)
    mot_chip = lax.ppermute(mot, "row", chip)
    gates, outer, cands, state = call(
        inner_kernel,
        [
            ((2, ROWS, EXT, 2 * UNITS), F32),
            ((2, 2, EXT, UNITS), F32),
            ((2, ROWS, TILE, UNITS), F32),
            ((2, ROWS, EXT, UNITS), BF),
        ],
        flops=10**9,
        bytes_accessed=4 * 10**6,
    )(hidden, context, mot, gate_kernel, candidate_kernel)
    return tuple(
        call(
            outer_kernel,
            [((2, ROWS, TILE, UNITS), BF), ((2, ROWS, TILE), F32)],
            scratch=[
                pltpu.VMEM((2, 2, ROWS + 1, TILE, UNITS), BF),
                pltpu.VMEM((2, 2, ROWS, EXT, UNITS), BF),
            ],
            flops=10**9,
            bytes_accessed=4 * 10**6,
        )(
            hidden,
            context,
            chip_in,
            link_in,
            mot_chip,
            mot_link,
            gates,
            outer,
            cands,
            state,
            gate_kernel,
            candidate_kernel,
            head_weight.reshape(1, -1),
        )
    )


def solution(mesh):
    band = ("pair", "row")
    in_specs = (
        P(None, None, band, "col"),
        P(None, band, "col"),
        P(None, band, "col", None),
        P(None, band, "col", None),
    ) + (P(),) * 9
    out_specs = (P(None, band, "col", None), P(None, band, "col"))
    return jax.shard_map(local, mesh=mesh, in_specs=in_specs, out_specs=out_specs, check_vma=False)
```

```python
import jax
import jax.numpy as jnp
import numpy as np
from jax import lax
from jax.experimental import pallas as pl
from jax.experimental.pallas import tpu as pltpu
from jax.sharding import PartitionSpec as P

BF = jnp.bfloat16
F32 = jnp.float32

ROWS = 2
TILE = 160
IMAGE = 640
PAD = 8
EXT = TILE + 2 * PAD
BINS = 15
UNITS = 128
NEAR = 48
FAR = 72
WINDOW = 512
LAST = FAR + 2 * TILE + NEAR - 1
TAPS = 9
LEVELS = 4
GROUP = 40
STARTS = (0, 17, 30, 41)
VMEM_LIMIT = 48 * 1024 * 1024


def tables():
    pool = np.zeros((128, 256), np.float32)
    firsts = (28, 12, 4, 0)
    counts = (17, 13, 11, 10)
    for level in range(LEVELS):
        width = 2**level
        for k in range(counts[level]):
            entry = firsts[level] + k
            weight = 1.0 / (16 * width)
            pool[entry * width : (entry + 1) * width, STARTS[level] + k] = weight
            pool[entry * width : (entry + 1) * width, 128 + STARTS[level] + k] = -weight
            if k:
                pool[entry * width : (entry + 1) * width, 127 + STARTS[level] + k] = weight
    lane = np.arange(128)
    member = lane % GROUP
    used = (member < LEVELS * TAPS) & (lane < 3 * GROUP)
    level = np.where(used, member // TAPS, 0)
    first = np.where(used, np.take(np.array(STARTS), level) + member % TAPS, 0)
    scale = np.where(used, 0.5**level, 0.0)
    low = ((lane >= GROUP) & (lane < 2 * GROUP)).astype(np.float32)
    rows = np.zeros((8, 128), np.float32)
    rows[0], rows[1], rows[2] = first, scale, low
    for level in range(LEVELS):
        rows[3, STARTS[level] : STARTS[level] + counts[level]] = 0.5**level
    return np.concatenate([pool, pool]).astype(jnp.bfloat16), rows


def split(value):
    high = value.astype(BF).astype(F32)
    return high, value - high


def silu_of_half(half):
    return half + half * jnp.tanh(half)


def sigmoid(value):
    return 0.5 * jnp.tanh(0.5 * value) + 0.5


def pack_kernel(
    vox_h,
    disp_h,
    hidden_h,
    context_h,
    first_h,
    bias_h,
    second_h,
    motion_h,
    scale_h,
    mbias_h,
    pool_h,
    rows_h,
    own,
    odd_out,
    even_out,
    far,
    chip,
    link,
    first,
    bias,
    w2,
    motion,
    pool,
    rows,
    scale,
    mbias,
    disp,
    vox,
    sems,
):
    row_odd = lax.axis_index("row") % 2
    pairs = [(vox_h, vox), (disp_h, disp)]
    for v in range(2):
        for target, y in ((chip, 1 - row_odd), (link, row_odd)):
            pairs += [
                (hidden_h.at[v], target.at[v, 0:ROWS]),
                (context_h.at[v, y, :, UNITS : 2 * UNITS], target.at[v, ROWS]),
            ]
    data = len(pairs)
    pairs += [
        (first_h, first),
        (bias_h, bias),
        (second_h, w2),
        (motion_h, motion),
        (scale_h, scale),
        (mbias_h, mbias),
        (pool_h, pool),
        (rows_h, rows),
    ]
    copies = [pltpu.make_async_copy(a, b, sems.at[k]) for k, (a, b) in enumerate(pairs)]
    for copy in copies:
        copy.start()
    for copy in copies[:2]:
        copy.wait()
    col = lax.axis_index("col")
    is_even = col % 2 == 0

    def emit(at, to_right, to_left):
        odd_out[at, :] = jnp.where(is_even, to_right, to_left).astype(BF)
        even_out[at, :] = jnp.where(is_even, to_left, to_right).astype(BF)

    parts = []
    for v in range(2):
        for y in range(ROWS):
            high, low = split(vox[v, :, y, :])
            ones = jnp.ones((1, TILE), F32)
            block = jnp.concatenate([high, ones, low, ones], axis=0)
            parts.append(block)
            own[2 * v + y] = jnp.concatenate(
                [block, jnp.zeros((32, 256 - TILE), F32)], axis=1
            ).astype(BF)
    blank = jnp.zeros((32, 256 - TILE - NEAR), F32)
    for y in range(ROWS):
        f0, f1 = parts[y], parts[ROWS + y]
        rows_at = pl.ds(32 * y, 32)
        emit(
            rows_at,
            jnp.concatenate([f1, f0[:, TILE - NEAR :], blank], axis=1),
            jnp.concatenate([f0, f1[:, :NEAR], blank], axis=1),
        )
        tail = jnp.concatenate([f1[:, TILE - FAR :], jnp.zeros((32, 128 - FAR), F32)], axis=1)
        far[rows_at, :] = jnp.where(col < 2, tail, f0[:, :128]).astype(BF)

    for copy in copies[2:data]:
        copy.wait()
    row_at = lax.broadcasted_iota(jnp.int32, (8, 128), 0)
    edges_right, edges_left = [], []
    for v in range(2):
        for y in range(ROWS):

            def context_at(at):
                on_chip, on_link = chip[v, ROWS, at].astype(F32), link[v, ROWS, at].astype(F32)
                return jnp.where(row_odd == y, on_link, on_chip)

            hid_last = pltpu.roll(chip[v, y, 144:160, :].astype(F32)[8:16], 2, 0)
            con_last = pltpu.roll(context_at(slice(144, 160))[8:16], 3, 0)
            hid_first = chip[v, y, 0:16, :].astype(F32)[0:8]
            con_first = pltpu.roll(context_at(slice(0, 16))[0:8], 2, 0)
            depth = disp[v, y : y + 1, :]
            d_last = pltpu.roll(jnp.broadcast_to(depth[:, 32:160], (8, 128)), 8, 1)
            d_first = jnp.broadcast_to(depth[:, 0:128], (8, 128))

            def edge(hid, con, dis):
                d_high, rest = split(dis)
                d_mid, d_low = split(rest)
                out = jnp.where(row_at < 2, hid, con)
                out = jnp.where(row_at == 3, d_high, out)
                out = jnp.where(row_at == 4, d_mid, out)
                return jnp.where(row_at >= 5, d_low, out)

            edges_right.append(edge(hid_last, con_last, d_last))
            edges_left.append(edge(hid_first, con_first, d_first))

    def gathered(edges):
        return jnp.concatenate(
            [
                jnp.concatenate([edges[0], edges[1]], axis=0),
                jnp.concatenate([edges[2], edges[3]], axis=0),
            ],
            axis=1,
        )

    emit(pl.ds(64, 16), gathered(edges_right), gathered(edges_left))
    for copy in copies[data:]:
        copy.wait()


def weight_kernel(first, bias, w2, motion, w1, w1t, w2t, mw):
    w_high, w_low = split(first[...] * 0.5)
    b_high, rest = split(bias[...] * 0.5)
    b_mid, b_low = split(rest)
    stacked = jnp.concatenate([w_high, b_high, w_high, b_mid, w_low, b_low], axis=0)
    block = jnp.concatenate([stacked, jnp.zeros((16, 256), F32)], axis=0).astype(BF)
    empty = jnp.zeros((64, 256), BF)
    for k in range(4):
        for m in range(4):
            w1[64 * k : 64 * k + 64, 256 * m : 256 * m + 256] = block if k == m else empty
    w1t[...] = jnp.concatenate([stacked, jnp.zeros((80, 256), F32)], axis=0).T.astype(BF)
    w2t[...] = w2[...].astype(F32).T.astype(BF)
    m_high, m_low = split(motion[...])
    gap = jnp.zeros((GROUP - LEVELS * TAPS, 128), F32)
    mw[...] = jnp.concatenate(
        [m_high, gap, m_high, gap, m_low, gap, jnp.zeros((8, 128), F32)], axis=0
    ).astype(BF)


def motion_kernel(
    own,
    odd_in,
    even_in,
    far_in,
    disp,
    w1,
    w1t,
    w2,
    w2t,
    mw,
    scale,
    bias,
    pool,
    rows,
    out,
):
    col = lax.axis_index("col")
    is_even = col % 2 == 0

    def received(at):
        first, second = odd_in[at, :].astype(F32), even_in[at, :].astype(F32)
        left = jnp.where(col > 0, jnp.where(is_even, second, first), 0.0)
        right = jnp.where(col < 3, jnp.where(is_even, first, second), 0.0)
        return left, right

    cases = [(v, y) for v in range(2) for y in range(ROWS)]
    edge_left, edge_right = received(pl.ds(64, 16))
    edges = [
        tuple(e[8 * y : 8 * y + 8, 128 * v : 128 * v + 128] for e in (edge_left, edge_right))
        for v, y in cases
    ]
    depth_rows = []
    for (v, y), (e_l, e_r) in zip(cases, edges):
        d_l = e_l[3:4] + e_l[4:5] + e_l[5:6]
        d_r = e_r[3:4] + e_r[4:5] + e_r[5:6]
        depth_rows.append(
            jnp.concatenate(
                [
                    d_l[:, :8],
                    disp[v, y : y + 1, :],
                    d_r[:, :8],
                    jnp.zeros((1, 80), F32),
                ],
                axis=1,
            )
        )
    depth_rows.append(jnp.zeros((4, 256), F32))
    depths = jnp.concatenate(depth_rows, axis=0).T

    blank = jnp.zeros((32, WINDOW - 1 - LAST), F32)
    sides = [received(pl.ds(32 * y, 32)) for y in range(ROWS)]
    queries, windows = [], []
    for v, y in cases:
        left, right = sides[y]
        far = far_in[32 * y : 32 * y + 32, :].astype(F32)[:, :FAR]
        mine = own[ROWS * v + y].astype(F32)[:, :TILE]
        other = own[ROWS * (1 - v) + y].astype(F32)[:, :TILE]
        if v == 0:
            far = jnp.where(col >= 2, far, 0.0)
            pieces = [far, left[:, :TILE], other, right[:, TILE : TILE + NEAR], blank]
            ends = (left[:, TILE + NEAR - PAD : TILE + NEAR], right[:, :PAD])
        else:
            far = jnp.where(col < 2, far, 0.0)
            pieces = [left[:, TILE : TILE + NEAR], other, right[:, :TILE], far, blank]
            ends = (left[:, TILE - PAD : TILE], right[:, TILE : TILE + PAD])
        window = jnp.concatenate(pieces, axis=1)
        windows.append(jnp.concatenate([window, window[:16]], axis=0).astype(BF))
        query = jnp.concatenate([ends[0], mine, ends[1], jnp.zeros((32, 256 - EXT), F32)], axis=1)
        queries += [query, query[:16], jnp.zeros((16, 256), F32)]

    stacked = jnp.concatenate(queries, axis=0).T.astype(BF)
    layer = silu_of_half(jnp.dot(stacked[:EXT], w1[...], preferred_element_type=F32)).astype(BF)
    layer = jnp.concatenate([layer[:, 256 * k : 256 * k + 256] for k in range(4)], axis=0)
    features = jnp.dot(layer, w2[...], preferred_element_type=F32).astype(BF)
    layer = silu_of_half(
        jnp.dot(w1t[:, :48], jnp.concatenate(windows, axis=1), preferred_element_type=F32)
    ).astype(BF)
    match = jnp.dot(w2t[...], layer, preferred_element_type=F32).astype(BF)

    first = rows[0:1, :].astype(jnp.int32)
    level_scale = rows[1:2, :]
    is_low = rows[2:3, :] > 0.5
    entry_scale = rows[3:4, :]
    lane = lax.broadcasted_iota(jnp.int32, (EXT, 128), 1)
    pixel = lax.broadcasted_iota(jnp.int32, (EXT, 1), 0)
    column = pixel + (col * TILE - PAD)
    inside = (column >= 0) & (column < IMAGE)
    pixel = pixel.astype(F32)
    depth_scale = scale[...] * (1.0 / 192.0)
    row_at = lax.broadcasted_iota(jnp.int32, (8, 128), 0)

    nears, rests = [], []
    for k, (v, y) in enumerate(cases):
        scores = jnp.dot(
            features[EXT * k : EXT * k + EXT],
            match[:, WINDOW * k : WINDOW * k + WINDOW],
            preferred_element_type=F32,
        )
        spot = (pixel - PAD if v == 0 else (EXT - 1 - PAD) - pixel) - depths[:EXT, k : k + 1]
        eighth = jnp.floor(spot * 0.125)
        rests.append(spot - 8.0 * eighth)
        start = (8.0 * eighth).astype(jnp.int32) + (FAR + TILE - 32)
        if v == 0:
            block, place = (start + 127 - lane) >> 7, (start + lane) & 127
        else:
            index = (LAST - start) - lane
            block, place = index >> 7, index & 127
        source = scores[:, :128]
        for m in range(1, WINDOW // 128):
            source = jnp.where(block == m, scores[:, 128 * m : 128 * m + 128], source)
        near = jnp.take_along_axis(source, place, axis=1, mode="promise_in_bounds")
        high, low = split(near)
        nears.append(jnp.concatenate([high.astype(BF), low.astype(BF)], axis=1))
    pooled = jnp.dot(jnp.concatenate(nears, axis=0), pool[...], preferred_element_type=F32)
    looks = []
    for k in range(4):
        table = pooled[EXT * k : EXT * k + EXT]
        at = rests[k] * entry_scale
        table = table[:, :128] + (at - jnp.floor(at)) * table[:, 128:]
        index = jnp.floor(rests[k] * level_scale).astype(jnp.int32) + first
        high, low = split(jnp.take_along_axis(table, index, axis=1, mode="promise_in_bounds"))
        looks.append(jnp.where(is_low, low, high).astype(BF))
    sums = jnp.dot(jnp.concatenate(looks, axis=0), mw[...], preferred_element_type=F32)
    for k, (v, y) in enumerate(cases):
        half = 0.5 * (
            sums[EXT * k : EXT * k + EXT] + depths[:EXT, k : k + 1] * depth_scale + bias[...]
        )
        value = jnp.where(inside, silu_of_half(half), 0.0)
        e_l, e_r = edges[k]
        out[v, y] = jnp.concatenate(
            [
                jnp.where(row_at < 6, e_l, value[:8]),
                value[8 : EXT - 8],
                jnp.where(row_at < 2, value[EXT - 8 :], pltpu.roll(e_r, 2, 0)),
            ],
            axis=0,
        ).astype(BF)


def widened(middle, ends, shift_left, shift_right):
    before = pltpu.roll(ends[:16].astype(F32)[:8], shift_left, 0)
    after = pltpu.roll(ends[EXT - 16 :].astype(F32)[8:], shift_right, 0)
    return jnp.concatenate([before, middle.astype(F32), after], axis=0)


def wide_hidden(middle, ends):
    return widened(middle, ends, 6, 6).astype(BF)


def wide_context(middle, ends):
    return widened(middle, ends, 5, 4)


def kernel_rows(kernel, rows, inputs=slice(None), outputs=slice(None)):
    return jnp.concatenate(
        [
            jnp.concatenate([kernel[a, b, inputs, outputs] for a in rows], axis=0)
            for b in range(3)
        ],
        axis=1,
    )


def convolved(pieces, weights):
    stacked = jnp.concatenate(
        [jnp.concatenate([piece[v] for piece in pieces], axis=1) for v in range(2)], axis=0
    )
    products = jnp.dot(stacked, weights, preferred_element_type=F32)
    width = weights.shape[1] // 3
    out = []
    for v in range(2):
        mine = products[EXT * v : EXT * v + EXT]
        before, at, after = (mine[:, width * b : width * b + width] for b in range(3))
        if v == 1:
            before, after = after, before
        out.append(pltpu.roll(before, 1, 0) + at + pltpu.roll(after, EXT - 1, 0))
    return out


RESET = slice(UNITS, 2 * UNITS)
FROM_STATE, FROM_MOTION = slice(0, UNITS), slice(UNITS, 2 * UNITS)


def inner_kernel(hidden, context, mot, gate_k, cand_k, gates, outer, cands, state):
    for v in range(2):
        for y in range(ROWS):
            state[v, y] = wide_hidden(hidden[v, y], mot[v, y])
    h2, h3 = ([state[v, y] for v in range(2)] for y in range(ROWS))
    m2, m3 = ([mot[v, y] for v in range(2)] for y in range(ROWS))
    for y, rows in ((0, (1, 2)), (1, (0, 1))):
        terms = convolved([h2, m2, h3, m3], kernel_rows(gate_k, rows))
        for v in range(2):
            wide = wide_context(context[v, y, :, RESET], mot[v, y])
            gates[v, y, :, :UNITS] = terms[v][:, :UNITS]
            gates[v, y, :, UNITS:] = terms[v][:, UNITS:] + wide
        terms = convolved([m2, m3], kernel_rows(cand_k, rows, FROM_MOTION))
        for v in range(2):
            cands[v, y] = terms[v][PAD : PAD + TILE] + context[v, y, :, 2 * UNITS :].astype(F32)
    for side, pieces, rows in ((0, [h2, m2], (2,)), (1, [h3, m3], (0,))):
        terms = convolved(pieces, kernel_rows(gate_k, rows, outputs=RESET))
        for v in range(2):
            outer[v, side] = terms[v]


def outer_kernel(
    hidden,
    context,
    chip_in,
    link_in,
    mot_chip,
    mot_link,
    gates,
    outer,
    cands,
    state,
    gate_k,
    cand_k,
    head,
    new,
    inc,
):
    row = lax.axis_index("row")
    row_even = row % 2 == 0
    linked = (row > 0) & (row < lax.axis_size("row") - 1)

    def chosen(side, on_link, on_chip):
        on_link = jnp.where(linked, on_link, jnp.zeros_like(on_link))
        return jnp.where(row_even == (side == 0), on_link, on_chip)

    def state_at(side, v, k):
        return chosen(side, link_in[v, k], chip_in[v, k])

    def beyond(side, y):
        mots = [chosen(side, mot_link[v, y], mot_chip[v, y]) for v in range(2)]
        return [wide_hidden(state_at(side, v, y), mots[v]) for v in range(2)], mots

    h0, m0 = beyond(0, 0)
    h1, m1 = beyond(0, 1)
    h4, m4 = beyond(1, 0)
    h5, m5 = beyond(1, 1)
    updates, resets = [], []
    for side, pieces, rows in ((0, [h0, m0, h1, m1], (0, 1)), (1, [h4, m4, h5, m5], (1, 2))):
        terms = convolved(pieces, kernel_rows(gate_k, rows, outputs=RESET))
        near_h, near_m = (h1, m1) if side == 0 else (h4, m4)
        resets.append([])
        for v in range(2):
            wide = wide_context(state_at(side, v, ROWS), near_m[v])
            gate = sigmoid(terms[v] + outer[v, side] + wide)
            resets[-1].append((gate * near_h[v].astype(F32)).astype(BF))
    for y, pieces, rows in ((0, [h1, m1], (0,)), (1, [h4, m4], (2,))):
        terms = convolved(pieces, kernel_rows(gate_k, rows))
        updates.append([])
        resets.append([])
        for v in range(2):
            both = terms[v] + gates[v, y]
            gate = sigmoid(both[:, UNITS:])
            resets[-1].append((gate * state[v, y].astype(F32)).astype(BF))
            updates[-1].append(
                sigmoid(
                    both[PAD : PAD + TILE, :UNITS] + context[v, y, :, :UNITS].astype(F32)
                )
            )
    r1, r4, r2, r3 = resets
    head_rows = jnp.broadcast_to(head[...].astype(F32), (8, UNITS)).astype(BF)
    for y, pieces, row_at in ((0, [r1, r2, r3, m1], 0), (1, [r2, r3, r4, m4], 2)):
        weights = jnp.concatenate(
            [
                kernel_rows(cand_k, (0, 1, 2), FROM_STATE),
                kernel_rows(cand_k, (row_at,), FROM_MOTION),
            ],
            axis=0,
        )
        terms = convolved(pieces, weights)
        for v in range(2):
            candidate = jnp.tanh(terms[v][PAD : PAD + TILE] + cands[v, y])
            old = hidden[v, y].astype(F32)
            update = updates[y][v]
            fresh = ((1.0 - update) * old + update * candidate).astype(BF)
            new[v, y] = fresh
            inc[v, y : y + 1, :] = lax.dot_general(
                head_rows, fresh, (((1,), (1,)), ((), ())), preferred_element_type=F32
            )[0:1]


def call(kernel, outs, in_specs=None, scratch=(), **cost):
    return pl.pallas_call(
        kernel,
        **({} if in_specs is None else {"in_specs": in_specs}),
        out_shape=[jax.ShapeDtypeStruct(shape, dtype) for shape, dtype in outs],
        scratch_shapes=list(scratch),
        compiler_params=pltpu.CompilerParams(vmem_limit_bytes=VMEM_LIMIT),
        cost_estimate=pl.CostEstimate(transcendentals=0, **cost),
    )


def local(
    voxels,
    disparity,
    hidden,
    context,
    embed_first,
    embed_bias,
    embed_second,
    motion_weight,
    motion_scale,
    motion_bias,
    gate_kernel,
    candidate_kernel,
    head_weight,
):
    cols = lax.axis_size("col")
    rows = lax.axis_size("row")
    odd = [(i, i ^ 1) for i in range(cols)]
    across = [(i, (i + 2) % cols) for i in range(cols)]
    chip = [(i, i ^ 1) for i in range(rows)]

    even, link = [], []
    for r in range(rows):
        for c in range(cols):
            outer_col, outer_row = c in (0, cols - 1), r in (0, rows - 1)
            even.append((r * cols + c, (r ^ 1) * cols + c if outer_col else r * cols + ((c - 1) ^ 1) + 1))
            link.append((r * cols + c, r * cols + (c ^ 1) if outer_row else (((r - 1) ^ 1) + 1) * cols + c))

    pool, lane_rows = tables()

    (own, odd_out, even_out, far, chip_out, link_out, *raw, pool, lane_rows, scale, bias, disp) = call(
        pack_kernel,
        [
            ((4, 32, 256), BF),
            ((80, 256), BF),
            ((80, 256), BF),
            ((64, 128), BF),
            ((2, ROWS + 1, TILE, UNITS), BF),
            ((2, ROWS + 1, TILE, UNITS), BF),
            ((BINS, 256), F32),
            ((1, 256), F32),
            ((256, 256), BF),
            ((LEVELS * TAPS, 128), F32),
            ((256, 256), BF),
            ((8, 128), F32),
            ((1, 128), F32),
            ((1, 128), F32),
            ((2, ROWS, TILE), F32),
        ],
        in_specs=[pl.BlockSpec(memory_space=pltpu.MemorySpace.HBM)] * 12,
        scratch=[
            pltpu.VMEM((2, BINS, ROWS, TILE), F32),
            pltpu.SemaphoreType.DMA((18,)),
        ],
        flops=10**6,
        bytes_accessed=2 * 10**6,
    )(
        *(
            pltpu.with_memory_space_constraint(x, pltpu.MemorySpace.HBM)
            for x in (
                voxels,
                disparity,
                hidden,
                context,
                embed_first,
                embed_bias.reshape(1, -1),
                embed_second,
                motion_weight,
                motion_scale.reshape(1, -1),
                motion_bias.reshape(1, -1),
                jnp.asarray(pool),
                jnp.asarray(lane_rows),
            )
        )
    )
    far_in = lax.ppermute(far, "col", across)
    odd_in = lax.ppermute(odd_out, "col", odd)
    even_in = lax.ppermute(even_out, ("row", "col"), even)
    link_in = lax.ppermute(link_out, ("row", "col"), link)
    chip_in = lax.ppermute(chip_out, "row", chip)
    w1, w1t, w2t, mw = call(
        weight_kernel,
        [((256, 1024), BF), ((256, 128), BF), ((256, 256), BF), ((128, 128), BF)],
        flops=10**6,
        bytes_accessed=2 * 10**6,
    )(*raw)
    w2 = raw[2]
    (mot,) = call(
        motion_kernel,
        [((2, ROWS, EXT, UNITS), BF)],
        flops=10**9,
        bytes_accessed=10**6,
    )(own, odd_in, even_in, far_in, disp, w1, w1t, w2, w2t, mw, scale, bias, pool, lane_rows)
    mot_link = lax.ppermute(mot, ("row", "col"), link)
    mot_chip = lax.ppermute(mot, "row", chip)
    gates, outer, cands, state = call(
        inner_kernel,
        [
            ((2, ROWS, EXT, 2 * UNITS), F32),
            ((2, 2, EXT, UNITS), F32),
            ((2, ROWS, TILE, UNITS), F32),
            ((2, ROWS, EXT, UNITS), BF),
        ],
        flops=10**9,
        bytes_accessed=4 * 10**6,
    )(hidden, context, mot, gate_kernel, candidate_kernel)
    return tuple(
        call(
            outer_kernel,
            [((2, ROWS, TILE, UNITS), BF), ((2, ROWS, TILE), F32)],
            flops=10**9,
            bytes_accessed=4 * 10**6,
        )(
            hidden,
            context,
            chip_in,
            link_in,
            mot_chip,
            mot_link,
            gates,
            outer,
            cands,
            state,
            gate_kernel,
            candidate_kernel,
            head_weight.reshape(1, -1),
        )
    )


def solution(mesh):
    band = ("pair", "row")
    in_specs = (
        P(None, None, band, "col"),
        P(None, band, "col"),
        P(None, band, "col", None),
        P(None, band, "col", None),
    ) + (P(),) * 9
    out_specs = (P(None, band, "col", None), P(None, band, "col"))
    return jax.shard_map(local, mesh=mesh, in_specs=in_specs, out_specs=out_specs, check_vma=False)
```

```python
import jax
import jax.numpy as jnp
import numpy as np
from jax import lax
from jax.experimental import pallas as pl
from jax.experimental.pallas import tpu as pltpu
from jax.sharding import PartitionSpec as P

BF = jnp.bfloat16
F32 = jnp.float32

ROWS = 2
TILE = 160
IMAGE = 640
PAD = 8
EXT = TILE + 2 * PAD
BINS = 15
UNITS = 128
NEAR = 48
CLOSE = 384
WINDOW = CLOSE + 128
TAPS = 9
LEVELS = 4
GROUP = 40
STARTS = (0, 17, 30, 41)
VMEM_LIMIT = 48 * 1024 * 1024


def tables():
    pool = np.zeros((128, 256), np.float32)
    firsts = (28, 12, 4, 0)
    counts = (17, 13, 11, 10)
    for level in range(LEVELS):
        width = 2**level
        for k in range(counts[level]):
            entry = firsts[level] + k
            weight = 1.0 / (16 * width)
            pool[entry * width : (entry + 1) * width, STARTS[level] + k] = weight
            pool[entry * width : (entry + 1) * width, 128 + STARTS[level] + k] = -weight
            if k:
                pool[entry * width : (entry + 1) * width, 127 + STARTS[level] + k] = weight
    lane = np.arange(128)
    member = lane % GROUP
    used = (member < LEVELS * TAPS) & (lane < 3 * GROUP)
    level = np.where(used, member // TAPS, 0)
    first = np.where(used, np.take(np.array(STARTS), level) + member % TAPS, 0)
    scale = np.where(used, 0.5**level, 0.0)
    low = ((lane >= GROUP) & (lane < 2 * GROUP)).astype(np.float32)
    rows = np.zeros((8, 128), np.float32)
    rows[0], rows[1], rows[2] = first, scale, low
    for level in range(LEVELS):
        rows[3, STARTS[level] : STARTS[level] + counts[level]] = 0.5**level
    return np.concatenate([pool, pool]).astype(jnp.bfloat16), rows


def split(value):
    high = value.astype(BF).astype(F32)
    return high, value - high


def silu_of_half(half):
    return half + half * jnp.tanh(half)


def sigmoid(value):
    return 0.5 * jnp.tanh(0.5 * value) + 0.5


def pack_kernel(
    vox_h,
    disp_h,
    hidden_h,
    context_h,
    first_h,
    bias_h,
    second_h,
    motion_h,
    scale_h,
    mbias_h,
    pool_h,
    rows_h,
    own,
    odd_out,
    even_out,
    far,
    chip,
    link,
    first,
    bias,
    w2,
    motion,
    pool,
    rows,
    scale,
    mbias,
    disp,
    vox,
    sems,
):
    row_odd = lax.axis_index("row") % 2
    pairs = [(vox_h, vox), (disp_h, disp)]
    for v in range(2):
        for target, y in ((chip, 1 - row_odd), (link, row_odd)):
            pairs += [
                (hidden_h.at[v], target.at[v, 0:ROWS]),
                (context_h.at[v, y, :, UNITS : 2 * UNITS], target.at[v, ROWS]),
            ]
    data = len(pairs)
    pairs += [
        (first_h, first),
        (bias_h, bias),
        (second_h, w2),
        (motion_h, motion),
        (scale_h, scale),
        (mbias_h, mbias),
        (pool_h, pool),
        (rows_h, rows),
    ]
    copies = [pltpu.make_async_copy(a, b, sems.at[k]) for k, (a, b) in enumerate(pairs)]
    for copy in copies:
        copy.start()
    for copy in copies[:2]:
        copy.wait()
    col = lax.axis_index("col")
    is_even = col % 2 == 0

    def emit(at, to_right, to_left):
        odd_out[at, :] = jnp.where(is_even, to_right, to_left).astype(BF)
        even_out[at, :] = jnp.where(is_even, to_left, to_right).astype(BF)

    parts = []
    for v in range(2):
        for y in range(ROWS):
            high, low = split(vox[v, :, y, :])
            ones = jnp.ones((1, TILE), F32)
            block = jnp.concatenate([high, ones, low, ones], axis=0)
            parts.append(block)
            own[2 * v + y] = jnp.concatenate(
                [block, jnp.zeros((32, 256 - TILE), F32)], axis=1
            ).astype(BF)
    blank = jnp.zeros((32, 256 - TILE - NEAR), F32)
    for y in range(ROWS):
        f0, f1 = parts[y], parts[ROWS + y]
        rows_at = pl.ds(32 * y, 32)
        emit(
            rows_at,
            jnp.concatenate([f1, f0[:, TILE - NEAR :], blank], axis=1),
            jnp.concatenate([f0, f1[:, :NEAR], blank], axis=1),
        )
        far[rows_at, :] = jnp.where(col < 2, f1[:, TILE - 128 :], f0[:, :128]).astype(BF)

    for copy in copies[2:data]:
        copy.wait()
    row_at = lax.broadcasted_iota(jnp.int32, (8, 128), 0)
    edges_right, edges_left = [], []
    for v in range(2):
        for y in range(ROWS):

            def context_at(at):
                on_chip, on_link = chip[v, ROWS, at].astype(F32), link[v, ROWS, at].astype(F32)
                return jnp.where(row_odd == y, on_link, on_chip)

            hid_last = pltpu.roll(chip[v, y, 144:160, :].astype(F32)[8:16], 2, 0)
            con_last = pltpu.roll(context_at(slice(144, 160))[8:16], 3, 0)
            hid_first = chip[v, y, 0:16, :].astype(F32)[0:8]
            con_first = pltpu.roll(context_at(slice(0, 16))[0:8], 2, 0)
            depth = disp[v, y : y + 1, :]
            d_last = pltpu.roll(jnp.broadcast_to(depth[:, 32:160], (8, 128)), 8, 1)
            d_first = jnp.broadcast_to(depth[:, 0:128], (8, 128))

            def edge(hid, con, dis):
                d_high, rest = split(dis)
                d_mid, d_low = split(rest)
                out = jnp.where(row_at < 2, hid, con)
                out = jnp.where(row_at == 3, d_high, out)
                out = jnp.where(row_at == 4, d_mid, out)
                return jnp.where(row_at >= 5, d_low, out)

            edges_right.append(edge(hid_last, con_last, d_last))
            edges_left.append(edge(hid_first, con_first, d_first))

    def gathered(edges):
        return jnp.concatenate(
            [
                jnp.concatenate([edges[0], edges[1]], axis=0),
                jnp.concatenate([edges[2], edges[3]], axis=0),
            ],
            axis=1,
        )

    emit(pl.ds(64, 16), gathered(edges_right), gathered(edges_left))
    for copy in copies[data:]:
        copy.wait()


def weight_kernel(first, bias, w2, motion, w1, w1t, w2t, mw):
    w_high, w_low = split(first[...] * 0.5)
    b_high, rest = split(bias[...] * 0.5)
    b_mid, b_low = split(rest)
    stacked = jnp.concatenate([w_high, b_high, w_high, b_mid, w_low, b_low], axis=0)
    block = jnp.concatenate([stacked, jnp.zeros((16, 256), F32)], axis=0).astype(BF)
    empty = jnp.zeros((64, 256), BF)
    for k in range(4):
        for m in range(4):
            w1[64 * k : 64 * k + 64, 256 * m : 256 * m + 256] = block if k == m else empty
    w1t[...] = jnp.concatenate([stacked, jnp.zeros((80, 256), F32)], axis=0).T.astype(BF)
    w2t[...] = w2[...].astype(F32).T.astype(BF)
    m_high, m_low = split(motion[...])
    gap = jnp.zeros((GROUP - LEVELS * TAPS, 128), F32)
    mw[...] = jnp.concatenate(
        [m_high, gap, m_high, gap, m_low, gap, jnp.zeros((8, 128), F32)], axis=0
    ).astype(BF)


def matched(windows, w1t, w2t):
    layer = silu_of_half(
        jnp.dot(w1t[:, :48], jnp.concatenate(windows, axis=1), preferred_element_type=F32)
    ).astype(BF)
    return jnp.dot(w2t[...], layer, preferred_element_type=F32).astype(BF)


CASES = [(v, y) for v in range(2) for y in range(ROWS)]


def close_kernel(own, odd_in, even_in, disp, w1, w1t, w2, w2t, query_out, match_out, depth_out, edge_out):
    col = lax.axis_index("col")
    is_even = col % 2 == 0

    def received(at):
        first, second = odd_in[at, :].astype(F32), even_in[at, :].astype(F32)
        left = jnp.where(col > 0, jnp.where(is_even, second, first), 0.0)
        right = jnp.where(col < 3, jnp.where(is_even, first, second), 0.0)
        return left, right

    edge_left, edge_right = received(pl.ds(64, 16))
    edges = [
        tuple(e[8 * y : 8 * y + 8, 128 * v : 128 * v + 128] for e in (edge_left, edge_right))
        for v, y in CASES
    ]
    depth_rows = []
    for (v, y), (e_l, e_r) in zip(CASES, edges):
        d_l = e_l[3:4] + e_l[4:5] + e_l[5:6]
        d_r = e_r[3:4] + e_r[4:5] + e_r[5:6]
        depth_rows.append(
            jnp.concatenate(
                [
                    d_l[:, :8],
                    disp[v, y : y + 1, :],
                    d_r[:, :8],
                    jnp.zeros((1, 80), F32),
                ],
                axis=1,
            )
        )
    depth_rows.append(jnp.zeros((4, 256), F32))
    depth_out[...] = jnp.concatenate(depth_rows, axis=0).T[:EXT]
    edge_out[0] = edge_left
    edge_out[1] = edge_right

    blank = jnp.zeros((32, CLOSE - 2 * TILE - NEAR), F32)
    sides = [received(pl.ds(32 * y, 32)) for y in range(ROWS)]
    queries, windows = [], []
    for v, y in CASES:
        left, right = sides[y]
        mine = own[ROWS * v + y].astype(F32)[:, :TILE]
        other = own[ROWS * (1 - v) + y].astype(F32)[:, :TILE]
        if v == 0:
            pieces = [left[:, :TILE], other, right[:, TILE : TILE + NEAR], blank]
            ends = (left[:, TILE + NEAR - PAD : TILE + NEAR], right[:, :PAD])
        else:
            pieces = [blank, left[:, TILE : TILE + NEAR], other, right[:, :TILE]]
            ends = (left[:, TILE - PAD : TILE], right[:, TILE : TILE + PAD])
        window = jnp.concatenate(pieces, axis=1)
        windows.append(jnp.concatenate([window, window[:16]], axis=0).astype(BF))
        query = jnp.concatenate([ends[0], mine, ends[1], jnp.zeros((32, 256 - EXT), F32)], axis=1)
        queries += [query, query[:16], jnp.zeros((16, 256), F32)]

    stacked = jnp.concatenate(queries, axis=0).T.astype(BF)
    layer = silu_of_half(jnp.dot(stacked[:EXT], w1[...], preferred_element_type=F32)).astype(BF)
    layer = jnp.concatenate([layer[:, 256 * k : 256 * k + 256] for k in range(4)], axis=0)
    query_out[...] = jnp.dot(layer, w2[...], preferred_element_type=F32).astype(BF)
    match_out[...] = matched(windows, w1t, w2t)


def motion_kernel(
    far_in, query, match, depths, edges, w1t, w2t, mw, scale, bias, pool, rows, out
):
    col = lax.axis_index("col")
    first = rows[0:1, :].astype(jnp.int32)
    level_scale = rows[1:2, :]
    is_low = rows[2:3, :] > 0.5
    entry_scale = rows[3:4, :]
    lane = lax.broadcasted_iota(jnp.int32, (EXT, 128), 1)
    pixel = lax.broadcasted_iota(jnp.int32, (EXT, 1), 0)
    column = pixel + (col * TILE - PAD)
    inside = (column >= 0) & (column < IMAGE)
    pixel = pixel.astype(F32)
    depth_scale = scale[...] * (1.0 / 192.0)
    row_at = lax.broadcasted_iota(jnp.int32, (8, 128), 0)

    windows = []
    for v, y in CASES:
        usable = col >= 2 if v == 0 else col < 2
        window = jnp.where(usable, far_in[32 * y : 32 * y + 32, :].astype(F32), 0.0)
        windows.append(jnp.concatenate([window, window[:16]], axis=0).astype(BF))
    far_match = matched(windows, w1t, w2t)

    nears, rests = [], []
    for k, (v, y) in enumerate(CASES):
        features = query[EXT * k : EXT * k + EXT, :]
        scores = jnp.dot(
            features, match[:, CLOSE * k : CLOSE * k + CLOSE], preferred_element_type=F32
        )
        far_scores = jnp.dot(
            features, far_match[:, 128 * k : 128 * k + 128], preferred_element_type=F32
        )
        blocks = [scores[:, 128 * m : 128 * m + 128] for m in range(CLOSE // 128)]
        blocks = [far_scores] + blocks if v == 0 else blocks + [far_scores]
        spot = (pixel - PAD if v == 0 else (EXT - 1 - PAD) - pixel) - depths[:, k : k + 1]
        eighth = jnp.floor(spot * 0.125)
        rests.append(spot - 8.0 * eighth)
        start = (8.0 * eighth).astype(jnp.int32) + (128 + TILE - 32)
        if v == 0:
            block, place = (start + 127 - lane) >> 7, (start + lane) & 127
        else:
            index = (WINDOW - 1 - start) - lane
            block, place = index >> 7, index & 127
        source = blocks[0]
        for m in range(1, WINDOW // 128):
            source = jnp.where(block == m, blocks[m], source)
        near = jnp.take_along_axis(source, place, axis=1, mode="promise_in_bounds")
        high, low = split(near)
        nears.append(jnp.concatenate([high.astype(BF), low.astype(BF)], axis=1))
    pooled = jnp.dot(jnp.concatenate(nears, axis=0), pool[...], preferred_element_type=F32)
    looks = []
    for k in range(4):
        table = pooled[EXT * k : EXT * k + EXT]
        at = rests[k] * entry_scale
        table = table[:, :128] + (at - jnp.floor(at)) * table[:, 128:]
        index = jnp.floor(rests[k] * level_scale).astype(jnp.int32) + first
        high, low = split(jnp.take_along_axis(table, index, axis=1, mode="promise_in_bounds"))
        looks.append(jnp.where(is_low, low, high).astype(BF))
    sums = jnp.dot(jnp.concatenate(looks, axis=0), mw[...], preferred_element_type=F32)
    for k, (v, y) in enumerate(CASES):
        half = 0.5 * (
            sums[EXT * k : EXT * k + EXT] + depths[:, k : k + 1] * depth_scale + bias[...]
        )
        value = jnp.where(inside, silu_of_half(half), 0.0)
        e_l, e_r = (edges[m, 8 * y : 8 * y + 8, 128 * v : 128 * v + 128] for m in range(2))
        out[v, y] = jnp.concatenate(
            [
                jnp.where(row_at < 6, e_l, value[:8]),
                value[8 : EXT - 8],
                jnp.where(row_at < 2, value[EXT - 8 :], pltpu.roll(e_r, 2, 0)),
            ],
            axis=0,
        ).astype(BF)


def widened(middle, ends, shift_left, shift_right):
    before = pltpu.roll(ends[:16].astype(F32)[:8], shift_left, 0)
    after = pltpu.roll(ends[EXT - 16 :].astype(F32)[8:], shift_right, 0)
    return jnp.concatenate([before, middle.astype(F32), after], axis=0)


def wide_hidden(middle, ends):
    return widened(middle, ends, 6, 6).astype(BF)


def wide_context(middle, ends):
    return widened(middle, ends, 5, 4)


def kernel_rows(kernel, rows, inputs=slice(None), outputs=slice(None)):
    return jnp.concatenate(
        [
            jnp.concatenate([kernel[a, b, inputs, outputs] for a in rows], axis=0)
            for b in range(3)
        ],
        axis=1,
    )


def convolved(pieces, weights):
    stacked = jnp.concatenate(
        [jnp.concatenate([piece[v] for piece in pieces], axis=1) for v in range(2)], axis=0
    )
    products = jnp.dot(stacked, weights, preferred_element_type=F32)
    width = weights.shape[1] // 3
    out = []
    for v in range(2):
        mine = products[EXT * v : EXT * v + EXT]
        before, at, after = (mine[:, width * b : width * b + width] for b in range(3))
        if v == 1:
            before, after = after, before
        out.append(pltpu.roll(before, 1, 0) + at + pltpu.roll(after, EXT - 1, 0))
    return out


RESET = slice(UNITS, 2 * UNITS)
FROM_STATE, FROM_MOTION = slice(0, UNITS), slice(UNITS, 2 * UNITS)


def inner_kernel(hidden, context, mot, gate_k, cand_k, gates, outer, cands, state):
    for v in range(2):
        for y in range(ROWS):
            state[v, y] = wide_hidden(hidden[v, y], mot[v, y])
    h2, h3 = ([state[v, y] for v in range(2)] for y in range(ROWS))
    m2, m3 = ([mot[v, y] for v in range(2)] for y in range(ROWS))
    for y, rows in ((0, (1, 2)), (1, (0, 1))):
        terms = convolved([h2, m2, h3, m3], kernel_rows(gate_k, rows))
        for v in range(2):
            wide = wide_context(context[v, y, :, RESET], mot[v, y])
            gates[v, y, :, :UNITS] = terms[v][:, :UNITS]
            gates[v, y, :, UNITS:] = terms[v][:, UNITS:] + wide
        terms = convolved([m2, m3], kernel_rows(cand_k, rows, FROM_MOTION))
        for v in range(2):
            cands[v, y] = terms[v][PAD : PAD + TILE] + context[v, y, :, 2 * UNITS :].astype(F32)
    for side, pieces, rows in ((0, [h2, m2], (2,)), (1, [h3, m3], (0,))):
        terms = convolved(pieces, kernel_rows(gate_k, rows, outputs=RESET))
        for v in range(2):
            outer[v, side] = terms[v]


def outer_kernel(
    hidden,
    context,
    chip_in,
    link_in,
    mot_chip,
    mot_link,
    gates,
    outer,
    cands,
    state,
    gate_k,
    cand_k,
    head,
    new,
    inc,
):
    row = lax.axis_index("row")
    row_even = row % 2 == 0
    linked = (row > 0) & (row < lax.axis_size("row") - 1)

    def chosen(side, on_link, on_chip):
        on_link = jnp.where(linked, on_link, jnp.zeros_like(on_link))
        return jnp.where(row_even == (side == 0), on_link, on_chip)

    def state_at(side, v, k):
        return chosen(side, link_in[v, k], chip_in[v, k])

    def beyond(side, y):
        mots = [chosen(side, mot_link[v, y], mot_chip[v, y]) for v in range(2)]
        return [wide_hidden(state_at(side, v, y), mots[v]) for v in range(2)], mots

    h0, m0 = beyond(0, 0)
    h1, m1 = beyond(0, 1)
    h4, m4 = beyond(1, 0)
    h5, m5 = beyond(1, 1)
    updates, resets = [], []
    for side, pieces, rows in ((0, [h0, m0, h1, m1], (0, 1)), (1, [h4, m4, h5, m5], (1, 2))):
        terms = convolved(pieces, kernel_rows(gate_k, rows, outputs=RESET))
        near_h, near_m = (h1, m1) if side == 0 else (h4, m4)
        resets.append([])
        for v in range(2):
            wide = wide_context(state_at(side, v, ROWS), near_m[v])
            gate = sigmoid(terms[v] + outer[v, side] + wide)
            resets[-1].append((gate * near_h[v].astype(F32)).astype(BF))
    for y, pieces, rows in ((0, [h1, m1], (0,)), (1, [h4, m4], (2,))):
        terms = convolved(pieces, kernel_rows(gate_k, rows))
        updates.append([])
        resets.append([])
        for v in range(2):
            both = terms[v] + gates[v, y]
            gate = sigmoid(both[:, UNITS:])
            resets[-1].append((gate * state[v, y].astype(F32)).astype(BF))
            updates[-1].append(
                sigmoid(
                    both[PAD : PAD + TILE, :UNITS] + context[v, y, :, :UNITS].astype(F32)
                )
            )
    r1, r4, r2, r3 = resets
    head_rows = jnp.broadcast_to(head[...].astype(F32), (8, UNITS)).astype(BF)
    for y, pieces, row_at in ((0, [r1, r2, r3, m1], 0), (1, [r2, r3, r4, m4], 2)):
        weights = jnp.concatenate(
            [
                kernel_rows(cand_k, (0, 1, 2), FROM_STATE),
                kernel_rows(cand_k, (row_at,), FROM_MOTION),
            ],
            axis=0,
        )
        terms = convolved(pieces, weights)
        for v in range(2):
            candidate = jnp.tanh(terms[v][PAD : PAD + TILE] + cands[v, y])
            old = hidden[v, y].astype(F32)
            update = updates[y][v]
            fresh = ((1.0 - update) * old + update * candidate).astype(BF)
            new[v, y] = fresh
            inc[v, y : y + 1, :] = lax.dot_general(
                head_rows, fresh, (((1,), (1,)), ((), ())), preferred_element_type=F32
            )[0:1]


def call(kernel, outs, in_specs=None, scratch=(), **cost):
    return pl.pallas_call(
        kernel,
        **({} if in_specs is None else {"in_specs": in_specs}),
        out_shape=[jax.ShapeDtypeStruct(shape, dtype) for shape, dtype in outs],
        scratch_shapes=list(scratch),
        compiler_params=pltpu.CompilerParams(vmem_limit_bytes=VMEM_LIMIT),
        cost_estimate=pl.CostEstimate(transcendentals=0, **cost),
    )


def local(
    voxels,
    disparity,
    hidden,
    context,
    embed_first,
    embed_bias,
    embed_second,
    motion_weight,
    motion_scale,
    motion_bias,
    gate_kernel,
    candidate_kernel,
    head_weight,
):
    cols = lax.axis_size("col")
    rows = lax.axis_size("row")
    odd = [(i, i ^ 1) for i in range(cols)]
    across = [(i, (i + 2) % cols) for i in range(cols)]
    chip = [(i, i ^ 1) for i in range(rows)]

    even, link = [], []
    for r in range(rows):
        for c in range(cols):
            outer_col, outer_row = c in (0, cols - 1), r in (0, rows - 1)
            even.append((r * cols + c, (r ^ 1) * cols + c if outer_col else r * cols + ((c - 1) ^ 1) + 1))
            link.append((r * cols + c, r * cols + (c ^ 1) if outer_row else (((r - 1) ^ 1) + 1) * cols + c))

    pool, lane_rows = tables()

    (own, odd_out, even_out, far, chip_out, link_out, *raw, pool, lane_rows, scale, bias, disp) = call(
        pack_kernel,
        [
            ((4, 32, 256), BF),
            ((80, 256), BF),
            ((80, 256), BF),
            ((64, 128), BF),
            ((2, ROWS + 1, TILE, UNITS), BF),
            ((2, ROWS + 1, TILE, UNITS), BF),
            ((BINS, 256), F32),
            ((1, 256), F32),
            ((256, 256), BF),
            ((LEVELS * TAPS, 128), F32),
            ((256, 256), BF),
            ((8, 128), F32),
            ((1, 128), F32),
            ((1, 128), F32),
            ((2, ROWS, TILE), F32),
        ],
        in_specs=[pl.BlockSpec(memory_space=pltpu.MemorySpace.HBM)] * 12,
        scratch=[
            pltpu.VMEM((2, BINS, ROWS, TILE), F32),
            pltpu.SemaphoreType.DMA((18,)),
        ],
        flops=10**6,
        bytes_accessed=2 * 10**6,
    )(
        *(
            pltpu.with_memory_space_constraint(x, pltpu.MemorySpace.HBM)
            for x in (
                voxels,
                disparity,
                hidden,
                context,
                embed_first,
                embed_bias.reshape(1, -1),
                embed_second,
                motion_weight,
                motion_scale.reshape(1, -1),
                motion_bias.reshape(1, -1),
                jnp.asarray(pool),
                jnp.asarray(lane_rows),
            )
        )
    )
    far_in = lax.ppermute(far, "col", across)
    odd_in = lax.ppermute(odd_out, "col", odd)
    even_in = lax.ppermute(even_out, ("row", "col"), even)
    link_in = lax.ppermute(link_out, ("row", "col"), link)
    chip_in = lax.ppermute(chip_out, "row", chip)
    w1, w1t, w2t, mw = call(
        weight_kernel,
        [((256, 1024), BF), ((256, 128), BF), ((256, 256), BF), ((128, 128), BF)],
        flops=10**6,
        bytes_accessed=2 * 10**6,
    )(*raw)
    w2 = raw[2]
    query, match, depths, edges = call(
        close_kernel,
        [
            ((4 * EXT, 256), BF),
            ((256, 4 * CLOSE), BF),
            ((EXT, 8), F32),
            ((2, 16, 256), F32),
        ],
        flops=10**9,
        bytes_accessed=10**6,
    )(own, odd_in, even_in, disp, w1, w1t, w2, w2t)
    (mot,) = call(
        motion_kernel,
        [((2, ROWS, EXT, UNITS), BF)],
        flops=10**9,
        bytes_accessed=10**6,
    )(far_in, query, match, depths, edges, w1t, w2t, mw, scale, bias, pool, lane_rows)
    mot_link = lax.ppermute(mot, ("row", "col"), link)
    mot_chip = lax.ppermute(mot, "row", chip)
    gates, outer, cands, state = call(
        inner_kernel,
        [
            ((2, ROWS, EXT, 2 * UNITS), F32),
            ((2, 2, EXT, UNITS), F32),
            ((2, ROWS, TILE, UNITS), F32),
            ((2, ROWS, EXT, UNITS), BF),
        ],
        flops=10**9,
        bytes_accessed=4 * 10**6,
    )(hidden, context, mot, gate_kernel, candidate_kernel)
    return tuple(
        call(
            outer_kernel,
            [((2, ROWS, TILE, UNITS), BF), ((2, ROWS, TILE), F32)],
            flops=10**9,
            bytes_accessed=4 * 10**6,
        )(
            hidden,
            context,
            chip_in,
            link_in,
            mot_chip,
            mot_link,
            gates,
            outer,
            cands,
            state,
            gate_kernel,
            candidate_kernel,
            head_weight.reshape(1, -1),
        )
    )


def solution(mesh):
    band = ("pair", "row")
    in_specs = (
        P(None, None, band, "col"),
        P(None, band, "col"),
        P(None, band, "col", None),
        P(None, band, "col", None),
    ) + (P(),) * 9
    out_specs = (P(None, band, "col", None), P(None, band, "col"))
    return jax.shard_map(local, mesh=mesh, in_specs=in_specs, out_specs=out_specs, check_vma=False)
```

```python
import jax
import jax.numpy as jnp
import numpy as np
from jax import lax
from jax.experimental import pallas as pl
from jax.experimental.pallas import tpu as pltpu
from jax.sharding import PartitionSpec as P

BF = jnp.bfloat16
F32 = jnp.float32

ROWS = 2
TILE = 160
IMAGE = 640
PAD = 8
EXT = TILE + 2 * PAD
BINS = 15
UNITS = 128
NEAR = 48
CLOSE = 384
WINDOW = CLOSE + 128
TAPS = 9
LEVELS = 4
GROUP = 40
STARTS = (0, 17, 30, 41)
VMEM_LIMIT = 48 * 1024 * 1024


def tables():
    pool = np.zeros((128, 256), np.float32)
    firsts = (28, 12, 4, 0)
    counts = (17, 13, 11, 10)
    for level in range(LEVELS):
        width = 2**level
        for k in range(counts[level]):
            entry = firsts[level] + k
            weight = 1.0 / (16 * width)
            pool[entry * width : (entry + 1) * width, STARTS[level] + k] = weight
            pool[entry * width : (entry + 1) * width, 128 + STARTS[level] + k] = -weight
            if k:
                pool[entry * width : (entry + 1) * width, 127 + STARTS[level] + k] = weight
    lane = np.arange(128)
    member = lane % GROUP
    used = (member < LEVELS * TAPS) & (lane < 3 * GROUP)
    level = np.where(used, member // TAPS, 0)
    first = np.where(used, np.take(np.array(STARTS), level) + member % TAPS, 0)
    scale = np.where(used, 0.5**level, 0.0)
    low = ((lane >= GROUP) & (lane < 2 * GROUP)).astype(np.float32)
    rows = np.zeros((8, 128), np.float32)
    rows[0], rows[1], rows[2] = first, scale, low
    for level in range(LEVELS):
        rows[3, STARTS[level] : STARTS[level] + counts[level]] = 0.5**level
    return pool.astype(jnp.bfloat16), rows


def split(value):
    high = value.astype(BF).astype(F32)
    return high, value - high


def silu_of_half(half):
    return half + half * jnp.tanh(half)


def sigmoid(value):
    return 0.5 * jnp.tanh(0.5 * value) + 0.5


def pack_kernel(
    vox_h,
    disp_h,
    hidden_h,
    context_h,
    first_h,
    bias_h,
    second_h,
    motion_h,
    scale_h,
    mbias_h,
    pool_h,
    rows_h,
    own,
    odd_out,
    even_out,
    far,
    chip,
    link,
    first,
    bias,
    w2,
    motion,
    pool,
    rows,
    scale,
    mbias,
    disp,
    vox,
    sems,
):
    row_odd = lax.axis_index("row") % 2
    pairs = [(vox_h, vox), (disp_h, disp)]
    for v in range(2):
        pairs.append((hidden_h.at[v], chip.at[v, 0:ROWS]))
        for target, y in ((chip, 1 - row_odd), (link, row_odd)):
            pairs.append((context_h.at[v, y, :, UNITS : 2 * UNITS], target.at[v, ROWS]))
    data = len(pairs)
    pairs += [
        (first_h, first),
        (bias_h, bias),
        (second_h, w2),
        (motion_h, motion),
        (scale_h, scale),
        (mbias_h, mbias),
        (pool_h, pool),
        (rows_h, rows),
    ]
    copies = [pltpu.make_async_copy(a, b, sems.at[k]) for k, (a, b) in enumerate(pairs)]
    for copy in copies:
        copy.start()
    for copy in copies[:2]:
        copy.wait()
    col = lax.axis_index("col")
    is_even = col % 2 == 0

    def emit(at, to_right, to_left):
        odd_out[at, :] = jnp.where(is_even, to_right, to_left).astype(BF)
        even_out[at, :] = jnp.where(is_even, to_left, to_right).astype(BF)

    parts = []
    for v in range(2):
        for y in range(ROWS):
            high, low = split(vox[v, :, y, :])
            ones = jnp.ones((1, TILE), F32)
            block = jnp.concatenate([high, ones, low, ones], axis=0)
            parts.append(block)
            own[2 * v + y] = jnp.concatenate(
                [block, jnp.zeros((32, 256 - TILE), F32)], axis=1
            ).astype(BF)
    blank = jnp.zeros((32, 256 - TILE - NEAR), F32)
    for y in range(ROWS):
        f0, f1 = parts[y], parts[ROWS + y]
        rows_at = pl.ds(32 * y, 32)
        emit(
            rows_at,
            jnp.concatenate([f1, f0[:, TILE - NEAR :], blank], axis=1),
            jnp.concatenate([f0, f1[:, :NEAR], blank], axis=1),
        )
        far[rows_at, :] = jnp.where(col < 2, f1[:, TILE - 128 :], f0[:, :128]).astype(BF)

    for copy in copies[2:data]:
        copy.wait()
    for v in range(2):
        link[v, 0:ROWS] = chip[v, 0:ROWS]
    row_at = lax.broadcasted_iota(jnp.int32, (8, 128), 0)
    edges_right, edges_left = [], []
    for v in range(2):
        for y in range(ROWS):

            def context_at(at):
                on_chip, on_link = chip[v, ROWS, at].astype(F32), link[v, ROWS, at].astype(F32)
                return jnp.where(row_odd == y, on_link, on_chip)

            hid_last = pltpu.roll(chip[v, y, 144:160, :].astype(F32)[8:16], 2, 0)
            con_last = pltpu.roll(context_at(slice(144, 160))[8:16], 3, 0)
            hid_first = chip[v, y, 0:16, :].astype(F32)[0:8]
            con_first = pltpu.roll(context_at(slice(0, 16))[0:8], 2, 0)
            depth = disp[v, y : y + 1, :]
            d_last = pltpu.roll(jnp.broadcast_to(depth[:, 32:160], (8, 128)), 8, 1)
            d_first = jnp.broadcast_to(depth[:, 0:128], (8, 128))

            def edge(hid, con, dis):
                d_high, rest = split(dis)
                d_mid, d_low = split(rest)
                out = jnp.where(row_at < 2, hid, con)
                out = jnp.where(row_at == 3, d_high, out)
                out = jnp.where(row_at == 4, d_mid, out)
                return jnp.where(row_at >= 5, d_low, out)

            edges_right.append(edge(hid_last, con_last, d_last))
            edges_left.append(edge(hid_first, con_first, d_first))

    def gathered(edges):
        return jnp.concatenate(
            [
                jnp.concatenate([edges[0], edges[1]], axis=0),
                jnp.concatenate([edges[2], edges[3]], axis=0),
            ],
            axis=1,
        )

    emit(pl.ds(64, 16), gathered(edges_right), gathered(edges_left))
    for copy in copies[data:]:
        copy.wait()


def weight_kernel(first, bias, w2, motion, w1, w1t, w2t, mw):
    w_high, w_low = split(first[...] * 0.5)
    b_high, rest = split(bias[...] * 0.5)
    b_mid, b_low = split(rest)
    stacked = jnp.concatenate([w_high, b_high, w_high, b_mid, w_low, b_low], axis=0)
    block = jnp.concatenate([stacked, jnp.zeros((16, 256), F32)], axis=0).astype(BF)
    empty = jnp.zeros((64, 256), BF)
    for k in range(2):
        for m in range(2):
            w1[64 * k : 64 * k + 64, 256 * m : 256 * m + 256] = block if k == m else empty
    w1t[...] = jnp.concatenate([stacked, jnp.zeros((80, 256), F32)], axis=0).T.astype(BF)
    w2t[...] = w2[...].astype(F32).T.astype(BF)
    m_high, m_low = split(motion[...])
    gap = jnp.zeros((GROUP - LEVELS * TAPS, 128), F32)
    mw[...] = jnp.concatenate(
        [m_high, gap, m_high, gap, m_low, gap, jnp.zeros((8, 128), F32)], axis=0
    ).astype(BF)


def matched(windows, w1t, w2t):
    layer = silu_of_half(
        jnp.dot(w1t[:, :48], jnp.concatenate(windows, axis=1), preferred_element_type=F32)
    ).astype(BF)
    return jnp.dot(w2t[...], layer, preferred_element_type=F32).astype(BF)


CASES = [(v, y) for v in range(2) for y in range(ROWS)]


def close_kernel(own, odd_in, even_in, disp, w1, w1t, w2, w2t, query_out, match_out, depth_out, edge_out):
    col = lax.axis_index("col")
    is_even = col % 2 == 0

    def received(at):
        first, second = odd_in[at, :].astype(F32), even_in[at, :].astype(F32)
        left = jnp.where(col > 0, jnp.where(is_even, second, first), 0.0)
        right = jnp.where(col < 3, jnp.where(is_even, first, second), 0.0)
        return left, right

    edge_left, edge_right = received(pl.ds(64, 16))
    edges = [
        tuple(e[8 * y : 8 * y + 8, 128 * v : 128 * v + 128] for e in (edge_left, edge_right))
        for v, y in CASES
    ]
    depth_rows = []
    for (v, y), (e_l, e_r) in zip(CASES, edges):
        d_l = e_l[3:4] + e_l[4:5] + e_l[5:6]
        d_r = e_r[3:4] + e_r[4:5] + e_r[5:6]
        depth_rows.append(
            jnp.concatenate(
                [
                    d_l[:, :8],
                    disp[v, y : y + 1, :],
                    d_r[:, :8],
                    jnp.zeros((1, 80), F32),
                ],
                axis=1,
            )
        )
    depth_rows.append(jnp.zeros((4, 256), F32))
    depth_out[...] = jnp.concatenate(depth_rows, axis=0).T[:EXT]
    edge_out[0] = edge_left
    edge_out[1] = edge_right

    blank = jnp.zeros((32, CLOSE - 2 * TILE - NEAR), F32)
    sides = [received(pl.ds(32 * y, 32)) for y in range(ROWS)]
    queries, windows = [], []
    for v, y in CASES:
        left, right = sides[y]
        mine = own[ROWS * v + y].astype(F32)[:, :TILE]
        other = own[ROWS * (1 - v) + y].astype(F32)[:, :TILE]
        if v == 0:
            pieces = [left[:, :TILE], other, right[:, TILE : TILE + NEAR], blank]
            ends = (left[:, TILE + NEAR - PAD : TILE + NEAR], right[:, :PAD])
        else:
            pieces = [blank, left[:, TILE : TILE + NEAR], other, right[:, :TILE]]
            ends = (left[:, TILE - PAD : TILE], right[:, TILE : TILE + PAD])
        window = jnp.concatenate(pieces, axis=1)
        windows.append(jnp.concatenate([window, window[:16]], axis=0).astype(BF))
        query = jnp.concatenate([ends[0], mine, ends[1], jnp.zeros((32, 256 - EXT), F32)], axis=1)
        queries += [query, query[:16], jnp.zeros((16, 256), F32)]

    stacked = jnp.concatenate(queries, axis=0).T.astype(BF)
    layers = []
    for half in (stacked[:EXT, :128], stacked[:EXT, 128:]):
        layer = silu_of_half(jnp.dot(half, w1[...], preferred_element_type=F32)).astype(BF)
        layers += [layer[:, :256], layer[:, 256:]]
    layer = jnp.concatenate(layers, axis=0)
    query_out[...] = jnp.dot(layer, w2[...], preferred_element_type=F32).astype(BF)
    match_out[...] = matched(windows, w1t, w2t)


def motion_kernel(
    far_in, query, match, depths, edges, w1t, w2t, mw, scale, bias, pool, rows, out
):
    col = lax.axis_index("col")
    first = rows[0:1, :].astype(jnp.int32)
    level_scale = rows[1:2, :]
    is_low = rows[2:3, :] > 0.5
    entry_scale = rows[3:4, :]
    lane = lax.broadcasted_iota(jnp.int32, (EXT, 128), 1)
    pixel = lax.broadcasted_iota(jnp.int32, (EXT, 1), 0)
    column = pixel + (col * TILE - PAD)
    inside = (column >= 0) & (column < IMAGE)
    pixel = pixel.astype(F32)
    depth_scale = scale[...] * (1.0 / 192.0)
    row_at = lax.broadcasted_iota(jnp.int32, (8, 128), 0)

    windows = []
    for v, y in CASES:
        usable = col >= 2 if v == 0 else col < 2
        window = jnp.where(usable, far_in[32 * y : 32 * y + 32, :].astype(F32), 0.0)
        windows.append(jnp.concatenate([window, window[:16]], axis=0).astype(BF))
    far_match = matched(windows, w1t, w2t)

    nears, rests = [], []
    for k, (v, y) in enumerate(CASES):
        features = query[EXT * k : EXT * k + EXT, :]
        scores = jnp.dot(
            features, match[:, CLOSE * k : CLOSE * k + CLOSE], preferred_element_type=F32
        )
        far_scores = jnp.dot(
            features, far_match[:, 128 * k : 128 * k + 128], preferred_element_type=F32
        )
        blocks = [scores[:, 128 * m : 128 * m + 128] for m in range(CLOSE // 128)]
        blocks = [far_scores] + blocks if v == 0 else blocks + [far_scores]
        spot = (pixel - PAD if v == 0 else (EXT - 1 - PAD) - pixel) - depths[:, k : k + 1]
        eighth = jnp.floor(spot * 0.125)
        rests.append(spot - 8.0 * eighth)
        start = (8.0 * eighth).astype(jnp.int32) + (128 + TILE - 32)
        if v == 0:
            block, place = (start + 127 - lane) >> 7, (start + lane) & 127
        else:
            index = (WINDOW - 1 - start) - lane
            block, place = index >> 7, index & 127
        source = blocks[0]
        for m in range(1, WINDOW // 128):
            source = jnp.where(block == m, blocks[m], source)
        near = jnp.take_along_axis(source, place, axis=1, mode="promise_in_bounds")
        high, low = split(near)
        nears.append(jnp.concatenate([high.astype(BF), low.astype(BF)], axis=1))
    twice = jnp.concatenate([pool[...], pool[...]], axis=0)
    pooled = jnp.dot(jnp.concatenate(nears, axis=0), twice, preferred_element_type=F32)
    looks = []
    for k in range(4):
        table = pooled[EXT * k : EXT * k + EXT]
        at = rests[k] * entry_scale
        table = table[:, :128] + (at - jnp.floor(at)) * table[:, 128:]
        index = jnp.floor(rests[k] * level_scale).astype(jnp.int32) + first
        high, low = split(jnp.take_along_axis(table, index, axis=1, mode="promise_in_bounds"))
        looks.append(jnp.where(is_low, low, high).astype(BF))
    sums = jnp.dot(jnp.concatenate(looks, axis=0), mw[...], preferred_element_type=F32)
    for k, (v, y) in enumerate(CASES):
        half = 0.5 * (
            sums[EXT * k : EXT * k + EXT] + depths[:, k : k + 1] * depth_scale + bias[...]
        )
        value = jnp.where(inside, silu_of_half(half), 0.0)
        e_l, e_r = (edges[m, 8 * y : 8 * y + 8, 128 * v : 128 * v + 128] for m in range(2))
        out[v, y] = jnp.concatenate(
            [
                jnp.where(row_at < 6, e_l, value[:8]),
                value[8 : EXT - 8],
                jnp.where(row_at < 2, value[EXT - 8 :], pltpu.roll(e_r, 2, 0)),
            ],
            axis=0,
        ).astype(BF)


def widened(middle, ends, shift_left, shift_right):
    before = pltpu.roll(ends[:16].astype(F32)[:8], shift_left, 0)
    after = pltpu.roll(ends[EXT - 16 :].astype(F32)[8:], shift_right, 0)
    return jnp.concatenate([before, middle.astype(F32), after], axis=0)


def wide_hidden(middle, ends):
    return widened(middle, ends, 6, 6).astype(BF)


def wide_context(middle, ends):
    return widened(middle, ends, 5, 4)


def kernel_rows(kernel, rows, inputs=slice(None), outputs=slice(None)):
    return jnp.concatenate(
        [
            jnp.concatenate([kernel[a, b, inputs, outputs] for a in rows], axis=0)
            for b in range(3)
        ],
        axis=1,
    )


def convolved(pieces, weights):
    stacked = jnp.concatenate(
        [jnp.concatenate([piece[v] for piece in pieces], axis=1) for v in range(2)], axis=0
    )
    products = jnp.dot(stacked, weights, preferred_element_type=F32)
    width = weights.shape[1] // 3
    out = []
    for v in range(2):
        mine = products[EXT * v : EXT * v + EXT]
        before, at, after = (mine[:, width * b : width * b + width] for b in range(3))
        if v == 1:
            before, after = after, before
        out.append(pltpu.roll(before, 1, 0) + at + pltpu.roll(after, EXT - 1, 0))
    return out


RESET = slice(UNITS, 2 * UNITS)
FROM_STATE, FROM_MOTION = slice(0, UNITS), slice(UNITS, 2 * UNITS)


def inner_kernel(hidden, context, mot, gate_k, cand_k, gates, outer, cands, state):
    for v in range(2):
        for y in range(ROWS):
            state[v, y] = wide_hidden(hidden[v, y], mot[v, y])
    h2, h3 = ([state[v, y] for v in range(2)] for y in range(ROWS))
    m2, m3 = ([mot[v, y] for v in range(2)] for y in range(ROWS))
    for y, rows in ((0, (1, 2)), (1, (0, 1))):
        terms = convolved([h2, m2, h3, m3], kernel_rows(gate_k, rows))
        for v in range(2):
            wide = wide_context(context[v, y, :, RESET], mot[v, y])
            gates[v, y, :, :UNITS] = terms[v][:, :UNITS]
            gates[v, y, :, UNITS:] = terms[v][:, UNITS:] + wide
        terms = convolved([m2, m3], kernel_rows(cand_k, rows, FROM_MOTION))
        for v in range(2):
            cands[v, y] = terms[v][PAD : PAD + TILE] + context[v, y, :, 2 * UNITS :].astype(F32)
    for side, pieces, rows in ((0, [h2, m2], (2,)), (1, [h3, m3], (0,))):
        terms = convolved(pieces, kernel_rows(gate_k, rows, outputs=RESET))
        for v in range(2):
            outer[v, side] = terms[v]


def outer_kernel(
    hidden,
    context,
    chip_in,
    link_in,
    mot_chip,
    mot_link,
    gates,
    outer,
    cands,
    state,
    gate_k,
    cand_k,
    head,
    new,
    inc,
):
    row = lax.axis_index("row")
    row_even = row % 2 == 0
    linked = (row > 0) & (row < lax.axis_size("row") - 1)

    def chosen(side, on_link, on_chip):
        on_link = jnp.where(linked, on_link, jnp.zeros_like(on_link))
        return jnp.where(row_even == (side == 0), on_link, on_chip)

    def state_at(side, v, k):
        return chosen(side, link_in[v, k], chip_in[v, k])

    def beyond(side, y):
        mots = [chosen(side, mot_link[v, y], mot_chip[v, y]) for v in range(2)]
        return [wide_hidden(state_at(side, v, y), mots[v]) for v in range(2)], mots

    h0, m0 = beyond(0, 0)
    h1, m1 = beyond(0, 1)
    h4, m4 = beyond(1, 0)
    h5, m5 = beyond(1, 1)
    updates, resets = [], []
    for side, pieces, rows in ((0, [h0, m0, h1, m1], (0, 1)), (1, [h4, m4, h5, m5], (1, 2))):
        terms = convolved(pieces, kernel_rows(gate_k, rows, outputs=RESET))
        near_h, near_m = (h1, m1) if side == 0 else (h4, m4)
        resets.append([])
        for v in range(2):
            wide = wide_context(state_at(side, v, ROWS), near_m[v])
            gate = sigmoid(terms[v] + outer[v, side] + wide)
            resets[-1].append((gate * near_h[v].astype(F32)).astype(BF))
    for y, pieces, rows in ((0, [h1, m1], (0,)), (1, [h4, m4], (2,))):
        terms = convolved(pieces, kernel_rows(gate_k, rows))
        updates.append([])
        resets.append([])
        for v in range(2):
            both = terms[v] + gates[v, y]
            gate = sigmoid(both[:, UNITS:])
            resets[-1].append((gate * state[v, y].astype(F32)).astype(BF))
            updates[-1].append(
                sigmoid(
                    both[PAD : PAD + TILE, :UNITS] + context[v, y, :, :UNITS].astype(F32)
                )
            )
    r1, r4, r2, r3 = resets
    head_rows = jnp.broadcast_to(head[...].astype(F32), (8, UNITS)).astype(BF)
    for y, pieces, row_at in ((0, [r1, r2, r3, m1], 0), (1, [r2, r3, r4, m4], 2)):
        weights = jnp.concatenate(
            [
                kernel_rows(cand_k, (0, 1, 2), FROM_STATE),
                kernel_rows(cand_k, (row_at,), FROM_MOTION),
            ],
            axis=0,
        )
        terms = convolved(pieces, weights)
        for v in range(2):
            candidate = jnp.tanh(terms[v][PAD : PAD + TILE] + cands[v, y])
            old = hidden[v, y].astype(F32)
            update = updates[y][v]
            fresh = ((1.0 - update) * old + update * candidate).astype(BF)
            new[v, y] = fresh
            inc[v, y : y + 1, :] = lax.dot_general(
                head_rows, fresh, (((1,), (1,)), ((), ())), preferred_element_type=F32
            )[0:1]


def call(kernel, outs, in_specs=None, scratch=(), **cost):
    return pl.pallas_call(
        kernel,
        **({} if in_specs is None else {"in_specs": in_specs}),
        out_shape=[jax.ShapeDtypeStruct(shape, dtype) for shape, dtype in outs],
        scratch_shapes=list(scratch),
        compiler_params=pltpu.CompilerParams(vmem_limit_bytes=VMEM_LIMIT),
        cost_estimate=pl.CostEstimate(transcendentals=0, **cost),
    )


def local(
    voxels,
    disparity,
    hidden,
    context,
    embed_first,
    embed_bias,
    embed_second,
    motion_weight,
    motion_scale,
    motion_bias,
    gate_kernel,
    candidate_kernel,
    head_weight,
):
    cols = lax.axis_size("col")
    rows = lax.axis_size("row")
    odd = [(i, i ^ 1) for i in range(cols)]
    across = [(i, (i + 2) % cols) for i in range(cols)]
    chip = [(i, i ^ 1) for i in range(rows)]

    even, link = [], []
    for r in range(rows):
        for c in range(cols):
            outer_col, outer_row = c in (0, cols - 1), r in (0, rows - 1)
            even.append((r * cols + c, (r ^ 1) * cols + c if outer_col else r * cols + ((c - 1) ^ 1) + 1))
            link.append((r * cols + c, r * cols + (c ^ 1) if outer_row else (((r - 1) ^ 1) + 1) * cols + c))

    pool, lane_rows = tables()

    (own, odd_out, even_out, far, chip_out, link_out, *raw, pool, lane_rows, scale, bias, disp) = call(
        pack_kernel,
        [
            ((4, 32, 256), BF),
            ((80, 256), BF),
            ((80, 256), BF),
            ((64, 128), BF),
            ((2, ROWS + 1, TILE, UNITS), BF),
            ((2, ROWS + 1, TILE, UNITS), BF),
            ((BINS, 256), F32),
            ((1, 256), F32),
            ((256, 256), BF),
            ((LEVELS * TAPS, 128), F32),
            ((128, 256), BF),
            ((8, 128), F32),
            ((1, 128), F32),
            ((1, 128), F32),
            ((2, ROWS, TILE), F32),
        ],
        in_specs=[pl.BlockSpec(memory_space=pltpu.MemorySpace.HBM)] * 12,
        scratch=[
            pltpu.VMEM((2, BINS, ROWS, TILE), F32),
            pltpu.SemaphoreType.DMA((16,)),
        ],
        flops=10**6,
        bytes_accessed=2 * 10**6,
    )(
        *(
            pltpu.with_memory_space_constraint(x, pltpu.MemorySpace.HBM)
            for x in (
                voxels,
                disparity,
                hidden,
                context,
                embed_first,
                embed_bias.reshape(1, -1),
                embed_second,
                motion_weight,
                motion_scale.reshape(1, -1),
                motion_bias.reshape(1, -1),
                jnp.asarray(pool),
                jnp.asarray(lane_rows),
            )
        )
    )
    far_in = lax.ppermute(far, "col", across)
    odd_in = lax.ppermute(odd_out, "col", odd)
    even_in = lax.ppermute(even_out, ("row", "col"), even)
    link_in = lax.ppermute(link_out, ("row", "col"), link)
    chip_in = lax.ppermute(chip_out, "row", chip)
    w1, w1t, w2t, mw = call(
        weight_kernel,
        [((128, 512), BF), ((256, 128), BF), ((256, 256), BF), ((128, 128), BF)],
        flops=10**6,
        bytes_accessed=2 * 10**6,
    )(*raw)
    w2 = raw[2]
    query, match, depths, edges = call(
        close_kernel,
        [
            ((4 * EXT, 256), BF),
            ((256, 4 * CLOSE), BF),
            ((EXT, 8), F32),
            ((2, 16, 256), F32),
        ],
        flops=10**9,
        bytes_accessed=10**6,
    )(own, odd_in, even_in, disp, w1, w1t, w2, w2t)
    (mot,) = call(
        motion_kernel,
        [((2, ROWS, EXT, UNITS), BF)],
        flops=10**9,
        bytes_accessed=10**6,
    )(far_in, query, match, depths, edges, w1t, w2t, mw, scale, bias, pool, lane_rows)
    mot_link = lax.ppermute(mot, ("row", "col"), link)
    mot_chip = lax.ppermute(mot, "row", chip)
    gates, outer, cands, state = call(
        inner_kernel,
        [
            ((2, ROWS, EXT, 2 * UNITS), F32),
            ((2, 2, EXT, UNITS), F32),
            ((2, ROWS, TILE, UNITS), F32),
            ((2, ROWS, EXT, UNITS), BF),
        ],
        flops=10**9,
        bytes_accessed=4 * 10**6,
    )(hidden, context, mot, gate_kernel, candidate_kernel)
    return tuple(
        call(
            outer_kernel,
            [((2, ROWS, TILE, UNITS), BF), ((2, ROWS, TILE), F32)],
            flops=10**9,
            bytes_accessed=4 * 10**6,
        )(
            hidden,
            context,
            chip_in,
            link_in,
            mot_chip,
            mot_link,
            gates,
            outer,
            cands,
            state,
            gate_kernel,
            candidate_kernel,
            head_weight.reshape(1, -1),
        )
    )


def solution(mesh):
    band = ("pair", "row")
    in_specs = (
        P(None, None, band, "col"),
        P(None, band, "col"),
        P(None, band, "col", None),
        P(None, band, "col", None),
    ) + (P(),) * 9
    out_specs = (P(None, band, "col", None), P(None, band, "col"))
    return jax.shard_map(local, mesh=mesh, in_specs=in_specs, out_specs=out_specs, check_vma=False)
```

```python
import jax
import jax.numpy as jnp
import numpy as np
from jax import lax
from jax.experimental import pallas as pl
from jax.experimental.pallas import tpu as pltpu
from jax.sharding import PartitionSpec as P

BF = jnp.bfloat16
F32 = jnp.float32

ROWS = 2
TILE = 160
IMAGE = 640
PAD = 8
EXT = TILE + 2 * PAD
BINS = 15
UNITS = 128
NEAR = 48
CLOSE = 384
WINDOW = CLOSE + 128
TAPS = 9
LEVELS = 4
GROUP = 40
STARTS = (0, 17, 30, 41)
VMEM_LIMIT = 48 * 1024 * 1024


def tables():
    pool = np.zeros((128, 256), np.float32)
    firsts = (28, 12, 4, 0)
    counts = (17, 13, 11, 10)
    for level in range(LEVELS):
        width = 2**level
        for k in range(counts[level]):
            entry = firsts[level] + k
            weight = 1.0 / (16 * width)
            pool[entry * width : (entry + 1) * width, STARTS[level] + k] = weight
            pool[entry * width : (entry + 1) * width, 128 + STARTS[level] + k] = -weight
            if k:
                pool[entry * width : (entry + 1) * width, 127 + STARTS[level] + k] = weight
    lane = np.arange(128)
    member = lane % GROUP
    used = (member < LEVELS * TAPS) & (lane < 3 * GROUP)
    level = np.where(used, member // TAPS, 0)
    first = np.where(used, np.take(np.array(STARTS), level) + member % TAPS, 0)
    scale = np.where(used, 0.5**level, 0.0)
    low = ((lane >= GROUP) & (lane < 2 * GROUP)).astype(np.float32)
    rows = np.zeros((8, 128), np.float32)
    rows[0], rows[1], rows[2] = first, scale, low
    for level in range(LEVELS):
        rows[3, STARTS[level] : STARTS[level] + counts[level]] = 0.5**level
    return pool.astype(jnp.bfloat16), rows


def split(value):
    high = value.astype(BF).astype(F32)
    return high, value - high


def silu_of_half(half):
    return half + half * jnp.tanh(half)


def sigmoid(value):
    return 0.5 * jnp.tanh(0.5 * value) + 0.5


def pack_kernel(
    vox_h,
    disp_h,
    hidden_h,
    context_h,
    first_h,
    bias_h,
    second_h,
    motion_h,
    scale_h,
    mbias_h,
    pool_h,
    rows_h,
    own,
    odd_out,
    even_out,
    far,
    chip,
    link,
    first,
    bias,
    w2,
    motion,
    pool,
    rows,
    scale,
    mbias,
    disp,
    vox,
    sems,
):
    row_odd = lax.axis_index("row") % 2
    pairs = [(vox_h, vox), (disp_h, disp)]
    for v in range(2):
        pairs.append((hidden_h.at[v], chip.at[v, 0:ROWS]))
        for target, y in ((chip, 1 - row_odd), (link, row_odd)):
            pairs.append((context_h.at[v, y, :, UNITS : 2 * UNITS], target.at[v, ROWS]))
    data = len(pairs)
    pairs += [
        (first_h, first),
        (bias_h, bias),
        (second_h, w2),
        (motion_h, motion),
        (scale_h, scale),
        (mbias_h, mbias),
        (pool_h, pool),
        (rows_h, rows),
    ]
    copies = [pltpu.make_async_copy(a, b, sems.at[k]) for k, (a, b) in enumerate(pairs)]
    for copy in copies:
        copy.start()
    for copy in copies[:2]:
        copy.wait()
    col = lax.axis_index("col")
    is_even = col % 2 == 0

    def emit(at, to_right, to_left):
        odd_out[at, :] = jnp.where(is_even, to_right, to_left).astype(BF)
        even_out[at, :] = jnp.where(is_even, to_left, to_right).astype(BF)

    parts = []
    for v in range(2):
        for y in range(ROWS):
            high, low = split(vox[v, :, y, :])
            ones = jnp.ones((1, TILE), F32)
            block = jnp.concatenate([high, ones, low, ones], axis=0)
            parts.append(block)
            own[2 * v + y] = jnp.concatenate(
                [block, jnp.zeros((32, 256 - TILE), F32)], axis=1
            ).astype(BF)
    blank = jnp.zeros((32, 256 - TILE - NEAR), F32)
    for y in range(ROWS):
        f0, f1 = parts[y], parts[ROWS + y]
        rows_at = pl.ds(32 * y, 32)
        emit(
            rows_at,
            jnp.concatenate([f1, f0[:, TILE - NEAR :], blank], axis=1),
            jnp.concatenate([f0, f1[:, :NEAR], blank], axis=1),
        )
        far[rows_at, :] = jnp.where(col < 2, f1[:, TILE - 128 :], f0[:, :128]).astype(BF)

    for copy in copies[2:data]:
        copy.wait()
    for v in range(2):
        link[v, 0:ROWS] = chip[v, 0:ROWS]
    row_at = lax.broadcasted_iota(jnp.int32, (8, 128), 0)
    edges_right, edges_left = [], []
    for v in range(2):
        for y in range(ROWS):

            def context_at(at):
                on_chip, on_link = chip[v, ROWS, at].astype(F32), link[v, ROWS, at].astype(F32)
                return jnp.where(row_odd == y, on_link, on_chip)

            hid_last = pltpu.roll(chip[v, y, 144:160, :].astype(F32)[8:16], 2, 0)
            con_last = pltpu.roll(context_at(slice(144, 160))[8:16], 3, 0)
            hid_first = chip[v, y, 0:16, :].astype(F32)[0:8]
            con_first = pltpu.roll(context_at(slice(0, 16))[0:8], 2, 0)
            depth = disp[v, y : y + 1, :]
            d_last = pltpu.roll(jnp.broadcast_to(depth[:, 32:160], (8, 128)), 8, 1)
            d_first = jnp.broadcast_to(depth[:, 0:128], (8, 128))

            def edge(hid, con, dis):
                d_high, rest = split(dis)
                d_mid, d_low = split(rest)
                out = jnp.where(row_at < 2, hid, con)
                out = jnp.where(row_at == 3, d_high, out)
                out = jnp.where(row_at == 4, d_mid, out)
                return jnp.where(row_at >= 5, d_low, out)

            edges_right.append(edge(hid_last, con_last, d_last))
            edges_left.append(edge(hid_first, con_first, d_first))

    def gathered(edges):
        return jnp.concatenate(
            [
                jnp.concatenate([edges[0], edges[1]], axis=0),
                jnp.concatenate([edges[2], edges[3]], axis=0),
            ],
            axis=1,
        )

    emit(pl.ds(64, 16), gathered(edges_right), gathered(edges_left))
    for copy in copies[data:]:
        copy.wait()


def weight_kernel(first, bias, w2, motion, w1, w1t, w2t, mw):
    w_high, w_low = split(first[...] * 0.5)
    b_high, rest = split(bias[...] * 0.5)
    b_mid, b_low = split(rest)
    stacked = jnp.concatenate([w_high, b_high, w_high, b_mid, w_low, b_low], axis=0)
    block = jnp.concatenate([stacked, jnp.zeros((16, 256), F32)], axis=0).astype(BF)
    empty = jnp.zeros((64, 256), BF)
    for k in range(2):
        for m in range(2):
            w1[64 * k : 64 * k + 64, 256 * m : 256 * m + 256] = block if k == m else empty
    w1t[...] = jnp.concatenate([stacked, jnp.zeros((80, 256), F32)], axis=0).T.astype(BF)
    w2t[...] = w2[...].astype(F32).T.astype(BF)
    m_high, m_low = split(motion[...])
    gap = jnp.zeros((GROUP - LEVELS * TAPS, 128), F32)
    mw[...] = jnp.concatenate(
        [m_high, gap, m_high, gap, m_low, gap, jnp.zeros((8, 128), F32)], axis=0
    ).astype(BF)


def matched(windows, w1t, w2t):
    layer = silu_of_half(
        jnp.dot(w1t[:, :48], jnp.concatenate(windows, axis=1), preferred_element_type=F32)
    ).astype(BF)
    return jnp.dot(w2t[...], layer, preferred_element_type=F32).astype(BF)


CASES = [(v, y) for v in range(2) for y in range(ROWS)]


def located(depth, v):
    lane = lax.broadcasted_iota(jnp.int32, (EXT, 128), 1)
    pixel = lax.broadcasted_iota(jnp.int32, (EXT, 1), 0).astype(F32)
    spot = (pixel - PAD if v == 0 else (EXT - 1 - PAD) - pixel) - depth
    eighth = jnp.floor(spot * 0.125)
    start = (8.0 * eighth).astype(jnp.int32) + (128 + TILE - 32)
    if v == 0:
        block, place = (start + 127 - lane) >> 7, (start + lane) & 127
    else:
        index = (WINDOW - 1 - start) - lane
        block, place = index >> 7, index & 127
    return spot - 8.0 * eighth, block, place


def close_kernel(own, odd_in, even_in, disp, w1, w1t, w2, w2t, query_out, near_out, depth_out, edge_out):
    col = lax.axis_index("col")
    is_even = col % 2 == 0

    def received(at):
        first, second = odd_in[at, :].astype(F32), even_in[at, :].astype(F32)
        left = jnp.where(col > 0, jnp.where(is_even, second, first), 0.0)
        right = jnp.where(col < 3, jnp.where(is_even, first, second), 0.0)
        return left, right

    edge_left, edge_right = received(pl.ds(64, 16))
    edges = [
        tuple(e[8 * y : 8 * y + 8, 128 * v : 128 * v + 128] for e in (edge_left, edge_right))
        for v, y in CASES
    ]
    depth_rows = []
    for (v, y), (e_l, e_r) in zip(CASES, edges):
        d_l = e_l[3:4] + e_l[4:5] + e_l[5:6]
        d_r = e_r[3:4] + e_r[4:5] + e_r[5:6]
        depth_rows.append(
            jnp.concatenate(
                [
                    d_l[:, :8],
                    disp[v, y : y + 1, :],
                    d_r[:, :8],
                    jnp.zeros((1, 80), F32),
                ],
                axis=1,
            )
        )
    depth_rows.append(jnp.zeros((4, 256), F32))
    depths = jnp.concatenate(depth_rows, axis=0).T[:EXT]
    depth_out[...] = depths
    edge_out[0] = edge_left
    edge_out[1] = edge_right

    blank = jnp.zeros((32, CLOSE - 2 * TILE - NEAR), F32)
    sides = [received(pl.ds(32 * y, 32)) for y in range(ROWS)]
    queries, windows = [], []
    for v, y in CASES:
        left, right = sides[y]
        mine = own[ROWS * v + y].astype(F32)[:, :TILE]
        other = own[ROWS * (1 - v) + y].astype(F32)[:, :TILE]
        if v == 0:
            pieces = [left[:, :TILE], other, right[:, TILE : TILE + NEAR], blank]
            ends = (left[:, TILE + NEAR - PAD : TILE + NEAR], right[:, :PAD])
        else:
            pieces = [blank, left[:, TILE : TILE + NEAR], other, right[:, :TILE]]
            ends = (left[:, TILE - PAD : TILE], right[:, TILE : TILE + PAD])
        window = jnp.concatenate(pieces, axis=1)
        windows.append(jnp.concatenate([window, window[:16]], axis=0).astype(BF))
        query = jnp.concatenate([ends[0], mine, ends[1], jnp.zeros((32, 256 - EXT), F32)], axis=1)
        queries += [query, query[:16], jnp.zeros((16, 256), F32)]

    stacked = jnp.concatenate(queries, axis=0).T.astype(BF)
    layers = []
    for half in (stacked[:EXT, :128], stacked[:EXT, 128:]):
        layer = silu_of_half(jnp.dot(half, w1[...], preferred_element_type=F32)).astype(BF)
        layers += [layer[:, :256], layer[:, 256:]]
    layer = jnp.concatenate(layers, axis=0)
    query = jnp.dot(layer, w2[...], preferred_element_type=F32).astype(BF)
    query_out[...] = query
    match = matched(windows, w1t, w2t)
    for k, (v, y) in enumerate(CASES):
        scores = jnp.dot(
            query[EXT * k : EXT * k + EXT],
            match[:, CLOSE * k : CLOSE * k + CLOSE],
            preferred_element_type=F32,
        )
        _, block, _ = located(depths[:, k : k + 1], v)
        source = scores[:, :128]
        for m in range(1, CLOSE // 128):
            at = m + 1 if v == 0 else m
            source = jnp.where(block == at, scores[:, 128 * m : 128 * m + 128], source)
        near_out[EXT * k : EXT * k + EXT, :] = source


def motion_kernel(
    far_in, query, near_scores, depths, edges, w1t, w2t, mw, scale, bias, pool, rows, out
):
    col = lax.axis_index("col")
    first = rows[0:1, :].astype(jnp.int32)
    level_scale = rows[1:2, :]
    is_low = rows[2:3, :] > 0.5
    entry_scale = rows[3:4, :]
    pixel = lax.broadcasted_iota(jnp.int32, (EXT, 1), 0)
    column = pixel + (col * TILE - PAD)
    inside = (column >= 0) & (column < IMAGE)
    depth_scale = scale[...] * (1.0 / 192.0)
    row_at = lax.broadcasted_iota(jnp.int32, (8, 128), 0)

    windows = []
    for v, y in CASES:
        usable = col >= 2 if v == 0 else col < 2
        window = jnp.where(usable, far_in[32 * y : 32 * y + 32, :].astype(F32), 0.0)
        windows.append(jnp.concatenate([window, window[:16]], axis=0).astype(BF))
    far_match = matched(windows, w1t, w2t)

    nears, rests = [], []
    for k, (v, y) in enumerate(CASES):
        features = query[EXT * k : EXT * k + EXT, :]
        far_scores = jnp.dot(
            features, far_match[:, 128 * k : 128 * k + 128], preferred_element_type=F32
        )
        rest, block, place = located(depths[:, k : k + 1], v)
        rests.append(rest)
        far_block = 0 if v == 0 else WINDOW // 128 - 1
        source = jnp.where(block == far_block, far_scores, near_scores[EXT * k : EXT * k + EXT, :])
        near = jnp.take_along_axis(source, place, axis=1, mode="promise_in_bounds")
        high, low = split(near)
        nears.append(jnp.concatenate([high.astype(BF), low.astype(BF)], axis=1))
    twice = jnp.concatenate([pool[...], pool[...]], axis=0)
    pooled = jnp.dot(jnp.concatenate(nears, axis=0), twice, preferred_element_type=F32)
    looks = []
    for k in range(4):
        table = pooled[EXT * k : EXT * k + EXT]
        at = rests[k] * entry_scale
        table = table[:, :128] + (at - jnp.floor(at)) * table[:, 128:]
        index = jnp.floor(rests[k] * level_scale).astype(jnp.int32) + first
        high, low = split(jnp.take_along_axis(table, index, axis=1, mode="promise_in_bounds"))
        looks.append(jnp.where(is_low, low, high).astype(BF))
    sums = jnp.dot(jnp.concatenate(looks, axis=0), mw[...], preferred_element_type=F32)
    for k, (v, y) in enumerate(CASES):
        half = 0.5 * (
            sums[EXT * k : EXT * k + EXT] + depths[:, k : k + 1] * depth_scale + bias[...]
        )
        value = jnp.where(inside, silu_of_half(half), 0.0)
        e_l, e_r = (edges[m, 8 * y : 8 * y + 8, 128 * v : 128 * v + 128] for m in range(2))
        out[v, y] = jnp.concatenate(
            [
                jnp.where(row_at < 6, e_l, value[:8]),
                value[8 : EXT - 8],
                jnp.where(row_at < 2, value[EXT - 8 :], pltpu.roll(e_r, 2, 0)),
            ],
            axis=0,
        ).astype(BF)


def widened(middle, ends, shift_left, shift_right):
    before = pltpu.roll(ends[:16].astype(F32)[:8], shift_left, 0)
    after = pltpu.roll(ends[EXT - 16 :].astype(F32)[8:], shift_right, 0)
    return jnp.concatenate([before, middle.astype(F32), after], axis=0)


def wide_hidden(middle, ends):
    return widened(middle, ends, 6, 6).astype(BF)


def wide_context(middle, ends):
    return widened(middle, ends, 5, 4)


def kernel_rows(kernel, rows, inputs=slice(None), outputs=slice(None)):
    return jnp.concatenate(
        [
            jnp.concatenate([kernel[a, b, inputs, outputs] for a in rows], axis=0)
            for b in range(3)
        ],
        axis=1,
    )


def convolved(pieces, weights):
    stacked = jnp.concatenate(
        [jnp.concatenate([piece[v] for piece in pieces], axis=1) for v in range(2)], axis=0
    )
    products = jnp.dot(stacked, weights, preferred_element_type=F32)
    width = weights.shape[1] // 3
    out = []
    for v in range(2):
        mine = products[EXT * v : EXT * v + EXT]
        before, at, after = (mine[:, width * b : width * b + width] for b in range(3))
        if v == 1:
            before, after = after, before
        out.append(pltpu.roll(before, 1, 0) + at + pltpu.roll(after, EXT - 1, 0))
    return out


RESET = slice(UNITS, 2 * UNITS)
FROM_STATE, FROM_MOTION = slice(0, UNITS), slice(UNITS, 2 * UNITS)


def inner_kernel(hidden, context, mot, gate_k, cand_k, gates, outer, cands, state):
    for v in range(2):
        for y in range(ROWS):
            state[v, y] = wide_hidden(hidden[v, y], mot[v, y])
    h2, h3 = ([state[v, y] for v in range(2)] for y in range(ROWS))
    m2, m3 = ([mot[v, y] for v in range(2)] for y in range(ROWS))
    for y, rows in ((0, (1, 2)), (1, (0, 1))):
        terms = convolved([h2, m2, h3, m3], kernel_rows(gate_k, rows))
        for v in range(2):
            wide = wide_context(context[v, y, :, RESET], mot[v, y])
            gates[v, y, :, :UNITS] = terms[v][:, :UNITS]
            gates[v, y, :, UNITS:] = terms[v][:, UNITS:] + wide
        terms = convolved([m2, m3], kernel_rows(cand_k, rows, FROM_MOTION))
        for v in range(2):
            cands[v, y] = terms[v][PAD : PAD + TILE] + context[v, y, :, 2 * UNITS :].astype(F32)
    for side, pieces, rows in ((0, [h2, m2], (2,)), (1, [h3, m3], (0,))):
        terms = convolved(pieces, kernel_rows(gate_k, rows, outputs=RESET))
        for v in range(2):
            outer[v, side] = terms[v]


def outer_kernel(
    hidden,
    context,
    chip_in,
    link_in,
    mot_chip,
    mot_link,
    gates,
    outer,
    cands,
    state,
    gate_k,
    cand_k,
    head,
    new,
    inc,
):
    row = lax.axis_index("row")
    row_even = row % 2 == 0
    linked = (row > 0) & (row < lax.axis_size("row") - 1)

    def chosen(side, on_link, on_chip):
        on_link = jnp.where(linked, on_link, jnp.zeros_like(on_link))
        return jnp.where(row_even == (side == 0), on_link, on_chip)

    def state_at(side, v, k):
        return chosen(side, link_in[v, k], chip_in[v, k])

    def beyond(side, y):
        mots = [chosen(side, mot_link[v, y], mot_chip[v, y]) for v in range(2)]
        return [wide_hidden(state_at(side, v, y), mots[v]) for v in range(2)], mots

    h0, m0 = beyond(0, 0)
    h1, m1 = beyond(0, 1)
    h4, m4 = beyond(1, 0)
    h5, m5 = beyond(1, 1)
    updates, resets = [], []
    for side, pieces, rows in ((0, [h0, m0, h1, m1], (0, 1)), (1, [h4, m4, h5, m5], (1, 2))):
        terms = convolved(pieces, kernel_rows(gate_k, rows, outputs=RESET))
        near_h, near_m = (h1, m1) if side == 0 else (h4, m4)
        resets.append([])
        for v in range(2):
            wide = wide_context(state_at(side, v, ROWS), near_m[v])
            gate = sigmoid(terms[v] + outer[v, side] + wide)
            resets[-1].append((gate * near_h[v].astype(F32)).astype(BF))
    for y, pieces, rows in ((0, [h1, m1], (0,)), (1, [h4, m4], (2,))):
        terms = convolved(pieces, kernel_rows(gate_k, rows))
        updates.append([])
        resets.append([])
        for v in range(2):
            both = terms[v] + gates[v, y]
            gate = sigmoid(both[:, UNITS:])
            resets[-1].append((gate * state[v, y].astype(F32)).astype(BF))
            updates[-1].append(
                sigmoid(
                    both[PAD : PAD + TILE, :UNITS] + context[v, y, :, :UNITS].astype(F32)
                )
            )
    r1, r4, r2, r3 = resets
    head_rows = jnp.broadcast_to(head[...].astype(F32), (8, UNITS)).astype(BF)
    for y, pieces, row_at in ((0, [r1, r2, r3, m1], 0), (1, [r2, r3, r4, m4], 2)):
        weights = jnp.concatenate(
            [
                kernel_rows(cand_k, (0, 1, 2), FROM_STATE),
                kernel_rows(cand_k, (row_at,), FROM_MOTION),
            ],
            axis=0,
        )
        terms = convolved(pieces, weights)
        for v in range(2):
            candidate = jnp.tanh(terms[v][PAD : PAD + TILE] + cands[v, y])
            old = hidden[v, y].astype(F32)
            update = updates[y][v]
            fresh = ((1.0 - update) * old + update * candidate).astype(BF)
            new[v, y] = fresh
            inc[v, y : y + 1, :] = lax.dot_general(
                head_rows, fresh, (((1,), (1,)), ((), ())), preferred_element_type=F32
            )[0:1]


def call(kernel, outs, in_specs=None, scratch=(), **cost):
    return pl.pallas_call(
        kernel,
        **({} if in_specs is None else {"in_specs": in_specs}),
        out_shape=[jax.ShapeDtypeStruct(shape, dtype) for shape, dtype in outs],
        scratch_shapes=list(scratch),
        compiler_params=pltpu.CompilerParams(vmem_limit_bytes=VMEM_LIMIT),
        cost_estimate=pl.CostEstimate(transcendentals=0, **cost),
    )


def local(
    voxels,
    disparity,
    hidden,
    context,
    embed_first,
    embed_bias,
    embed_second,
    motion_weight,
    motion_scale,
    motion_bias,
    gate_kernel,
    candidate_kernel,
    head_weight,
):
    cols = lax.axis_size("col")
    rows = lax.axis_size("row")
    odd = [(i, i ^ 1) for i in range(cols)]
    across = [(i, (i + 2) % cols) for i in range(cols)]
    chip = [(i, i ^ 1) for i in range(rows)]

    even, link = [], []
    for r in range(rows):
        for c in range(cols):
            outer_col, outer_row = c in (0, cols - 1), r in (0, rows - 1)
            even.append((r * cols + c, (r ^ 1) * cols + c if outer_col else r * cols + ((c - 1) ^ 1) + 1))
            link.append((r * cols + c, r * cols + (c ^ 1) if outer_row else (((r - 1) ^ 1) + 1) * cols + c))

    pool, lane_rows = tables()

    (own, odd_out, even_out, far, chip_out, link_out, *raw, pool, lane_rows, scale, bias, disp) = call(
        pack_kernel,
        [
            ((4, 32, 256), BF),
            ((80, 256), BF),
            ((80, 256), BF),
            ((64, 128), BF),
            ((2, ROWS + 1, TILE, UNITS), BF),
            ((2, ROWS + 1, TILE, UNITS), BF),
            ((BINS, 256), F32),
            ((1, 256), F32),
            ((256, 256), BF),
            ((LEVELS * TAPS, 128), F32),
            ((128, 256), BF),
            ((8, 128), F32),
            ((1, 128), F32),
            ((1, 128), F32),
            ((2, ROWS, TILE), F32),
        ],
        in_specs=[pl.BlockSpec(memory_space=pltpu.MemorySpace.HBM)] * 12,
        scratch=[
            pltpu.VMEM((2, BINS, ROWS, TILE), F32),
            pltpu.SemaphoreType.DMA((16,)),
        ],
        flops=10**6,
        bytes_accessed=2 * 10**6,
    )(
        *(
            pltpu.with_memory_space_constraint(x, pltpu.MemorySpace.HBM)
            for x in (
                voxels,
                disparity,
                hidden,
                context,
                embed_first,
                embed_bias.reshape(1, -1),
                embed_second,
                motion_weight,
                motion_scale.reshape(1, -1),
                motion_bias.reshape(1, -1),
                jnp.asarray(pool),
                jnp.asarray(lane_rows),
            )
        )
    )
    far_in = lax.ppermute(far, "col", across)
    odd_in = lax.ppermute(odd_out, "col", odd)
    even_in = lax.ppermute(even_out, ("row", "col"), even)
    link_in = lax.ppermute(link_out, ("row", "col"), link)
    chip_in = lax.ppermute(chip_out, "row", chip)
    w1, w1t, w2t, mw = call(
        weight_kernel,
        [((128, 512), BF), ((256, 128), BF), ((256, 256), BF), ((128, 128), BF)],
        flops=10**6,
        bytes_accessed=2 * 10**6,
    )(*raw)
    w2 = raw[2]
    query, near, depths, edges = call(
        close_kernel,
        [
            ((4 * EXT, 256), BF),
            ((4 * EXT, 128), F32),
            ((EXT, 8), F32),
            ((2, 16, 256), F32),
        ],
        flops=10**9,
        bytes_accessed=10**6,
    )(own, odd_in, even_in, disp, w1, w1t, w2, w2t)
    (mot,) = call(
        motion_kernel,
        [((2, ROWS, EXT, UNITS), BF)],
        flops=10**9,
        bytes_accessed=10**6,
    )(far_in, query, near, depths, edges, w1t, w2t, mw, scale, bias, pool, lane_rows)
    mot_link = lax.ppermute(mot, ("row", "col"), link)
    mot_chip = lax.ppermute(mot, "row", chip)
    gates, outer, cands, state = call(
        inner_kernel,
        [
            ((2, ROWS, EXT, 2 * UNITS), F32),
            ((2, 2, EXT, UNITS), F32),
            ((2, ROWS, TILE, UNITS), F32),
            ((2, ROWS, EXT, UNITS), BF),
        ],
        flops=10**9,
        bytes_accessed=4 * 10**6,
    )(hidden, context, mot, gate_kernel, candidate_kernel)
    return tuple(
        call(
            outer_kernel,
            [((2, ROWS, TILE, UNITS), BF), ((2, ROWS, TILE), F32)],
            flops=10**9,
            bytes_accessed=4 * 10**6,
        )(
            hidden,
            context,
            chip_in,
            link_in,
            mot_chip,
            mot_link,
            gates,
            outer,
            cands,
            state,
            gate_kernel,
            candidate_kernel,
            head_weight.reshape(1, -1),
        )
    )


def solution(mesh):
    band = ("pair", "row")
    in_specs = (
        P(None, None, band, "col"),
        P(None, band, "col"),
        P(None, band, "col", None),
        P(None, band, "col", None),
    ) + (P(),) * 9
    out_specs = (P(None, band, "col", None), P(None, band, "col"))
    return jax.shard_map(local, mesh=mesh, in_specs=in_specs, out_specs=out_specs, check_vma=False)
```

```python
import jax
import jax.numpy as jnp
import numpy as np
from jax import lax
from jax.experimental import pallas as pl
from jax.experimental.pallas import tpu as pltpu
from jax.sharding import PartitionSpec as P

BF = jnp.bfloat16
F32 = jnp.float32

ROWS = 2
TILE = 160
IMAGE = 640
PAD = 8
EXT = TILE + 2 * PAD
BINS = 15
UNITS = 128
NEAR = 48
CLOSE = 384
WINDOW = CLOSE + 128
TAPS = 9
LEVELS = 4
GROUP = 40
STARTS = (0, 17, 30, 41)
VMEM_LIMIT = 48 * 1024 * 1024


def tables():
    pool = np.zeros((128, 256), np.float32)
    firsts = (28, 12, 4, 0)
    counts = (17, 13, 11, 10)
    for level in range(LEVELS):
        width = 2**level
        for k in range(counts[level]):
            entry = firsts[level] + k
            weight = 1.0 / (16 * width)
            pool[entry * width : (entry + 1) * width, STARTS[level] + k] = weight
            pool[entry * width : (entry + 1) * width, 128 + STARTS[level] + k] = -weight
            if k:
                pool[entry * width : (entry + 1) * width, 127 + STARTS[level] + k] = weight
    lane = np.arange(128)
    member = lane % GROUP
    used = (member < LEVELS * TAPS) & (lane < 3 * GROUP)
    level = np.where(used, member // TAPS, 0)
    first = np.where(used, np.take(np.array(STARTS), level) + member % TAPS, 0)
    scale = np.where(used, 0.5**level, 0.0)
    low = ((lane >= GROUP) & (lane < 2 * GROUP)).astype(np.float32)
    rows = np.zeros((8, 128), np.float32)
    rows[0], rows[1], rows[2] = first, scale, low
    for level in range(LEVELS):
        rows[3, STARTS[level] : STARTS[level] + counts[level]] = 0.5**level
    return pool.astype(jnp.bfloat16), rows


def split(value):
    high = value.astype(BF).astype(F32)
    return high, value - high


def silu_of_half(half):
    return half + half * jnp.tanh(half)


def sigmoid(value):
    return 0.5 * jnp.tanh(0.5 * value) + 0.5


def pack_kernel(
    vox_h,
    disp_h,
    hidden_h,
    context_h,
    first_h,
    bias_h,
    second_h,
    motion_h,
    scale_h,
    mbias_h,
    pool_h,
    rows_h,
    own,
    odd_out,
    even_out,
    far,
    chip,
    link,
    first,
    bias,
    w2,
    motion,
    pool,
    rows,
    scale,
    mbias,
    disp,
    vox,
    sems,
):
    row_odd = lax.axis_index("row") % 2
    pairs = [(vox_h, vox), (disp_h, disp)]
    for v in range(2):
        pairs.append((hidden_h.at[v], chip.at[v, 0:ROWS]))
        for target, y in ((chip, 1 - row_odd), (link, row_odd)):
            pairs.append((context_h.at[v, y, :, UNITS : 2 * UNITS], target.at[v, ROWS]))
    data = len(pairs)
    pairs += [
        (first_h, first),
        (bias_h, bias),
        (second_h, w2),
        (motion_h, motion),
        (scale_h, scale),
        (mbias_h, mbias),
        (pool_h, pool),
        (rows_h, rows),
    ]
    copies = [pltpu.make_async_copy(a, b, sems.at[k]) for k, (a, b) in enumerate(pairs)]
    for copy in copies:
        copy.start()
    for copy in copies[:2]:
        copy.wait()
    col = lax.axis_index("col")
    is_even = col % 2 == 0

    def emit(at, to_right, to_left):
        odd_out[at, :] = jnp.where(is_even, to_right, to_left).astype(BF)
        even_out[at, :] = jnp.where(is_even, to_left, to_right).astype(BF)

    parts = []
    for v in range(2):
        for y in range(ROWS):
            high, low = split(vox[v, :, y, :])
            ones = jnp.ones((1, TILE), F32)
            block = jnp.concatenate([high, ones, low, ones], axis=0)
            parts.append(block)
            own[2 * v + y] = jnp.concatenate(
                [block, jnp.zeros((32, 256 - TILE), F32)], axis=1
            ).astype(BF)
    blank = jnp.zeros((32, 256 - TILE - NEAR), F32)
    for y in range(ROWS):
        f0, f1 = parts[y], parts[ROWS + y]
        rows_at = pl.ds(32 * y, 32)
        emit(
            rows_at,
            jnp.concatenate([f1, f0[:, TILE - NEAR :], blank], axis=1),
            jnp.concatenate([f0, f1[:, :NEAR], blank], axis=1),
        )
        far[rows_at, :] = jnp.where(col < 2, f1[:, TILE - 128 :], f0[:, :128]).astype(BF)

    for copy in copies[2:data]:
        copy.wait()
    for v in range(2):
        link[v, 0:ROWS] = chip[v, 0:ROWS]
    row_at = lax.broadcasted_iota(jnp.int32, (8, 128), 0)
    edges_right, edges_left = [], []
    for v in range(2):
        for y in range(ROWS):

            def context_at(at):
                on_chip, on_link = chip[v, ROWS, at].astype(F32), link[v, ROWS, at].astype(F32)
                return jnp.where(row_odd == y, on_link, on_chip)

            hid_last = pltpu.roll(chip[v, y, 144:160, :].astype(F32)[8:16], 2, 0)
            con_last = pltpu.roll(context_at(slice(144, 160))[8:16], 3, 0)
            hid_first = chip[v, y, 0:16, :].astype(F32)[0:8]
            con_first = pltpu.roll(context_at(slice(0, 16))[0:8], 2, 0)
            depth = disp[v, y : y + 1, :]
            d_last = pltpu.roll(jnp.broadcast_to(depth[:, 32:160], (8, 128)), 8, 1)
            d_first = jnp.broadcast_to(depth[:, 0:128], (8, 128))

            def edge(hid, con, dis):
                d_high, rest = split(dis)
                d_mid, d_low = split(rest)
                out = jnp.where(row_at < 2, hid, con)
                out = jnp.where(row_at == 3, d_high, out)
                out = jnp.where(row_at == 4, d_mid, out)
                return jnp.where(row_at >= 5, d_low, out)

            edges_right.append(edge(hid_last, con_last, d_last))
            edges_left.append(edge(hid_first, con_first, d_first))

    def gathered(edges):
        return jnp.concatenate(
            [
                jnp.concatenate([edges[0], edges[1]], axis=0),
                jnp.concatenate([edges[2], edges[3]], axis=0),
            ],
            axis=1,
        )

    emit(pl.ds(64, 16), gathered(edges_right), gathered(edges_left))
    for copy in copies[data:]:
        copy.wait()


def prepare_weights(first, bias, w2, motion, w1, w1t, w2t, mw):
    w_high, w_low = split(first[...] * 0.5)
    b_high, rest = split(bias[...] * 0.5)
    b_mid, b_low = split(rest)
    stacked = jnp.concatenate([w_high, b_high, w_high, b_mid, w_low, b_low], axis=0)
    block = jnp.concatenate([stacked, jnp.zeros((16, 256), F32)], axis=0).astype(BF)
    empty = jnp.zeros((64, 256), BF)
    for k in range(2):
        for m in range(2):
            w1[64 * k : 64 * k + 64, 256 * m : 256 * m + 256] = block if k == m else empty
    w1t[...] = jnp.concatenate([stacked, jnp.zeros((80, 256), F32)], axis=0).T.astype(BF)
    w2t[...] = w2[...].astype(F32).T.astype(BF)
    m_high, m_low = split(motion[...])
    gap = jnp.zeros((GROUP - LEVELS * TAPS, 128), F32)
    mw[...] = jnp.concatenate(
        [m_high, gap, m_high, gap, m_low, gap, jnp.zeros((8, 128), F32)], axis=0
    ).astype(BF)


def matched(windows, w1t, w2t):
    layer = silu_of_half(
        jnp.dot(w1t[:, :48], jnp.concatenate(windows, axis=1), preferred_element_type=F32)
    ).astype(BF)
    return jnp.dot(w2t[...], layer, preferred_element_type=F32).astype(BF)


CASES = [(v, y) for v in range(2) for y in range(ROWS)]


def close_kernel(
    own,
    odd_in,
    even_in,
    disp,
    first_layer,
    bias,
    w2,
    motion,
    query_out,
    match_out,
    depth_out,
    edge_out,
    w1t,
    w2t,
    mw,
    w1,
):
    prepare_weights(first_layer, bias, w2, motion, w1, w1t, w2t, mw)
    col = lax.axis_index("col")
    is_even = col % 2 == 0

    def received(at):
        first, second = odd_in[at, :].astype(F32), even_in[at, :].astype(F32)
        left = jnp.where(col > 0, jnp.where(is_even, second, first), 0.0)
        right = jnp.where(col < 3, jnp.where(is_even, first, second), 0.0)
        return left, right

    edge_left, edge_right = received(pl.ds(64, 16))
    edges = [
        tuple(e[8 * y : 8 * y + 8, 128 * v : 128 * v + 128] for e in (edge_left, edge_right))
        for v, y in CASES
    ]
    depth_rows = []
    for (v, y), (e_l, e_r) in zip(CASES, edges):
        d_l = e_l[3:4] + e_l[4:5] + e_l[5:6]
        d_r = e_r[3:4] + e_r[4:5] + e_r[5:6]
        depth_rows.append(
            jnp.concatenate(
                [
                    d_l[:, :8],
                    disp[v, y : y + 1, :],
                    d_r[:, :8],
                    jnp.zeros((1, 80), F32),
                ],
                axis=1,
            )
        )
    depth_rows.append(jnp.zeros((4, 256), F32))
    depth_out[...] = jnp.concatenate(depth_rows, axis=0).T[:EXT]
    edge_out[0] = edge_left
    edge_out[1] = edge_right

    blank = jnp.zeros((32, CLOSE - 2 * TILE - NEAR), F32)
    sides = [received(pl.ds(32 * y, 32)) for y in range(ROWS)]
    queries, windows = [], []
    for v, y in CASES:
        left, right = sides[y]
        mine = own[ROWS * v + y].astype(F32)[:, :TILE]
        other = own[ROWS * (1 - v) + y].astype(F32)[:, :TILE]
        if v == 0:
            pieces = [left[:, :TILE], other, right[:, TILE : TILE + NEAR], blank]
            ends = (left[:, TILE + NEAR - PAD : TILE + NEAR], right[:, :PAD])
        else:
            pieces = [blank, left[:, TILE : TILE + NEAR], other, right[:, :TILE]]
            ends = (left[:, TILE - PAD : TILE], right[:, TILE : TILE + PAD])
        window = jnp.concatenate(pieces, axis=1)
        windows.append(jnp.concatenate([window, window[:16]], axis=0).astype(BF))
        query = jnp.concatenate([ends[0], mine, ends[1], jnp.zeros((32, 256 - EXT), F32)], axis=1)
        queries += [query, query[:16], jnp.zeros((16, 256), F32)]

    stacked = jnp.concatenate(queries, axis=0).T.astype(BF)
    layers = []
    for half in (stacked[:EXT, :128], stacked[:EXT, 128:]):
        layer = silu_of_half(jnp.dot(half, w1[...], preferred_element_type=F32)).astype(BF)
        layers += [layer[:, :256], layer[:, 256:]]
    layer = jnp.concatenate(layers, axis=0)
    query_out[...] = jnp.dot(layer, w2[...], preferred_element_type=F32).astype(BF)
    match_out[...] = matched(windows, w1t, w2t)


def motion_kernel(
    far_in, query, match, depths, edges, w1t, w2t, mw, scale, bias, pool, rows, out
):
    col = lax.axis_index("col")
    first = rows[0:1, :].astype(jnp.int32)
    level_scale = rows[1:2, :]
    is_low = rows[2:3, :] > 0.5
    entry_scale = rows[3:4, :]
    lane = lax.broadcasted_iota(jnp.int32, (EXT, 128), 1)
    pixel = lax.broadcasted_iota(jnp.int32, (EXT, 1), 0)
    column = pixel + (col * TILE - PAD)
    inside = (column >= 0) & (column < IMAGE)
    pixel = pixel.astype(F32)
    depth_scale = scale[...] * (1.0 / 192.0)
    row_at = lax.broadcasted_iota(jnp.int32, (8, 128), 0)

    windows = []
    for v, y in CASES:
        usable = col >= 2 if v == 0 else col < 2
        window = jnp.where(usable, far_in[32 * y : 32 * y + 32, :].astype(F32), 0.0)
        windows.append(jnp.concatenate([window, window[:16]], axis=0).astype(BF))
    far_match = matched(windows, w1t, w2t)

    nears, rests = [], []
    for k, (v, y) in enumerate(CASES):
        features = query[EXT * k : EXT * k + EXT, :]
        scores = jnp.dot(
            features, match[:, CLOSE * k : CLOSE * k + CLOSE], preferred_element_type=F32
        )
        far_scores = jnp.dot(
            features, far_match[:, 128 * k : 128 * k + 128], preferred_element_type=F32
        )
        blocks = [scores[:, 128 * m : 128 * m + 128] for m in range(CLOSE // 128)]
        blocks = [far_scores] + blocks if v == 0 else blocks + [far_scores]
        spot = (pixel - PAD if v == 0 else (EXT - 1 - PAD) - pixel) - depths[:, k : k + 1]
        eighth = jnp.floor(spot * 0.125)
        rests.append(spot - 8.0 * eighth)
        start = (8.0 * eighth).astype(jnp.int32) + (128 + TILE - 32)
        if v == 0:
            block, place = (start + 127 - lane) >> 7, (start + lane) & 127
        else:
            index = (WINDOW - 1 - start) - lane
            block, place = index >> 7, index & 127
        source = blocks[0]
        for m in range(1, WINDOW // 128):
            source = jnp.where(block == m, blocks[m], source)
        near = jnp.take_along_axis(source, place, axis=1, mode="promise_in_bounds")
        high, low = split(near)
        nears.append(jnp.concatenate([high.astype(BF), low.astype(BF)], axis=1))
    twice = jnp.concatenate([pool[...], pool[...]], axis=0)
    pooled = jnp.dot(jnp.concatenate(nears, axis=0), twice, preferred_element_type=F32)
    looks = []
    for k in range(4):
        table = pooled[EXT * k : EXT * k + EXT]
        at = rests[k] * entry_scale
        table = table[:, :128] + (at - jnp.floor(at)) * table[:, 128:]
        index = jnp.floor(rests[k] * level_scale).astype(jnp.int32) + first
        high, low = split(jnp.take_along_axis(table, index, axis=1, mode="promise_in_bounds"))
        looks.append(jnp.where(is_low, low, high).astype(BF))
    sums = jnp.dot(jnp.concatenate(looks, axis=0), mw[...], preferred_element_type=F32)
    for k, (v, y) in enumerate(CASES):
        half = 0.5 * (
            sums[EXT * k : EXT * k + EXT] + depths[:, k : k + 1] * depth_scale + bias[...]
        )
        value = jnp.where(inside, silu_of_half(half), 0.0)
        e_l, e_r = (edges[m, 8 * y : 8 * y + 8, 128 * v : 128 * v + 128] for m in range(2))
        out[v, y] = jnp.concatenate(
            [
                jnp.where(row_at < 6, e_l, value[:8]),
                value[8 : EXT - 8],
                jnp.where(row_at < 2, value[EXT - 8 :], pltpu.roll(e_r, 2, 0)),
            ],
            axis=0,
        ).astype(BF)


def widened(middle, ends, shift_left, shift_right):
    before = pltpu.roll(ends[:16].astype(F32)[:8], shift_left, 0)
    after = pltpu.roll(ends[EXT - 16 :].astype(F32)[8:], shift_right, 0)
    return jnp.concatenate([before, middle.astype(F32), after], axis=0)


def wide_hidden(middle, ends):
    return widened(middle, ends, 6, 6).astype(BF)


def wide_context(middle, ends):
    return widened(middle, ends, 5, 4)


def kernel_rows(kernel, rows, inputs=slice(None), outputs=slice(None)):
    return jnp.concatenate(
        [
            jnp.concatenate([kernel[a, b, inputs, outputs] for a in rows], axis=0)
            for b in range(3)
        ],
        axis=1,
    )


def convolved(pieces, weights):
    stacked = jnp.concatenate(
        [jnp.concatenate([piece[v] for piece in pieces], axis=1) for v in range(2)], axis=0
    )
    products = jnp.dot(stacked, weights, preferred_element_type=F32)
    width = weights.shape[1] // 3
    out = []
    for v in range(2):
        mine = products[EXT * v : EXT * v + EXT]
        before, at, after = (mine[:, width * b : width * b + width] for b in range(3))
        if v == 1:
            before, after = after, before
        out.append(pltpu.roll(before, 1, 0) + at + pltpu.roll(after, EXT - 1, 0))
    return out


RESET = slice(UNITS, 2 * UNITS)
FROM_STATE, FROM_MOTION = slice(0, UNITS), slice(UNITS, 2 * UNITS)


def inner_kernel(hidden, context, mot, gate_k, cand_k, gates, outer, cands, state):
    for v in range(2):
        for y in range(ROWS):
            state[v, y] = wide_hidden(hidden[v, y], mot[v, y])
    h2, h3 = ([state[v, y] for v in range(2)] for y in range(ROWS))
    m2, m3 = ([mot[v, y] for v in range(2)] for y in range(ROWS))
    for y, rows in ((0, (1, 2)), (1, (0, 1))):
        terms = convolved([h2, m2, h3, m3], kernel_rows(gate_k, rows))
        for v in range(2):
            wide = wide_context(context[v, y, :, RESET], mot[v, y])
            gates[v, y, :, :UNITS] = terms[v][:, :UNITS]
            gates[v, y, :, UNITS:] = terms[v][:, UNITS:] + wide
        terms = convolved([m2, m3], kernel_rows(cand_k, rows, FROM_MOTION))
        for v in range(2):
            cands[v, y] = terms[v][PAD : PAD + TILE] + context[v, y, :, 2 * UNITS :].astype(F32)
    for side, pieces, rows in ((0, [h2, m2], (2,)), (1, [h3, m3], (0,))):
        terms = convolved(pieces, kernel_rows(gate_k, rows, outputs=RESET))
        for v in range(2):
            outer[v, side] = terms[v]


def outer_kernel(
    hidden,
    context,
    chip_in,
    link_in,
    mot_chip,
    mot_link,
    gates,
    outer,
    cands,
    state,
    gate_k,
    cand_k,
    head,
    new,
    inc,
):
    row = lax.axis_index("row")
    row_even = row % 2 == 0
    linked = (row > 0) & (row < lax.axis_size("row") - 1)

    def chosen(side, on_link, on_chip):
        on_link = jnp.where(linked, on_link, jnp.zeros_like(on_link))
        return jnp.where(row_even == (side == 0), on_link, on_chip)

    def state_at(side, v, k):
        return chosen(side, link_in[v, k], chip_in[v, k])

    def beyond(side, y):
        mots = [chosen(side, mot_link[v, y], mot_chip[v, y]) for v in range(2)]
        return [wide_hidden(state_at(side, v, y), mots[v]) for v in range(2)], mots

    h0, m0 = beyond(0, 0)
    h1, m1 = beyond(0, 1)
    h4, m4 = beyond(1, 0)
    h5, m5 = beyond(1, 1)
    updates, resets = [], []
    for side, pieces, rows in ((0, [h0, m0, h1, m1], (0, 1)), (1, [h4, m4, h5, m5], (1, 2))):
        terms = convolved(pieces, kernel_rows(gate_k, rows, outputs=RESET))
        near_h, near_m = (h1, m1) if side == 0 else (h4, m4)
        resets.append([])
        for v in range(2):
            wide = wide_context(state_at(side, v, ROWS), near_m[v])
            gate = sigmoid(terms[v] + outer[v, side] + wide)
            resets[-1].append((gate * near_h[v].astype(F32)).astype(BF))
    for y, pieces, rows in ((0, [h1, m1], (0,)), (1, [h4, m4], (2,))):
        terms = convolved(pieces, kernel_rows(gate_k, rows))
        updates.append([])
        resets.append([])
        for v in range(2):
            both = terms[v] + gates[v, y]
            gate = sigmoid(both[:, UNITS:])
            resets[-1].append((gate * state[v, y].astype(F32)).astype(BF))
            updates[-1].append(
                sigmoid(
                    both[PAD : PAD + TILE, :UNITS] + context[v, y, :, :UNITS].astype(F32)
                )
            )
    r1, r4, r2, r3 = resets
    head_rows = jnp.broadcast_to(head[...].astype(F32), (8, UNITS)).astype(BF)
    for y, pieces, row_at in ((0, [r1, r2, r3, m1], 0), (1, [r2, r3, r4, m4], 2)):
        weights = jnp.concatenate(
            [
                kernel_rows(cand_k, (0, 1, 2), FROM_STATE),
                kernel_rows(cand_k, (row_at,), FROM_MOTION),
            ],
            axis=0,
        )
        terms = convolved(pieces, weights)
        for v in range(2):
            candidate = jnp.tanh(terms[v][PAD : PAD + TILE] + cands[v, y])
            old = hidden[v, y].astype(F32)
            update = updates[y][v]
            fresh = ((1.0 - update) * old + update * candidate).astype(BF)
            new[v, y] = fresh
            inc[v, y : y + 1, :] = lax.dot_general(
                head_rows, fresh, (((1,), (1,)), ((), ())), preferred_element_type=F32
            )[0:1]


def call(kernel, outs, in_specs=None, scratch=(), **cost):
    return pl.pallas_call(
        kernel,
        **({} if in_specs is None else {"in_specs": in_specs}),
        out_shape=[jax.ShapeDtypeStruct(shape, dtype) for shape, dtype in outs],
        scratch_shapes=list(scratch),
        compiler_params=pltpu.CompilerParams(vmem_limit_bytes=VMEM_LIMIT),
        cost_estimate=pl.CostEstimate(transcendentals=0, **cost),
    )


def local(
    voxels,
    disparity,
    hidden,
    context,
    embed_first,
    embed_bias,
    embed_second,
    motion_weight,
    motion_scale,
    motion_bias,
    gate_kernel,
    candidate_kernel,
    head_weight,
):
    cols = lax.axis_size("col")
    rows = lax.axis_size("row")
    odd = [(i, i ^ 1) for i in range(cols)]
    across = [(i, (i + 2) % cols) for i in range(cols)]
    chip = [(i, i ^ 1) for i in range(rows)]

    even, link = [], []
    for r in range(rows):
        for c in range(cols):
            outer_col, outer_row = c in (0, cols - 1), r in (0, rows - 1)
            even.append((r * cols + c, (r ^ 1) * cols + c if outer_col else r * cols + ((c - 1) ^ 1) + 1))
            link.append((r * cols + c, r * cols + (c ^ 1) if outer_row else (((r - 1) ^ 1) + 1) * cols + c))

    pool, lane_rows = tables()

    (own, odd_out, even_out, far, chip_out, link_out, *raw, pool, lane_rows, scale, bias, disp) = call(
        pack_kernel,
        [
            ((4, 32, 256), BF),
            ((80, 256), BF),
            ((80, 256), BF),
            ((64, 128), BF),
            ((2, ROWS + 1, TILE, UNITS), BF),
            ((2, ROWS + 1, TILE, UNITS), BF),
            ((BINS, 256), F32),
            ((1, 256), F32),
            ((256, 256), BF),
            ((LEVELS * TAPS, 128), F32),
            ((128, 256), BF),
            ((8, 128), F32),
            ((1, 128), F32),
            ((1, 128), F32),
            ((2, ROWS, TILE), F32),
        ],
        in_specs=[pl.BlockSpec(memory_space=pltpu.MemorySpace.HBM)] * 12,
        scratch=[
            pltpu.VMEM((2, BINS, ROWS, TILE), F32),
            pltpu.SemaphoreType.DMA((16,)),
        ],
        flops=10**6,
        bytes_accessed=2 * 10**6,
    )(
        *(
            pltpu.with_memory_space_constraint(x, pltpu.MemorySpace.HBM)
            for x in (
                voxels,
                disparity,
                hidden,
                context,
                embed_first,
                embed_bias.reshape(1, -1),
                embed_second,
                motion_weight,
                motion_scale.reshape(1, -1),
                motion_bias.reshape(1, -1),
                jnp.asarray(pool),
                jnp.asarray(lane_rows),
            )
        )
    )
    far_in = lax.ppermute(far, "col", across)
    odd_in = lax.ppermute(odd_out, "col", odd)
    even_in = lax.ppermute(even_out, ("row", "col"), even)
    link_in = lax.ppermute(link_out, ("row", "col"), link)
    chip_in = lax.ppermute(chip_out, "row", chip)
    query, match, depths, edges, w1t, w2t, mw = call(
        close_kernel,
        [
            ((4 * EXT, 256), BF),
            ((256, 4 * CLOSE), BF),
            ((EXT, 8), F32),
            ((2, 16, 256), F32),
            ((256, 128), BF),
            ((256, 256), BF),
            ((128, 128), BF),
        ],
        scratch=[pltpu.VMEM((128, 512), BF)],
        flops=10**9,
        bytes_accessed=10**6,
    )(own, odd_in, even_in, disp, *raw)
    (mot,) = call(
        motion_kernel,
        [((2, ROWS, EXT, UNITS), BF)],
        flops=10**9,
        bytes_accessed=10**6,
    )(far_in, query, match, depths, edges, w1t, w2t, mw, scale, bias, pool, lane_rows)
    mot_link = lax.ppermute(mot, ("row", "col"), link)
    mot_chip = lax.ppermute(mot, "row", chip)
    gates, outer, cands, state = call(
        inner_kernel,
        [
            ((2, ROWS, EXT, 2 * UNITS), F32),
            ((2, 2, EXT, UNITS), F32),
            ((2, ROWS, TILE, UNITS), F32),
            ((2, ROWS, EXT, UNITS), BF),
        ],
        flops=10**9,
        bytes_accessed=4 * 10**6,
    )(hidden, context, mot, gate_kernel, candidate_kernel)
    return tuple(
        call(
            outer_kernel,
            [((2, ROWS, TILE, UNITS), BF), ((2, ROWS, TILE), F32)],
            flops=10**9,
            bytes_accessed=4 * 10**6,
        )(
            hidden,
            context,
            chip_in,
            link_in,
            mot_chip,
            mot_link,
            gates,
            outer,
            cands,
            state,
            gate_kernel,
            candidate_kernel,
            head_weight.reshape(1, -1),
        )
    )


def solution(mesh):
    band = ("pair", "row")
    in_specs = (
        P(None, None, band, "col"),
        P(None, band, "col"),
        P(None, band, "col", None),
        P(None, band, "col", None),
    ) + (P(),) * 9
    out_specs = (P(None, band, "col", None), P(None, band, "col"))
    return jax.shard_map(local, mesh=mesh, in_specs=in_specs, out_specs=out_specs, check_vma=False)
```
